256 devices in a mesh: dom: 256 (over x, y, z, core).
Axes of the slice: x: 4, y: 4, z: 8, core: 2. Of those that a mesh axis runs over, the one named last changes fastest.
Arguments:
- entities: float32 [200, 98304], P(None, 'dom'), may hold values from -3 to 3
- entity_state: float32 [98304], P('dom'), may hold values from 0.05 to 1
- relations: float32 [200, 7424], replicated, may hold values from -3 to 3
- relation_state: float32 [7424], replicated, may hold values from 0.05 to 1
- head_rows: int32 [256, 2048], P('dom'), may hold values from 0 to 383
- relation_ids: int32 [256, 2048], P('dom'), may hold values from 0 to 7423
- tail_rows: int32 [256, 2048], P('dom'), may hold values from 0 to 383
- neg_rows: int32 [256, 2, 2, 384], P('dom'), may hold values from 0 to 383
- edge_counts: int32 [256], P('dom'), may hold values from 1 to 2048, 262144 in all
- matching: int32 [256], P('dom'), may hold values from 0 to 255, as said below
Outputs:
- new_entities: float32 [200, 98304], P(None, 'dom')
- new_entity_state: float32 [98304], P('dom')
- new_relations: float32 [200, 7424], replicated
- new_relation_state: float32 [7424], replicated
The draws below stay inside these ranges and needn't reach their ends.
Inputs may be any that keep to these rules, and one draw needn't show every extreme that they name: matching[b] = b XOR s for one s of 1 to 255 shared by all b, so matching is its own inverse and never fixes a bucket.
All inputs are finite; a program needn't handle non-finite values. No bound on the sum of `edge_counts` on one device may be relied on, other than what follows from the above.
Results may differ from the reference program's by a relative error of at most 0.0003.
Values sent between devices are 32-bit elements; how exact they have to be, the bound alone decides.
No kernel may reach another device: no remote copies, remote signals or barrier semaphores. Data moves between devices by JAX's collectives and lax.ppermute only.
A program may use at most 128 MiB of HBM per device.

```python
import math
import jax
import jax.numpy as jnp
import numpy as np
from jax import lax

DIM = 200
NREL = 7424
ROWS_DEV = 384
EDGES = 2048
GROUP = 1024
NNEG = 384
GROUPS = 2
BUCKETS = 256
ROWS = 98304
N_DOM = 256


def draw_matching(key, part):
    key = jax.random.fold_in(key, 11)
    xor_value = jax.random.randint(key, (), 1, N_DOM, dtype=jnp.int32)
    return jnp.bitwise_xor(jnp.arange(N_DOM, dtype=jnp.int32), xor_value)


def place_ends(drawn, own_key, smallest, largest):
    longest = drawn.shape.index(max(drawn.shape))
    spots = []
    for shift in (0, 1):
        where = [jax.random.randint(jax.random.fold_in(own_key, axis), (), 0, length) for axis, length in enumerate(drawn.shape)]
        where[longest] = (where[longest] + shift) % drawn.shape[longest]
        spots.append(tuple(where))
    return drawn.at[spots[0]].set(smallest).at[spots[1]].set(largest)


def level_of(own_key, extent, cuts, low, high):
    loudness = 1.0
    for axis_at, blocks in cuts:
        heights = jax.random.uniform(jax.random.fold_in(jax.random.fold_in(own_key, 6), axis_at), (blocks,), jnp.float32, low / len(cuts), high / len(cuts))
        loudness = loudness * jnp.repeat(jnp.exp(heights), extent[axis_at] // blocks).reshape((-1,) + (1,) * (len(extent) - 1 - axis_at))
    return loudness


def cumulative_ranks(count, skew):
    loads = [(1 << 20) // math.isqrt(grade ** skew) + 1 for grade in range(1, count + 1)]
    scale = 1 + sum(loads) // (1 << 30)
    return np.cumsum(np.array([max(1, weight // scale) for weight in loads]))


def ranked_ids(key, dims, count, slope):
    grid = cumulative_ranks(count, slope)
    ticket = jax.random.randint(jax.random.fold_in(key, 1), dims, 0, int(grid[count - 1]))
    rank = jnp.searchsorted(jnp.asarray(grid, jnp.int32), ticket, side="right")
    return jax.random.permutation(jax.random.fold_in(key, 2), count)[rank].astype(jnp.int32)


def length_profile(amount, total, reach, skew):
    loads = [(1 << 20) // math.isqrt(rank ** skew) + 1 for rank in range(2, amount + 1)]
    surplus, counts = total - reach - (amount - 1), [1] * (amount - 1)
    while surplus > 0:
        movable = [i for i in range(amount - 1) if counts[i] < reach]
        pool, remaining = sum([loads[i] for i in movable]), surplus
        for i in movable:
            more = min(reach - counts[i], max(1, remaining * loads[i] // pool), surplus)
            counts[i] = counts[i] + more
            surplus = surplus - more
    return np.array([reach] + counts)


def ragged_sizes(rng, count, total, limit, skew):
    if count == 2:
        one = jax.random.randint(rng, (), max(1, total - limit), min(limit, total - 1) + 1)
        return jnp.stack([one, total - one])
    sizes = jnp.asarray(length_profile(count, total, limit, skew), jnp.int32)
    pairs = (count - 1) // 2
    donor, receiver = sizes[1:1 + 2 * pairs:2], sizes[2:2 + 2 * pairs:2]
    slack = jnp.minimum(donor - 1, limit - receiver)
    passed = jax.random.randint(jax.random.fold_in(rng, 1), (pairs,), 0, 1 << 20) % (slack + 1)
    sizes = sizes.at[1:1 + 2 * pairs:2].set(donor - passed).at[2:2 + 2 * pairs:2].set(receiver + passed)
    return sizes[jax.random.permutation(jax.random.fold_in(rng, 2), count)]


def gaussian(own_key, shape, width, most, split=(), kind=jnp.bfloat16):
    values = jax.random.normal(own_key, shape, jnp.float32) * width
    if len(split) > 0:
        values = level_of(own_key, shape, split, -0.22, 0.18) * values
    return jnp.clip(values, min=-most, max=most).astype(kind)


def setup_inputs(seed: int = 0) -> dict:
    arg_keys = jax.random.split(jax.random.key(seed), 11)
    entities = gaussian(arg_keys[0], (DIM, ROWS), 0.5, 3.0, ((1, 256),), jnp.float32)
    entity_state = jnp.clip(jnp.exp(math.log(1.0) - 2.9957323 * jax.random.uniform(arg_keys[1], (ROWS,), jnp.float32) ** level_of(arg_keys[1], (ROWS,), ((0, 256),), -0.2, 0.2)), 0.05, 1.0)
    relations = gaussian(arg_keys[2], (DIM, NREL), 0.6, 3.0, (), jnp.float32)
    relation_state = jnp.clip(jnp.exp(jax.random.uniform(arg_keys[3], (NREL,), jnp.float32, math.log(0.05), math.log(1.0))), 0.05, 1.0)
    head_rows = place_ends(jax.random.randint(arg_keys[4], (BUCKETS, EDGES), 0, ROWS_DEV), jax.random.fold_in(arg_keys[4], 1), 0, ROWS_DEV - 1).astype(jnp.int32)
    relation_ids = place_ends(ranked_ids(arg_keys[5], (BUCKETS, EDGES), NREL, 2), jax.random.fold_in(arg_keys[5], 3), 0, NREL - 1).astype(jnp.int32)
    tail_rows = place_ends(jax.random.randint(arg_keys[6], (BUCKETS, EDGES), 0, ROWS_DEV), jax.random.fold_in(arg_keys[6], 1), 0, ROWS_DEV - 1).astype(jnp.int32)
    neg_rows = place_ends(jax.random.randint(arg_keys[7], (BUCKETS, GROUPS, 2, NNEG), 0, ROWS_DEV), jax.random.fold_in(arg_keys[7], 1), 0, ROWS_DEV - 1).astype(jnp.int32)
    edge_counts = ragged_sizes(arg_keys[8], BUCKETS, BUCKETS * EDGES // 2, EDGES, 2).astype(jnp.int32)
    matching = draw_matching(jax.random.fold_in(arg_keys[10], 71), 0)
    return dict(entities=entities, entity_state=entity_state, relations=relations, relation_state=relation_state, head_rows=head_rows, relation_ids=relation_ids, tail_rows=tail_rows, neg_rows=neg_rows, edge_counts=edge_counts, matching=matching)


step_rate = 0.3
epsilon = 1e-08
full_precision = lax.Precision.HIGHEST

def tail_query(head_cols, rel_cols):
    half_width = head_cols.shape[0] // 2
    head_re, head_im = (head_cols[:half_width], head_cols[half_width:])
    rel_re, rel_im = (rel_cols[:half_width], rel_cols[half_width:])
    return jnp.concatenate([head_re * rel_re - head_im * rel_im, head_re * rel_im + head_im * rel_re], axis=0)

def head_query(tail_cols, rel_cols):
    half_width = tail_cols.shape[0] // 2
    tail_re, tail_im = (tail_cols[:half_width], tail_cols[half_width:])
    rel_re, rel_im = (rel_cols[:half_width], rel_cols[half_width:])
    return jnp.concatenate([rel_re * tail_re + rel_im * tail_im, rel_re * tail_im - rel_im * tail_re], axis=0)

def pair_scores(query, candidates):
    return lax.dot_general(query, candidates, (((0,), (0,)), ((), ())), precision=full_precision, preferred_element_type=jnp.float32)

def group_loss(head_blk, tail_blk, rel_table, head_idx, rel_idx, tail_idx, live_mask, tail_negs, head_negs):
    head_cols = jnp.take(head_blk, head_idx, axis=1)
    tail_cols = jnp.take(tail_blk, tail_idx, axis=1)
    rel_cols = jnp.take(rel_table, rel_idx, axis=1)
    query_tail = tail_query(head_cols, rel_cols)
    query_head = head_query(tail_cols, rel_cols)
    positive = lax.optimization_barrier(jnp.sum(query_tail * tail_cols, axis=0))
    tail_scores = pair_scores(query_tail, jnp.take(tail_blk, tail_negs, axis=1))
    head_scores = pair_scores(query_head, jnp.take(head_blk, head_negs, axis=1))
    negatives = lax.optimization_barrier(jnp.sum(jax.nn.softplus(tail_scores), axis=1)) + lax.optimization_barrier(jnp.sum(jax.nn.softplus(head_scores), axis=1))
    per_edge = jax.nn.softplus(-positive) + negatives / tail_negs.shape[0]
    return jnp.sum(per_edge * live_mask)

def bucket_loss(head_blk, tail_blk, rel_table, head_idx, rel_idx, tail_idx, live_count, negatives):
    total = jnp.zeros((), jnp.float32)
    for block in range(GROUPS):
        first_edge = block * GROUP
        slots = first_edge + jnp.arange(GROUP, dtype=jnp.int32)
        live_mask = (slots < live_count).astype(jnp.float32)
        total = total + group_loss(head_blk, tail_blk, rel_table, head_idx[first_edge:first_edge + GROUP], rel_idx[first_edge:first_edge + GROUP], tail_idx[first_edge:first_edge + GROUP], live_mask, negatives[block, 0], negatives[block, 1])
    return total

def reference(entities, entity_state, relations, relation_state, head_rows, relation_ids, tail_rows, neg_rows, edge_counts, matching):
    blocks = entities.reshape(DIM, N_DOM, ROWS_DEV).transpose(1, 0, 2)
    gradient_fn = jax.grad(bucket_loss, argnums=(0, 1, 2))

    def train_bucket(rel_total, bucket):
        partner = matching[bucket]
        head_blk = blocks[bucket]
        tail_blk = blocks[partner]
        grad_head, grad_tail, grad_rel = gradient_fn(head_blk, tail_blk, relations, head_rows[bucket], relation_ids[bucket], tail_rows[bucket], edge_counts[bucket], neg_rows[bucket])
        return (rel_total + grad_rel, (grad_head, grad_tail))
    rel_total, (grad_heads, grad_tails) = lax.scan(train_bucket, jnp.zeros((DIM, NREL), jnp.float32), jnp.arange(N_DOM, dtype=jnp.int32))
    combined = grad_heads + jnp.take(grad_tails, matching, axis=0)
    state_blocks = entity_state.reshape(N_DOM, ROWS_DEV) + lax.optimization_barrier(jnp.mean(combined * combined, axis=1))
    updated = blocks - step_rate * combined / jnp.sqrt(state_blocks + epsilon)[:, None, :]
    new_entities = updated.transpose(1, 0, 2).reshape(DIM, N_DOM * ROWS_DEV)
    new_entity_state = state_blocks.reshape(N_DOM * ROWS_DEV)
    new_relation_state = relation_state + lax.optimization_barrier(jnp.mean(rel_total * rel_total, axis=0))
    new_relations = relations - step_rate * rel_total / jnp.sqrt(new_relation_state + epsilon)
    return (new_entities, new_entity_state, new_relations, new_relation_state)
```

```python
import jax
import jax.numpy as jnp
from jax import lax
from jax.sharding import PartitionSpec as P

GROUP = 1024
TILE = 128
STEP_RATE = 0.3
EPSILON = 1e-08
FULL = lax.Precision.HIGHEST

CORE = (0, 1)
Z = (1, 3)
Y = (4, 2)
X = (6, 2)


def xor_permute(value, mask):
    size = lax.axis_size("dom")
    return lax.ppermute(value, "dom", [(i, i ^ mask) for i in range(size)])


def partner_exchange(value, xor_value, low, width):
    pick = (xor_value >> low) & (2**width - 1)
    branches = [lambda v, m=m: xor_permute(v, m << low) if m else v for m in range(2**width)]
    return lax.switch(pick, branches, value)


def members(axis, cores):
    low, width = axis
    mask = (2**width - 1) << low
    size = lax.axis_size("dom")
    return [
        [base | (k << low) for k in range(2**width)]
        for base in range(size)
        if base & mask == 0 and (base & 1) in cores
    ]


def swap_chunks(value, groups):
    return lax.all_to_all(value, "dom", 0, 0, axis_index_groups=groups, tiled=True)


def scatter_sum(value, groups):
    ways = len(groups[0])
    moved = swap_chunks(value, groups)
    return jnp.sum(moved.reshape((ways, value.shape[0] // ways) + value.shape[1:]), axis=0)


def spread(value, groups):
    ways = len(groups[0])
    copies = jnp.broadcast_to(value[None], (ways,) + value.shape)
    return swap_chunks(copies.reshape((ways * value.shape[0],) + value.shape[1:]), groups)


def update_relations(grad_tiles, relations, relation_state):
    me = lax.axis_index("dom")
    core, cy, cx = me & 1, (me >> 4) & 3, (me >> 6) & 3
    tiles, width, _ = grad_tiles.shape
    half = tiles // 2
    first = members(X, (0,)) + members(Y, (1,))
    second = members(Y, (0,)) + members(X, (1,))
    along_z = members(Z, (0, 1))

    keep = lax.dynamic_slice_in_dim(grad_tiles, core * half, half)
    send = lax.dynamic_slice_in_dim(grad_tiles, (1 - core) * half, half)
    part = keep + xor_permute(send, 1)
    part = scatter_sum(part, first)
    part = scatter_sum(part, second)
    owned = part.shape[0]
    flat = part.reshape(owned * width // 8, 8, TILE)
    rows = flat.shape[0]
    flat = jnp.pad(flat, ((0, -rows % 8), (0, 0), (0, 0)))
    flat = spread(scatter_sum(flat, along_z), along_z)
    total = flat[:rows].reshape(owned, width, TILE).transpose(1, 0, 2).reshape(width, owned * TILE)

    outer = jnp.where(core == 0, cx, cy)
    inner = jnp.where(core == 0, cy, cx)
    start = (core * half + outer * (half // 4) + inner * owned) * TILE
    values = lax.dynamic_slice_in_dim(relations, start, owned * TILE, 1)
    state = lax.dynamic_slice_in_dim(relation_state, start, owned * TILE)
    new_state = state + jnp.mean(total * total, axis=0)
    new_values = values - STEP_RATE * total / jnp.sqrt(new_state + EPSILON)[None, :]
    packed = jnp.concatenate([new_values, jnp.broadcast_to(new_state[None], (8, owned * TILE))], axis=0)
    packed = packed.reshape(width + 8, owned, TILE).transpose(1, 0, 2)
    packed = spread(packed, second)
    packed = spread(packed, first)
    other = xor_permute(packed, 1)
    low = jnp.where(core == 0, packed, other)
    high = jnp.where(core == 0, other, packed)
    count = relations.shape[1]
    both = jnp.concatenate([low, high[: count // TILE - half]], axis=0)
    new_relations = both[:, :width].transpose(1, 0, 2).reshape(width, count)
    return new_relations, both[:, width].reshape(count)


def tail_query(head_cols, rel_cols):
    half_width = head_cols.shape[0] // 2
    head_re, head_im = (head_cols[:half_width], head_cols[half_width:])
    rel_re, rel_im = (rel_cols[:half_width], rel_cols[half_width:])
    return jnp.concatenate(
        [head_re * rel_re - head_im * rel_im, head_re * rel_im + head_im * rel_re], axis=0
    )


def head_query(tail_cols, rel_cols):
    half_width = tail_cols.shape[0] // 2
    tail_re, tail_im = (tail_cols[:half_width], tail_cols[half_width:])
    rel_re, rel_im = (rel_cols[:half_width], rel_cols[half_width:])
    return jnp.concatenate(
        [rel_re * tail_re + rel_im * tail_im, rel_re * tail_im - rel_im * tail_re], axis=0
    )


def pair_scores(query, candidates):
    return lax.dot_general(
        query,
        candidates,
        (((0,), (0,)), ((), ())),
        precision=FULL,
        preferred_element_type=jnp.float32,
    )


def group_loss(
    head_blk, tail_blk, rel_table, head_idx, rel_idx, tail_idx, live_mask, tail_negs, head_negs
):
    head_cols = jnp.take(head_blk, head_idx, axis=1)
    tail_cols = jnp.take(tail_blk, tail_idx, axis=1)
    rel_cols = jnp.take(rel_table, rel_idx, axis=1)
    query_tail = tail_query(head_cols, rel_cols)
    query_head = head_query(tail_cols, rel_cols)
    positive = jnp.sum(query_tail * tail_cols, axis=0)
    tail_scores = pair_scores(query_tail, jnp.take(tail_blk, tail_negs, axis=1))
    head_scores = pair_scores(query_head, jnp.take(head_blk, head_negs, axis=1))
    negatives = jnp.sum(jax.nn.softplus(tail_scores), axis=1) + jnp.sum(
        jax.nn.softplus(head_scores), axis=1
    )
    per_edge = jax.nn.softplus(-positive) + negatives / tail_negs.shape[0]
    return jnp.sum(per_edge * live_mask)


def on_device(
    entities,
    entity_state,
    relations,
    relation_state,
    head_rows,
    relation_ids,
    tail_rows,
    neg_rows,
    edge_counts,
    matching,
):
    xor_value = jnp.bitwise_xor(matching[0], lax.axis_index("dom"))
    tail_blk = partner_exchange(entities, xor_value, 0, 4)
    tail_blk = partner_exchange(tail_blk, xor_value, 4, 4)
    live_count = edge_counts[0]
    gradient_fn = jax.grad(group_loss, argnums=(0, 1, 2))

    def add_block(block, totals):
        first_edge = block * GROUP
        head_idx = lax.dynamic_slice_in_dim(head_rows[0], first_edge, GROUP)
        rel_idx = lax.dynamic_slice_in_dim(relation_ids[0], first_edge, GROUP)
        tail_idx = lax.dynamic_slice_in_dim(tail_rows[0], first_edge, GROUP)
        negatives = lax.dynamic_index_in_dim(neg_rows[0], block, 0, keepdims=False)
        slots = first_edge + jnp.arange(GROUP, dtype=jnp.int32)
        live_mask = (slots < live_count).astype(jnp.float32)
        block_grads = gradient_fn(
            entities,
            tail_blk,
            relations,
            head_idx,
            rel_idx,
            tail_idx,
            live_mask,
            negatives[0],
            negatives[1],
        )
        return (totals[0] + block_grads[0], totals[1] + block_grads[1], totals[2] + block_grads[2])

    start_grads = (jnp.zeros_like(entities), jnp.zeros_like(tail_blk), jnp.zeros_like(relations))
    totals = lax.fori_loop(0, head_rows.shape[1] // GROUP, add_block, start_grads)
    tail_grad = partner_exchange(totals[1], xor_value, 0, 4)
    tail_grad = partner_exchange(tail_grad, xor_value, 4, 4)
    combined = totals[0] + tail_grad
    new_entity_state = entity_state + jnp.mean(combined * combined, axis=0)
    new_entities = entities - STEP_RATE * combined / jnp.sqrt(new_entity_state + EPSILON)[None, :]

    width, count = relations.shape
    tiles = -(-count // (64 * TILE)) * 64
    grad = jnp.pad(totals[2], ((0, 0), (0, tiles * TILE - count)))
    grad_tiles = grad.reshape(width, tiles, TILE).transpose(1, 0, 2)
    new_relations, new_relation_state = update_relations(grad_tiles, relations, relation_state)
    return (new_entities, new_entity_state, new_relations, new_relation_state)


def solution(mesh):
    in_specs = (
        P(None, "dom"),
        P("dom"),
        P(),
        P(),
        P("dom", None),
        P("dom", None),
        P("dom", None),
        P("dom", None, None, None),
        P("dom"),
        P("dom"),
    )
    out_specs = (P(None, "dom"), P("dom"), P(), P())
    return jax.shard_map(
        on_device, mesh=mesh, in_specs=in_specs, out_specs=out_specs, check_vma=False
    )
```

```python
import functools

import jax
import jax.numpy as jnp
from jax import lax
from jax.experimental import pallas as pl
from jax.experimental.pallas import tpu as pltpu
from jax.sharding import PartitionSpec as P

TILE = 128
HALF = 104
PART = 2 * HALF
VMEM_LIMIT = 48 * 2**20
STEP_RATE = 0.3
EPSILON = 1e-08

CORE = (0, 1)
Z = (1, 3)
Y = (4, 2)
X = (6, 2)


def xor_permute(value, mask):
    size = lax.axis_size("dom")
    return lax.ppermute(value, "dom", [(i, i ^ mask) for i in range(size)])


def partner_exchange(value, xor_value, low, width, work, *operands):
    pick = (xor_value >> low) & (2**width - 1)

    def branch(mask, v, *rest):
        moved = xor_permute(v, mask << low) if mask else v
        return moved, work(*rest)

    branches = [functools.partial(branch, mask) for mask in range(2**width)]
    return lax.switch(pick, branches, value, *operands)


def members(axis, cores):
    low, width = axis
    mask = (2**width - 1) << low
    size = lax.axis_size("dom")
    return [
        [base | (k << low) for k in range(2**width)]
        for base in range(size)
        if base & mask == 0 and (base & 1) in cores
    ]


def swap_chunks(value, groups):
    return lax.all_to_all(value, "dom", 0, 0, axis_index_groups=groups, tiled=True)


def scatter_sum(value, groups):
    ways = len(groups[0])
    moved = swap_chunks(value, groups)
    return jnp.sum(moved.reshape((ways, value.shape[0] // ways) + value.shape[1:]), axis=0)


def spread(value, groups):
    ways = len(groups[0])
    copies = jnp.broadcast_to(value[None], (ways,) + value.shape)
    return swap_chunks(copies.reshape((ways * value.shape[0],) + value.shape[1:]), groups)


def update_relations(keep, received, relations, relation_state):
    me = lax.axis_index("dom")
    core, cy, cx = me & 1, (me >> 4) & 3, (me >> 6) & 3
    half, width, _ = keep.shape
    first = members(X, (0,)) + members(Y, (1,))
    second = members(Y, (0,)) + members(X, (1,))
    along_z = members(Z, (0, 1))

    part = keep + received
    part = scatter_sum(part, first)
    part = scatter_sum(part, second)
    owned = part.shape[0]
    flat = part.reshape(owned * width // 8, 8, TILE)
    rows = flat.shape[0]
    flat = jnp.pad(flat, ((0, -rows % 8), (0, 0), (0, 0)))
    flat = spread(scatter_sum(flat, along_z), along_z)
    total = flat[:rows].reshape(owned, width, TILE).transpose(1, 0, 2).reshape(width, owned * TILE)

    outer = jnp.where(core == 0, cx, cy)
    inner = jnp.where(core == 0, cy, cx)
    start = (core * half + outer * (half // 4) + inner * owned) * TILE
    values = lax.dynamic_slice_in_dim(relations, start, owned * TILE, 1)
    state = lax.dynamic_slice_in_dim(relation_state, start, owned * TILE)
    new_state = state + jnp.mean(total * total, axis=0)
    new_values = values - STEP_RATE * total / jnp.sqrt(new_state + EPSILON)[None, :]
    packed = jnp.concatenate([new_values, jnp.broadcast_to(new_state[None], (8, owned * TILE))], axis=0)
    packed = packed.reshape(width + 8, owned, TILE).transpose(1, 0, 2)
    packed = spread(packed, second)
    packed = spread(packed, first)
    other = xor_permute(packed, 1)
    low = jnp.where(core == 0, packed, other)
    high = jnp.where(core == 0, other, packed)
    count = relations.shape[1]
    both = jnp.concatenate([low, high[: count // TILE - half]], axis=0)
    new_relations = both[:, :width].transpose(1, 0, 2).reshape(width, count)
    return new_relations, both[:, width].reshape(count)


def split_parts(x):
    high = x.astype(jnp.bfloat16)
    low = (x - high.astype(jnp.float32)).astype(jnp.bfloat16)
    return high, low


def dot(a, b):
    return jnp.dot(a, b, preferred_element_type=jnp.float32)


def dot_nt(a, b):
    return lax.dot_general(a, b, (((1,), (1,)), ((), ())), preferred_element_type=jnp.float32)


def one_hot(condition):
    return jnp.where(condition, 1.0, 0.0).astype(jnp.bfloat16)


def gather_kernel(first_slot, live_ref, ids_ref, table_ref, out_ref, parts):
    width, count = table_ref.shape
    high, low = split_parts(table_ref[...])
    blank = jnp.zeros((PART - width, count), jnp.bfloat16)
    parts[:PART, :] = jnp.concatenate([high, blank], axis=0)
    parts[PART:, :] = jnp.concatenate([low, blank], axis=0)
    edges = ids_ref.shape[1]
    chunk = 256
    half = width // 2

    @pl.loop(0, edges // chunk)
    def _(c):
        at = pl.ds(pl.multiple_of(c * chunk, chunk), chunk)
        slots = first_slot + c * chunk + lax.broadcasted_iota(jnp.int32, (1, chunk), 1)
        ids = jnp.where(slots < live_ref[0], ids_ref[:, at], -1)
        hot = one_hot(lax.broadcasted_iota(jnp.int32, (count, chunk), 0) == ids)
        cols = dot(parts[...], hot)
        cols = cols[:PART] + cols[PART:]
        out_ref[:HALF, at] = cols[:HALF]
        out_ref[HALF:, at] = cols[half : half + HALF]


def gather_relations(live, ids, relations, first_slot):
    width, count = relations.shape
    edges = ids.shape[1]
    return pl.pallas_call(
        functools.partial(gather_kernel, first_slot),
        out_shape=jax.ShapeDtypeStruct((PART, edges), jnp.float32),
        in_specs=[
            pl.BlockSpec(memory_space=pltpu.SMEM),
            pl.BlockSpec(memory_space=pltpu.VMEM),
            pl.BlockSpec(memory_space=pltpu.VMEM),
        ],
        out_specs=pl.BlockSpec(memory_space=pltpu.VMEM),
        scratch_shapes=[pltpu.VMEM((2 * PART, count), jnp.bfloat16)],
        compiler_params=pltpu.CompilerParams(vmem_limit_bytes=VMEM_LIMIT),
        cost_estimate=pl.CostEstimate(
            flops=4 * PART * count * edges, bytes_accessed=width * count * 4, transcendentals=0
        ),
        name="gather_relations",
    )(live, ids, relations)


def padded_halves(block):
    half = block.shape[0] // 2
    blank = jnp.zeros((HALF - half, block.shape[1]), block.dtype)
    return jnp.concatenate([block[:half], blank, block[half:], blank], axis=0)


def edge_kernel(
    live_ref, heads_ref, tails_ref, negs_ref, head_ref, tail_ref, rels_ref,
    head_grad_ref, tail_grad_ref, rel_grad_ref,
    cols_ref, flip_ref, wide_ref, query_ref, weight_ref, counts_ref, sums_ref,
):
    width, rows = head_ref.shape
    edges = heads_ref.shape[1]
    chunk = weight_ref.shape[1]
    groups = negs_ref.shape[0]
    half = width // 2

    for side, ref in enumerate((head_ref, tail_ref)):
        block = padded_halves(ref[...])
        high, low = split_parts(block)
        cols_ref[side, :PART, :] = high
        cols_ref[side, PART:, :] = low
        wide_ref[side, :, :rows] = high
        wide_ref[side, :, rows : 2 * rows] = high
        wide_ref[side, :, 2 * rows :] = low
        turned = jnp.concatenate([block, jnp.zeros((256 - PART, rows), jnp.float32)], axis=0).T
        high, low = split_parts(turned)
        flip_ref[side, :, :256] = high
        flip_ref[side, :, 256:512] = high
        flip_ref[side, :, 512:] = low
    for group in range(groups):
        for which in range(2):
            hits = lax.broadcasted_iota(jnp.int32, (rows, negs_ref.shape[-1]), 0) == negs_ref[group, which][None, :]
            count = jnp.sum(jnp.where(hits, 1.0 / negs_ref.shape[-1], 0.0), axis=1, keepdims=True)
            counts_ref[group, which] = jnp.broadcast_to(count, (rows, 128))
    query_ref[...] = jnp.zeros_like(query_ref)
    sums_ref[...] = jnp.zeros_like(sums_ref)

    def put_query(side, query):
        high, low = split_parts(query)
        query_ref[side, :PART, :] = high
        query_ref[side, 256 : 256 + PART, :] = low
        query_ref[side, 512 : 512 + PART, :] = high

    def put_weight(side, weight):
        high, low = split_parts(weight)
        weight_ref[side * 3 * rows : side * 3 * rows + rows, :] = high
        weight_ref[side * 3 * rows + rows : side * 3 * rows + 2 * rows, :] = low
        weight_ref[side * 3 * rows + 2 * rows : side * 3 * rows + 3 * rows, :] = high

    def add_sums(side, left, right, left_again, right_low):
        both = dot_nt(left, right)
        total = both[:PART] + both[256 : 256 + PART]
        if left_again is not None:
            total = total + dot_nt(left_again, right_low)
        sums_ref[side] += total

    @pl.loop(0, edges // chunk)
    def _(c):
        at = pl.ds(pl.multiple_of(c * chunk, chunk), chunk)
        group = c // (edges // groups // chunk)
        slots = c * chunk + lax.broadcasted_iota(jnp.int32, (1, chunk), 1)
        alive = slots < live_ref[0]
        heads = jnp.where(alive, heads_ref[:, at], -1)
        tails = jnp.where(alive, tails_ref[:, at], -1)
        row = lax.broadcasted_iota(jnp.int32, (rows, chunk), 0)
        head_hot = one_hot(row == heads)
        tail_is = row == tails
        tail_hot = one_hot(tail_is)
        h = dot(cols_ref[0], head_hot)
        h = h[:PART] + h[PART:]
        t = dot(cols_ref[1], tail_hot)
        t = t[:PART] + t[PART:]
        r = rels_ref[:, at]
        h_re, h_im, t_re, t_im, r_re, r_im = h[:HALF], h[HALF:], t[:HALF], t[HALF:], r[:HALF], r[HALF:]
        put_query(0, jnp.concatenate([r_re * t_re + r_im * t_im, r_re * t_im - r_im * t_re], axis=0))
        put_query(1, jnp.concatenate([h_re * r_re - h_im * r_im, h_re * r_im + h_im * r_re], axis=0))
        grads = []
        for side in range(2):
            scores = dot(flip_ref[side], query_ref[side])
            chance = 0.5 * jnp.tanh(0.5 * scores) + 0.5
            count = counts_ref[group, 1 - side][:, :1]
            if side == 0:
                weight = chance * count
            else:
                hot = jnp.where(tail_is, 1.0, 0.0)
                weight = chance * (count + hot) - hot
            put_weight(side, weight)
            base = side * 3 * rows
            grads.append(dot(wide_ref[side], weight_ref[base : base + 3 * rows, :]))
            add_sums(
                side, query_ref[side, : 256 + PART, :], weight_ref[base : base + rows, :],
                query_ref[side, :PART, :], weight_ref[base + rows : base + 2 * rows, :],
            )
        qh_re, qh_im, qt_re, qt_im = grads[0][:HALF], grads[0][HALF:], grads[1][:HALF], grads[1][HALF:]
        dh = jnp.concatenate([qt_re * r_re + qt_im * r_im, qt_im * r_re - qt_re * r_im], axis=0)
        dt = jnp.concatenate([qh_re * r_re - qh_im * r_im, qh_re * r_im + qh_im * r_re], axis=0)
        dr = jnp.concatenate(
            [
                qt_re * h_re + qt_im * h_im + qh_re * t_re + qh_im * t_im,
                qt_im * h_re - qt_re * h_im + qh_re * t_im - qh_im * t_re,
            ],
            axis=0,
        )
        high, low = split_parts(dr)
        rel_grad_ref[:PART, at] = high
        rel_grad_ref[PART:, at] = low
        put_query(0, dh)
        add_sums(0, query_ref[0, : 256 + PART, :], head_hot, None, None)
        put_query(1, dt)
        add_sums(1, query_ref[1, : 256 + PART, :], tail_hot, None, None)

    for side, ref in enumerate((head_grad_ref, tail_grad_ref)):
        ref[:half, :] = sums_ref[side, :half, :]
        ref[half:, :] = sums_ref[side, HALF : HALF + half, :]


def edge_gradients(live, heads, tails, negs, head_blk, tail_blk, rels):
    width, rows = head_blk.shape
    edges = heads.shape[1]
    chunk = 512
    vmem = pl.BlockSpec(memory_space=pltpu.VMEM)
    return pl.pallas_call(
        edge_kernel,
        out_shape=(
            jax.ShapeDtypeStruct((width, rows), jnp.float32),
            jax.ShapeDtypeStruct((width, rows), jnp.float32),
            jax.ShapeDtypeStruct((2 * PART, edges), jnp.bfloat16),
        ),
        in_specs=[pl.BlockSpec(memory_space=pltpu.SMEM)] + [vmem] * 6,
        out_specs=(vmem, vmem, vmem),
        scratch_shapes=[
            pltpu.VMEM((2, 2 * PART, rows), jnp.bfloat16),
            pltpu.VMEM((2, rows, 768), jnp.bfloat16),
            pltpu.VMEM((2, PART, 3 * rows), jnp.bfloat16),
            pltpu.VMEM((2, 768, chunk), jnp.bfloat16),
            pltpu.VMEM((6 * rows, chunk), jnp.bfloat16),
            pltpu.VMEM((negs.shape[0], 2, rows, 128), jnp.float32),
            pltpu.VMEM((2, PART, rows), jnp.float32),
        ],
        compiler_params=pltpu.CompilerParams(vmem_limit_bytes=VMEM_LIMIT),
        cost_estimate=pl.CostEstimate(
            flops=40 * PART * rows * edges, bytes_accessed=4 * PART * edges, transcendentals=2 * rows * edges
        ),
        name="edge_gradients",
    )(live, heads, tails, negs, head_blk, tail_blk, rels)


def scatter_kernel(first_ref, ids_ref, grad_ref, out_ref, spread_ref):
    tiles, width, tile = out_ref.shape
    edges = ids_ref.shape[0]
    half = width // 2
    spread_ref[...] = jnp.broadcast_to(ids_ref[...], spread_ref.shape)

    @pl.loop(0, tiles // 2)
    def _(j):
        lane = lax.broadcasted_iota(jnp.int32, (edges, tile), 1)
        start = (first_ref[0] + 2 * j) * tile
        hot = jnp.concatenate(
            [one_hot(lane + start == spread_ref[...]), one_hot(lane + (start + tile) == spread_ref[...])], axis=1
        )
        cols = dot(grad_ref[...], hot)
        cols = cols[:PART] + cols[PART:]
        for side in range(2):
            part = cols[:, side * tile : (side + 1) * tile]
            out_ref[2 * j + side, :half, :] = part[:half]
            out_ref[2 * j + side, half:, :] = part[HALF : HALF + half]


def scatter_relations(first_tile, ids, grads, tiles, width):
    edges = grads.shape[1]
    vmem = pl.BlockSpec(memory_space=pltpu.VMEM)
    return pl.pallas_call(
        scatter_kernel,
        out_shape=jax.ShapeDtypeStruct((tiles, width, TILE), jnp.float32),
        in_specs=[pl.BlockSpec(memory_space=pltpu.SMEM), vmem, vmem],
        out_specs=vmem,
        scratch_shapes=[pltpu.VMEM((edges, TILE), jnp.int32)],
        compiler_params=pltpu.CompilerParams(vmem_limit_bytes=VMEM_LIMIT),
        cost_estimate=pl.CostEstimate(
            flops=4 * PART * edges * tiles * TILE, bytes_accessed=tiles * width * TILE * 4, transcendentals=0
        ),
        name="scatter_relations",
    )(first_tile, ids, grads)


def on_device(
    entities,
    entity_state,
    relations,
    relation_state,
    head_rows,
    relation_ids,
    tail_rows,
    neg_rows,
    edge_counts,
    matching,
):
    me = lax.axis_index("dom")
    core = me & 1
    xor_value = jnp.bitwise_xor(matching[0], me)
    width, count = relations.shape
    edges = head_rows.shape[1]
    mid = edges // 2
    half = -(-count // (64 * TILE)) * 32

    def gather(first):
        ids = relation_ids[:, first : first + mid]
        return lambda live, ids, table: gather_relations(live, ids, table, first), ids

    work, ids = gather(0)
    tail_blk, rels_low = partner_exchange(entities, xor_value, 0, 4, work, edge_counts, ids, relations)
    work, ids = gather(mid)
    tail_blk, rels_high = partner_exchange(tail_blk, xor_value, 4, 4, work, edge_counts, ids, relations)
    rels = jnp.concatenate([rels_low, rels_high], axis=1)
    head_grad, tail_grad, rel_grad = edge_gradients(
        edge_counts, head_rows, tail_rows, neg_rows[0], entities, tail_blk, rels
    )

    column = relation_ids.reshape(edges, 1)
    first_keep = (core * half).reshape(1)
    first_send = ((1 - core) * half).reshape(1)

    def scatter(first, ids, grads):
        return scatter_relations(first, ids, grads, half, width)

    def scatter_and_swap(first, ids, grads, send):
        received = xor_permute(send, 1)
        return scatter(first, ids, grads), received

    tail_grad, send = partner_exchange(tail_grad, xor_value, 0, 4, scatter, first_send, column, rel_grad)
    tail_grad, (keep, received) = partner_exchange(
        tail_grad, xor_value, 4, 4, scatter_and_swap, first_keep, column, rel_grad, send
    )
    combined = head_grad + tail_grad
    new_entity_state = entity_state + jnp.mean(combined * combined, axis=0)
    new_entities = entities - STEP_RATE * combined / jnp.sqrt(new_entity_state + EPSILON)[None, :]
    new_relations, new_relation_state = update_relations(keep, received, relations, relation_state)
    return (new_entities, new_entity_state, new_relations, new_relation_state)


def solution(mesh):
    in_specs = (
        P(None, "dom"),
        P("dom"),
        P(),
        P(),
        P("dom", None),
        P("dom", None),
        P("dom", None),
        P("dom", None, None, None),
        P("dom"),
        P("dom"),
    )
    out_specs = (P(None, "dom"), P("dom"), P(), P())
    return jax.shard_map(
        on_device, mesh=mesh, in_specs=in_specs, out_specs=out_specs, check_vma=False
    )
```

```python
import functools

import jax
import jax.numpy as jnp
from jax import lax
from jax.experimental import pallas as pl
from jax.experimental.pallas import tpu as pltpu
from jax.sharding import PartitionSpec as P

TILE = 128
HALF = 104
PART = 2 * HALF
VMEM_LIMIT = 48 * 2**20
STEP_RATE = 0.3
EPSILON = 1e-08

CORE = (0, 1)
Z = (1, 3)
Y = (4, 2)
X = (6, 2)


def xor_permute(value, mask):
    size = lax.axis_size("dom")
    return lax.ppermute(value, "dom", [(i, i ^ mask) for i in range(size)])


def partner_exchange(value, xor_value, low, width, work, *operands):
    pick = (xor_value >> low) & (2**width - 1)

    def branch(mask, v, *rest):
        moved = xor_permute(v, mask << low) if mask else v
        return moved, work(*rest)

    branches = [functools.partial(branch, mask) for mask in range(2**width)]
    return lax.switch(pick, branches, value, *operands)


def members(axis, cores):
    low, width = axis
    mask = (2**width - 1) << low
    size = lax.axis_size("dom")
    return [
        [base | (k << low) for k in range(2**width)]
        for base in range(size)
        if base & mask == 0 and (base & 1) in cores
    ]


def swap_chunks(value, groups):
    return lax.all_to_all(value, "dom", 0, 0, axis_index_groups=groups, tiled=True)


def scatter_sum(value, groups):
    ways = len(groups[0])
    moved = swap_chunks(value, groups)
    return jnp.sum(moved.reshape((ways, value.shape[0] // ways) + value.shape[1:]), axis=0)


def spread(value, groups):
    ways = len(groups[0])
    copies = jnp.broadcast_to(value[None], (ways,) + value.shape)
    return swap_chunks(copies.reshape((ways * value.shape[0],) + value.shape[1:]), groups)


def update_relations(keep, received, relations, relation_state):
    me = lax.axis_index("dom")
    core, cy, cx = me & 1, (me >> 4) & 3, (me >> 6) & 3
    half, width, _ = keep.shape
    first = members(X, (0,)) + members(Y, (1,))
    second = members(Y, (0,)) + members(X, (1,))
    along_z = members(Z, (0, 1))

    part = keep + received
    part = scatter_sum(part, first)
    part = scatter_sum(part, second)
    owned = part.shape[0]
    flat = part.reshape(owned * width // 8, 8, TILE)
    rows = flat.shape[0]
    flat = jnp.pad(flat, ((0, -rows % 8), (0, 0), (0, 0)))
    flat = spread(scatter_sum(flat, along_z), along_z)
    total = flat[:rows].reshape(owned, width, TILE).transpose(1, 0, 2).reshape(width, owned * TILE)

    outer = jnp.where(core == 0, cx, cy)
    inner = jnp.where(core == 0, cy, cx)
    start = (core * half + outer * (half // 4) + inner * owned) * TILE
    values = lax.dynamic_slice_in_dim(relations, start, owned * TILE, 1)
    state = lax.dynamic_slice_in_dim(relation_state, start, owned * TILE)
    new_state = state + jnp.mean(total * total, axis=0)
    new_values = values - STEP_RATE * total / jnp.sqrt(new_state + EPSILON)[None, :]
    packed = jnp.concatenate([new_values, jnp.broadcast_to(new_state[None], (8, owned * TILE))], axis=0)
    packed = packed.reshape(width + 8, owned, TILE).transpose(1, 0, 2)
    packed = spread(packed, second)
    packed = spread(packed, first)
    other = xor_permute(packed, 1)
    low = jnp.where(core == 0, packed, other)
    high = jnp.where(core == 0, other, packed)
    count = relations.shape[1]
    both = jnp.concatenate([low, high[: count // TILE - half]], axis=0)
    new_relations = both[:, :width].transpose(1, 0, 2).reshape(width, count)
    return new_relations, both[:, width].reshape(count)


def split_parts(x):
    high = x.astype(jnp.bfloat16)
    low = (x - high.astype(jnp.float32)).astype(jnp.bfloat16)
    return high, low


def dot(a, b):
    return jnp.dot(a, b, preferred_element_type=jnp.float32)


def dot_nt(a, b):
    return lax.dot_general(a, b, (((1,), (1,)), ((), ())), preferred_element_type=jnp.float32)


def one_hot(condition):
    return jnp.where(condition, 1.0, 0.0).astype(jnp.bfloat16)


def gather_kernel(first_slot, live_ref, ids_ref, table_ref, out_ref, table, parts, sums, ready):
    width, count = table_ref.shape
    edges = ids_ref.shape[1]
    half = width // 2
    depth = 7
    step = depth * 256
    pieces = count // step

    def piece(i, size=step):
        at = pl.ds(pl.multiple_of(i * step, 256), size)
        return pltpu.make_async_copy(table_ref.at[:, at], table.at[:, at], ready.at[i])

    rest = count - pieces * step
    for i in range(pieces):
        piece(i).start()
    if rest:
        piece(pieces, rest).start()
    sums[...] = jnp.zeros_like(sums)

    def add_tiles(i, tiles):
        @pl.loop(0, tiles)
        def _(k):
            at = pl.ds(pl.multiple_of(i * step + k * 256, 256), 256)
            tile = jnp.concatenate([table[:, at], jnp.zeros((PART - width, 256), jnp.float32)], axis=0)
            there = pl.ds(pl.multiple_of(k * 256, 256), 256)
            high, low = split_parts(tile)
            parts[:PART, there] = high
            parts[PART:, there] = low

        @pl.loop(0, edges // 256)
        def _(c):
            there = pl.ds(pl.multiple_of(c * 256, 256), 256)
            slots = first_slot + c * 256 + lax.broadcasted_iota(jnp.int32, (1, 256), 1)
            ids = jnp.where(slots < live_ref[0], ids_ref[:, there], -1) - i * step
            row = lax.broadcasted_iota(jnp.int32, (256, 256), 0)
            cols = sums[:, there]
            for k in range(tiles):
                cols += dot(parts[:, k * 256 : (k + 1) * 256], one_hot(row + k * 256 == ids))
            sums[:, there] = cols

    @pl.loop(0, pieces)
    def _(i):
        piece(i).wait()
        add_tiles(i, depth)

    if rest:
        piece(pieces, rest).wait()
        add_tiles(pieces, rest // 256)

    @pl.loop(0, edges // 256)
    def _(c):
        there = pl.ds(pl.multiple_of(c * 256, 256), 256)
        cols = sums[:PART, there] + sums[PART:, there]
        out_ref[:HALF, there] = cols[:HALF]
        out_ref[HALF:, there] = cols[half : half + HALF]


def gather_relations(live, ids, relations, first_slot):
    width, count = relations.shape
    edges = ids.shape[1]
    vmem = pl.BlockSpec(memory_space=pltpu.VMEM)
    return pl.pallas_call(
        functools.partial(gather_kernel, first_slot),
        out_shape=jax.ShapeDtypeStruct((PART, edges), jnp.float32),
        in_specs=[pl.BlockSpec(memory_space=pltpu.SMEM), vmem, pl.BlockSpec(memory_space=pl.ANY)],
        out_specs=vmem,
        scratch_shapes=[
            pltpu.VMEM((width, count), jnp.float32),
            pltpu.VMEM((2 * PART, 7 * 256), jnp.bfloat16),
            pltpu.VMEM((2 * PART, edges), jnp.float32),
            pltpu.SemaphoreType.DMA((8,)),
        ],
        compiler_params=pltpu.CompilerParams(vmem_limit_bytes=VMEM_LIMIT),
        cost_estimate=pl.CostEstimate(
            flops=4 * PART * count * edges, bytes_accessed=width * count * 4, transcendentals=0
        ),
        name="gather_relations",
    )(live, ids, relations)


def padded_halves(block):
    half = block.shape[0] // 2
    blank = jnp.zeros((HALF - half, block.shape[1]), block.dtype)
    return jnp.concatenate([block[:half], blank, block[half:], blank], axis=0)


def edge_kernel(
    live_ref, heads_ref, tails_ref, negs_ref, head_ref, tail_ref, rels_ref,
    head_grad_ref, tail_grad_ref, rel_grad_ref,
    cols_ref, flip_ref, wide_ref, query_ref, weight_ref, counts_ref, sums_ref,
):
    width, rows = head_ref.shape
    edges = heads_ref.shape[1]
    chunk = weight_ref.shape[1]
    groups = negs_ref.shape[0]
    half = width // 2

    for side, ref in enumerate((head_ref, tail_ref)):
        block = padded_halves(ref[...])
        high, low = split_parts(block)
        cols_ref[side, :PART, :] = high
        cols_ref[side, PART:, :] = low
        wide_ref[side, :, :rows] = high
        wide_ref[side, :, rows : 2 * rows] = high
        wide_ref[side, :, 2 * rows :] = low
        turned = jnp.concatenate([block, jnp.zeros((256 - PART, rows), jnp.float32)], axis=0).T
        high, low = split_parts(turned)
        flip_ref[side, :, :256] = high
        flip_ref[side, :, 256:512] = high
        flip_ref[side, :, 512:] = low
    for group in range(groups):
        for which in range(2):
            hits = lax.broadcasted_iota(jnp.int32, (rows, negs_ref.shape[-1]), 0) == negs_ref[group, which][None, :]
            count = jnp.sum(jnp.where(hits, 1.0 / negs_ref.shape[-1], 0.0), axis=1, keepdims=True)
            counts_ref[group, which] = jnp.broadcast_to(count, (rows, 128))
    query_ref[...] = jnp.zeros_like(query_ref)
    sums_ref[...] = jnp.zeros_like(sums_ref)

    def put_query(side, query):
        high, low = split_parts(query)
        query_ref[side, :PART, :] = high
        query_ref[side, 256 : 256 + PART, :] = low
        query_ref[side, 512 : 512 + PART, :] = high

    def put_weight(side, weight):
        high, low = split_parts(weight)
        weight_ref[side * 3 * rows : side * 3 * rows + rows, :] = high
        weight_ref[side * 3 * rows + rows : side * 3 * rows + 2 * rows, :] = low
        weight_ref[side * 3 * rows + 2 * rows : side * 3 * rows + 3 * rows, :] = high

    def add_sums(side, left, right, left_again, right_low):
        both = dot_nt(left, right)
        total = both[:PART] + both[256 : 256 + PART]
        if left_again is not None:
            total = total + dot_nt(left_again, right_low)
        sums_ref[side] += total

    @pl.loop(0, edges // chunk)
    def _(c):
        at = pl.ds(pl.multiple_of(c * chunk, chunk), chunk)
        group = c // (edges // groups // chunk)
        slots = c * chunk + lax.broadcasted_iota(jnp.int32, (1, chunk), 1)
        alive = slots < live_ref[0]
        heads = jnp.where(alive, heads_ref[:, at], -1)
        tails = jnp.where(alive, tails_ref[:, at], -1)
        row = lax.broadcasted_iota(jnp.int32, (rows, chunk), 0)
        head_hot = one_hot(row == heads)
        tail_is = row == tails
        tail_hot = one_hot(tail_is)
        h = dot(cols_ref[0], head_hot)
        h = h[:PART] + h[PART:]
        t = dot(cols_ref[1], tail_hot)
        t = t[:PART] + t[PART:]
        r = rels_ref[:, at]
        h_re, h_im, t_re, t_im, r_re, r_im = h[:HALF], h[HALF:], t[:HALF], t[HALF:], r[:HALF], r[HALF:]
        put_query(0, jnp.concatenate([r_re * t_re + r_im * t_im, r_re * t_im - r_im * t_re], axis=0))
        put_query(1, jnp.concatenate([h_re * r_re - h_im * r_im, h_re * r_im + h_im * r_re], axis=0))
        grads = []
        for side in range(2):
            scores = dot(flip_ref[side], query_ref[side])
            chance = 0.5 * jnp.tanh(0.5 * scores) + 0.5
            count = counts_ref[group, 1 - side][:, :1]
            if side == 0:
                weight = chance * count
            else:
                hot = jnp.where(tail_is, 1.0, 0.0)
                weight = chance * (count + hot) - hot
            put_weight(side, weight)
            base = side * 3 * rows
            grads.append(dot(wide_ref[side], weight_ref[base : base + 3 * rows, :]))
            add_sums(
                side, query_ref[side, : 256 + PART, :], weight_ref[base : base + rows, :],
                query_ref[side, :PART, :], weight_ref[base + rows : base + 2 * rows, :],
            )
        qh_re, qh_im, qt_re, qt_im = grads[0][:HALF], grads[0][HALF:], grads[1][:HALF], grads[1][HALF:]
        dh = jnp.concatenate([qt_re * r_re + qt_im * r_im, qt_im * r_re - qt_re * r_im], axis=0)
        dt = jnp.concatenate([qh_re * r_re - qh_im * r_im, qh_re * r_im + qh_im * r_re], axis=0)
        dr = jnp.concatenate(
            [
                qt_re * h_re + qt_im * h_im + qh_re * t_re + qh_im * t_im,
                qt_im * h_re - qt_re * h_im + qh_re * t_im - qh_im * t_re,
            ],
            axis=0,
        )
        high, low = split_parts(dr)
        rel_grad_ref[:PART, at] = high
        rel_grad_ref[PART:, at] = low
        put_query(0, dh)
        add_sums(0, query_ref[0, : 256 + PART, :], head_hot, None, None)
        put_query(1, dt)
        add_sums(1, query_ref[1, : 256 + PART, :], tail_hot, None, None)

    for side, ref in enumerate((head_grad_ref, tail_grad_ref)):
        ref[:half, :] = sums_ref[side, :half, :]
        ref[half:, :] = sums_ref[side, HALF : HALF + half, :]


def edge_gradients(live, heads, tails, negs, head_blk, tail_blk, rels):
    width, rows = head_blk.shape
    edges = heads.shape[1]
    chunk = 512
    vmem = pl.BlockSpec(memory_space=pltpu.VMEM)
    return pl.pallas_call(
        edge_kernel,
        out_shape=(
            jax.ShapeDtypeStruct((width, rows), jnp.float32),
            jax.ShapeDtypeStruct((width, rows), jnp.float32),
            jax.ShapeDtypeStruct((2 * PART, edges), jnp.bfloat16),
        ),
        in_specs=[pl.BlockSpec(memory_space=pltpu.SMEM)] + [vmem] * 6,
        out_specs=(vmem, vmem, vmem),
        scratch_shapes=[
            pltpu.VMEM((2, 2 * PART, rows), jnp.bfloat16),
            pltpu.VMEM((2, rows, 768), jnp.bfloat16),
            pltpu.VMEM((2, PART, 3 * rows), jnp.bfloat16),
            pltpu.VMEM((2, 768, chunk), jnp.bfloat16),
            pltpu.VMEM((6 * rows, chunk), jnp.bfloat16),
            pltpu.VMEM((negs.shape[0], 2, rows, 128), jnp.float32),
            pltpu.VMEM((2, PART, rows), jnp.float32),
        ],
        compiler_params=pltpu.CompilerParams(vmem_limit_bytes=VMEM_LIMIT),
        cost_estimate=pl.CostEstimate(
            flops=40 * PART * rows * edges, bytes_accessed=4 * PART * edges, transcendentals=2 * rows * edges
        ),
        name="edge_gradients",
    )(live, heads, tails, negs, head_blk, tail_blk, rels)


def scatter_kernel(first_ref, ids_ref, grad_ref, out_ref, spread_ref):
    tiles, width, tile = out_ref.shape
    edges = ids_ref.shape[0]
    half = width // 2
    spread_ref[...] = jnp.broadcast_to(ids_ref[...], spread_ref.shape)

    @pl.loop(0, tiles // 2)
    def _(j):
        start = (first_ref[0] + 2 * j) * tile
        lane = lax.broadcasted_iota(jnp.int32, (256, tile), 1)
        cols = None
        for c in range(0, edges, 256):
            ids = spread_ref[c : c + 256, :]
            hot = jnp.concatenate([one_hot(lane + start == ids), one_hot(lane + (start + tile) == ids)], axis=1)
            part = dot(grad_ref[:, c : c + 256], hot)
            cols = part if cols is None else cols + part
        cols = cols[:PART] + cols[PART:]
        for side in range(2):
            part = cols[:, side * tile : (side + 1) * tile]
            out_ref[2 * j + side, :half, :] = part[:half]
            out_ref[2 * j + side, half:, :] = part[HALF : HALF + half]


def scatter_relations(first_tile, ids, grads, tiles, width):
    edges = grads.shape[1]
    vmem = pl.BlockSpec(memory_space=pltpu.VMEM)
    return pl.pallas_call(
        scatter_kernel,
        out_shape=jax.ShapeDtypeStruct((tiles, width, TILE), jnp.float32),
        in_specs=[pl.BlockSpec(memory_space=pltpu.SMEM), vmem, vmem],
        out_specs=vmem,
        scratch_shapes=[pltpu.VMEM((edges, TILE), jnp.int32)],
        compiler_params=pltpu.CompilerParams(vmem_limit_bytes=VMEM_LIMIT),
        cost_estimate=pl.CostEstimate(
            flops=4 * PART * edges * tiles * TILE, bytes_accessed=tiles * width * TILE * 4, transcendentals=0
        ),
        name="scatter_relations",
    )(first_tile, ids, grads)


def on_device(
    entities,
    entity_state,
    relations,
    relation_state,
    head_rows,
    relation_ids,
    tail_rows,
    neg_rows,
    edge_counts,
    matching,
):
    me = lax.axis_index("dom")
    core = me & 1
    xor_value = jnp.bitwise_xor(matching[0], me)
    width, count = relations.shape
    edges = head_rows.shape[1]
    mid = edges // 2
    half = -(-count // (64 * TILE)) * 32

    def gather(first):
        ids = relation_ids[:, first : first + mid]
        return lambda live, ids, table: gather_relations(live, ids, table, first), ids

    work, ids = gather(0)
    tail_blk, rels_low = partner_exchange(entities, xor_value, 0, 4, work, edge_counts, ids, relations)
    work, ids = gather(mid)
    tail_blk, rels_high = partner_exchange(tail_blk, xor_value, 4, 4, work, edge_counts, ids, relations)
    rels = jnp.concatenate([rels_low, rels_high], axis=1)
    head_grad, tail_grad, rel_grad = edge_gradients(
        edge_counts, head_rows, tail_rows, neg_rows[0], entities, tail_blk, rels
    )

    column = relation_ids.reshape(edges, 1)
    first_keep = (core * half).reshape(1)
    first_send = ((1 - core) * half).reshape(1)

    def scatter(first, ids, grads):
        return scatter_relations(first, ids, grads, half, width)

    def scatter_and_swap(first, ids, grads, send):
        received = xor_permute(send, 1)
        return scatter(first, ids, grads), received

    tail_grad, send = partner_exchange(tail_grad, xor_value, 0, 4, scatter, first_send, column, rel_grad)
    tail_grad, (keep, received) = partner_exchange(
        tail_grad, xor_value, 4, 4, scatter_and_swap, first_keep, column, rel_grad, send
    )
    combined = head_grad + tail_grad
    new_entity_state = entity_state + jnp.mean(combined * combined, axis=0)
    new_entities = entities - STEP_RATE * combined / jnp.sqrt(new_entity_state + EPSILON)[None, :]
    new_relations, new_relation_state = update_relations(keep, received, relations, relation_state)
    return (new_entities, new_entity_state, new_relations, new_relation_state)


def solution(mesh):
    in_specs = (
        P(None, "dom"),
        P("dom"),
        P(),
        P(),
        P("dom", None),
        P("dom", None),
        P("dom", None),
        P("dom", None, None, None),
        P("dom"),
        P("dom"),
    )
    out_specs = (P(None, "dom"), P("dom"), P(), P())
    return jax.shard_map(
        on_device, mesh=mesh, in_specs=in_specs, out_specs=out_specs, check_vma=False
    )
```

```python
import functools

import jax
import jax.numpy as jnp
from jax import lax
from jax.experimental import pallas as pl
from jax.experimental.pallas import tpu as pltpu
from jax.sharding import PartitionSpec as P

TILE = 128
HALF = 104
PART = 2 * HALF
VMEM_LIMIT = 48 * 2**20
STEP_RATE = 0.3
EPSILON = 1e-08


def pair_permute(value, low_mask, high_mask):
    size = lax.axis_size("dom")
    return lax.ppermute(value, "dom", [(i, i ^ (high_mask if i & 1 else low_mask)) for i in range(size)])


def xor_permute(value, mask):
    return pair_permute(value, mask, mask)


def outer_permute(value, k):
    return pair_permute(value, k << 6, k << 4)


def inner_permute(value, k):
    return pair_permute(value, k << 4, k << 6)


def partner_exchange(value, xor_value, low, width, work, *operands):
    pick = (xor_value >> low) & (2**width - 1)

    def branch(mask, v, *rest):
        moved = xor_permute(v, mask << low) if mask else v
        return moved, work(*rest)

    branches = [functools.partial(branch, mask) for mask in range(2**width)]
    return lax.switch(pick, branches, value, *operands)


def z_groups():
    size = lax.axis_size("dom")
    return [[base | (k << 1) for k in range(8)] for base in range(size) if base & 14 == 0]


def z_swap(value):
    return lax.all_to_all(value, "dom", 0, 0, axis_index_groups=z_groups(), tiled=True)


def z_total(part):
    rows = part.shape[0]
    flat = jnp.pad(part, ((0, -rows % 8), (0, 0), (0, 0)))
    share = flat.shape[0] // 8
    mine = jnp.sum(z_swap(flat).reshape(8, share, 8, TILE), axis=0)
    return z_swap(jnp.tile(mine, (8, 1, 1)))[:rows]


def update_relations(place, keep, received, relations, relation_state):
    half, width, _ = keep.shape
    chunk, owned = half // 4, half // 16
    parts = [keep[k * chunk : (k + 1) * chunk] + received[k * chunk : (k + 1) * chunk] for k in range(4)]
    moved = [outer_permute(parts[k], k) for k in (1, 2, 3)]
    part = parts[0] + moved[0] + moved[1] + moved[2]
    moved = [inner_permute(part[k * owned : (k + 1) * owned], k) for k in (1, 2, 3)]
    part = part[:owned] + moved[0] + moved[1] + moved[2]
    total = z_total(part.reshape(owned * width // 8, 8, TILE))
    total = total.reshape(owned, width, TILE).transpose(1, 0, 2).reshape(width, owned * TILE)

    start = tile_at(0, place, place[0]) * TILE
    values = lax.dynamic_slice_in_dim(relations, start, owned * TILE, 1)
    state = lax.dynamic_slice_in_dim(relation_state, start, owned * TILE)
    new_state = state + jnp.mean(total * total, axis=0)
    new_values = values - STEP_RATE * total / jnp.sqrt(new_state + EPSILON)[None, :]
    packed = jnp.concatenate([new_values, jnp.broadcast_to(new_state[None], (8, owned * TILE))], axis=0)
    packed = packed.reshape(width + 8, owned, TILE).transpose(1, 0, 2)
    packed = jnp.concatenate([packed] + [inner_permute(packed, k) for k in (1, 2, 3)], axis=0)
    mine = [packed] + [outer_permute(packed, k) for k in (1, 2, 3)]
    others = [xor_permute(value, 1) for value in mine]
    new_relations, state_rows = place_columns(place, mine, others, width, relations.shape[1])
    return new_relations, state_rows[0]


def split_parts(x):
    high = x.astype(jnp.bfloat16)
    low = (x - high.astype(jnp.float32)).astype(jnp.bfloat16)
    return high, low


def dot(a, b):
    return jnp.dot(a, b, preferred_element_type=jnp.float32)


def dot_nt(a, b):
    return lax.dot_general(a, b, (((1,), (1,)), ((), ())), preferred_element_type=jnp.float32)


def one_hot(condition):
    return jnp.where(condition, 1.0, 0.0).astype(jnp.bfloat16)


def gather_kernel(first_slot, live_ref, ids_ref, table_ref, out_ref, table, parts, sums, ready):
    width, count = table_ref.shape
    edges = ids_ref.shape[1]
    half = width // 2
    depth = 7
    step = depth * 256
    pieces = count // step

    def piece(i, size=step):
        at = pl.ds(pl.multiple_of(i * step, 256), size)
        return pltpu.make_async_copy(table_ref.at[:, at], table.at[:, at], ready.at[i])

    rest = count - pieces * step
    for i in range(pieces):
        piece(i).start()
    if rest:
        piece(pieces, rest).start()
    sums[...] = jnp.zeros_like(sums)

    def add_tiles(i, tiles):
        @pl.loop(0, tiles)
        def _(k):
            at = pl.ds(pl.multiple_of(i * step + k * 256, 256), 256)
            tile = jnp.concatenate([table[:, at], jnp.zeros((PART - width, 256), jnp.float32)], axis=0)
            there = pl.ds(pl.multiple_of(k * 256, 256), 256)
            high, low = split_parts(tile)
            parts[:PART, there] = high
            parts[PART:, there] = low

        @pl.loop(0, edges // 256)
        def _(c):
            there = pl.ds(pl.multiple_of(c * 256, 256), 256)
            slots = first_slot + c * 256 + lax.broadcasted_iota(jnp.int32, (1, 256), 1)
            ids = jnp.where(slots < live_ref[0], ids_ref[:, there], -1) - i * step
            row = lax.broadcasted_iota(jnp.int32, (256, 256), 0)
            cols = sums[:, there]
            for k in range(tiles):
                cols += dot(parts[:, k * 256 : (k + 1) * 256], one_hot(row + k * 256 == ids))
            sums[:, there] = cols

    @pl.loop(0, pieces)
    def _(i):
        piece(i).wait()
        add_tiles(i, depth)

    if rest:
        piece(pieces, rest).wait()
        add_tiles(pieces, rest // 256)

    @pl.loop(0, edges // 256)
    def _(c):
        there = pl.ds(pl.multiple_of(c * 256, 256), 256)
        cols = sums[:PART, there] + sums[PART:, there]
        out_ref[:HALF, there] = cols[:HALF]
        out_ref[HALF:, there] = cols[half : half + HALF]


def gather_relations(live, ids, relations, first_slot):
    width, count = relations.shape
    edges = ids.shape[1]
    vmem = pl.BlockSpec(memory_space=pltpu.VMEM)
    return pl.pallas_call(
        functools.partial(gather_kernel, first_slot),
        out_shape=jax.ShapeDtypeStruct((PART, edges), jnp.float32),
        in_specs=[pl.BlockSpec(memory_space=pltpu.SMEM), vmem, pl.BlockSpec(memory_space=pl.ANY)],
        out_specs=vmem,
        scratch_shapes=[
            pltpu.VMEM((width, count), jnp.float32),
            pltpu.VMEM((2 * PART, 7 * 256), jnp.bfloat16),
            pltpu.VMEM((2 * PART, edges), jnp.float32),
            pltpu.SemaphoreType.DMA((8,)),
        ],
        compiler_params=pltpu.CompilerParams(vmem_limit_bytes=VMEM_LIMIT),
        cost_estimate=pl.CostEstimate(
            flops=4 * PART * count * edges, bytes_accessed=width * count * 4, transcendentals=0
        ),
        name="gather_relations",
    )(live, ids, relations)


def padded_halves(block):
    half = block.shape[0] // 2
    blank = jnp.zeros((HALF - half, block.shape[1]), block.dtype)
    return jnp.concatenate([block[:half], blank, block[half:], blank], axis=0)


def edge_kernel(
    live_ref, heads_ref, tails_ref, negs_ref, head_ref, tail_ref, rels_ref,
    head_grad_ref, tail_grad_ref, rel_grad_ref,
    cols_ref, flip_ref, wide_ref, query_ref, weight_ref, counts_ref, sums_ref,
):
    width, rows = head_ref.shape
    edges = heads_ref.shape[1]
    chunk = weight_ref.shape[1]
    groups = negs_ref.shape[0]
    half = width // 2

    for side, ref in enumerate((head_ref, tail_ref)):
        block = padded_halves(ref[...])
        high, low = split_parts(block)
        cols_ref[side, :PART, :] = high
        cols_ref[side, PART:, :] = low
        wide_ref[side, :, :rows] = high
        wide_ref[side, :, rows : 2 * rows] = high
        wide_ref[side, :, 2 * rows :] = low
        turned = jnp.concatenate([block, jnp.zeros((256 - PART, rows), jnp.float32)], axis=0).T
        high, low = split_parts(turned)
        flip_ref[side, :, :256] = high
        flip_ref[side, :, 256:512] = high
        flip_ref[side, :, 512:] = low
    for group in range(groups):
        for which in range(2):
            hits = lax.broadcasted_iota(jnp.int32, (rows, negs_ref.shape[-1]), 0) == negs_ref[group, which][None, :]
            count = jnp.sum(jnp.where(hits, 1.0 / negs_ref.shape[-1], 0.0), axis=1, keepdims=True)
            counts_ref[group, which] = jnp.broadcast_to(count, (rows, 128))
    query_ref[...] = jnp.zeros_like(query_ref)
    sums_ref[...] = jnp.zeros_like(sums_ref)

    def put_query(side, query):
        high, low = split_parts(query)
        query_ref[side, :PART, :] = high
        query_ref[side, 256 : 256 + PART, :] = low
        query_ref[side, 512 : 512 + PART, :] = high

    def put_weight(side, weight):
        high, low = split_parts(weight)
        weight_ref[side * 3 * rows : side * 3 * rows + rows, :] = high
        weight_ref[side * 3 * rows + rows : side * 3 * rows + 2 * rows, :] = low
        weight_ref[side * 3 * rows + 2 * rows : side * 3 * rows + 3 * rows, :] = high

    def add_sums(side, left, right, left_again, right_low):
        both = dot_nt(left, right)
        total = both[:PART] + both[256 : 256 + PART]
        if left_again is not None:
            total = total + dot_nt(left_again, right_low)
        sums_ref[side] += total

    @pl.loop(0, edges // chunk)
    def _(c):
        at = pl.ds(pl.multiple_of(c * chunk, chunk), chunk)
        group = c // (edges // groups // chunk)
        slots = c * chunk + lax.broadcasted_iota(jnp.int32, (1, chunk), 1)
        alive = slots < live_ref[0]
        heads = jnp.where(alive, heads_ref[:, at], -1)
        tails = jnp.where(alive, tails_ref[:, at], -1)
        row = lax.broadcasted_iota(jnp.int32, (rows, chunk), 0)
        head_hot = one_hot(row == heads)
        tail_is = row == tails
        tail_hot = one_hot(tail_is)
        h = dot(cols_ref[0], head_hot)
        h = h[:PART] + h[PART:]
        t = dot(cols_ref[1], tail_hot)
        t = t[:PART] + t[PART:]
        r = rels_ref[:, at]
        h_re, h_im, t_re, t_im, r_re, r_im = h[:HALF], h[HALF:], t[:HALF], t[HALF:], r[:HALF], r[HALF:]
        put_query(0, jnp.concatenate([r_re * t_re + r_im * t_im, r_re * t_im - r_im * t_re], axis=0))
        put_query(1, jnp.concatenate([h_re * r_re - h_im * r_im, h_re * r_im + h_im * r_re], axis=0))
        grads = []
        for side in range(2):
            scores = dot(flip_ref[side], query_ref[side])
            chance = 0.5 * jnp.tanh(0.5 * scores) + 0.5
            count = counts_ref[group, 1 - side][:, :1]
            if side == 0:
                weight = chance * count
            else:
                hot = jnp.where(tail_is, 1.0, 0.0)
                weight = chance * (count + hot) - hot
            put_weight(side, weight)
            base = side * 3 * rows
            grads.append(dot(wide_ref[side], weight_ref[base : base + 3 * rows, :]))
            add_sums(
                side, query_ref[side, : 256 + PART, :], weight_ref[base : base + rows, :],
                query_ref[side, :PART, :], weight_ref[base + rows : base + 2 * rows, :],
            )
        qh_re, qh_im, qt_re, qt_im = grads[0][:HALF], grads[0][HALF:], grads[1][:HALF], grads[1][HALF:]
        dh = jnp.concatenate([qt_re * r_re + qt_im * r_im, qt_im * r_re - qt_re * r_im], axis=0)
        dt = jnp.concatenate([qh_re * r_re - qh_im * r_im, qh_re * r_im + qh_im * r_re], axis=0)
        dr = jnp.concatenate(
            [
                qt_re * h_re + qt_im * h_im + qh_re * t_re + qh_im * t_im,
                qt_im * h_re - qt_re * h_im + qh_re * t_im - qh_im * t_re,
            ],
            axis=0,
        )
        high, low = split_parts(dr)
        rel_grad_ref[:PART, at] = high
        rel_grad_ref[PART:, at] = low
        put_query(0, dh)
        add_sums(0, query_ref[0, : 256 + PART, :], head_hot, None, None)
        put_query(1, dt)
        add_sums(1, query_ref[1, : 256 + PART, :], tail_hot, None, None)

    for side, ref in enumerate((head_grad_ref, tail_grad_ref)):
        ref[:half, :] = sums_ref[side, :half, :]
        ref[half:, :] = sums_ref[side, HALF : HALF + half, :]


def edge_gradients(live, heads, tails, negs, head_blk, tail_blk, rels):
    width, rows = head_blk.shape
    edges = heads.shape[1]
    chunk = 512
    vmem = pl.BlockSpec(memory_space=pltpu.VMEM)
    return pl.pallas_call(
        edge_kernel,
        out_shape=(
            jax.ShapeDtypeStruct((width, rows), jnp.float32),
            jax.ShapeDtypeStruct((width, rows), jnp.float32),
            jax.ShapeDtypeStruct((2 * PART, edges), jnp.bfloat16),
        ),
        in_specs=[pl.BlockSpec(memory_space=pltpu.SMEM)] + [vmem] * 6,
        out_specs=(vmem, vmem, vmem),
        scratch_shapes=[
            pltpu.VMEM((2, 2 * PART, rows), jnp.bfloat16),
            pltpu.VMEM((2, rows, 768), jnp.bfloat16),
            pltpu.VMEM((2, PART, 3 * rows), jnp.bfloat16),
            pltpu.VMEM((2, 768, chunk), jnp.bfloat16),
            pltpu.VMEM((6 * rows, chunk), jnp.bfloat16),
            pltpu.VMEM((negs.shape[0], 2, rows, 128), jnp.float32),
            pltpu.VMEM((2, PART, rows), jnp.float32),
        ],
        compiler_params=pltpu.CompilerParams(vmem_limit_bytes=VMEM_LIMIT),
        cost_estimate=pl.CostEstimate(
            flops=40 * PART * rows * edges, bytes_accessed=4 * PART * edges, transcendentals=2 * rows * edges
        ),
        name="edge_gradients",
    )(live, heads, tails, negs, head_blk, tail_blk, rels)


def tile_at(position, place_ref, core):
    outer = (position // 8) ^ place_ref[1 + core]
    inner = (position // 2 % 4) ^ place_ref[2 - core]
    return core * 32 + outer * 8 + inner * 2 + position % 2


def scatter_kernel(other, place_ref, ids_ref, grad_ref, out_ref, spread_ref):
    tiles, width, tile = out_ref.shape
    core = jnp.where(other, 1 - place_ref[0], place_ref[0])
    edges = ids_ref.shape[0]
    half = width // 2
    spread_ref[...] = jnp.broadcast_to(ids_ref[...], spread_ref.shape)

    @pl.loop(0, tiles // 2)
    def _(j):
        start = tile_at(2 * j, place_ref, core) * tile
        lane = lax.broadcasted_iota(jnp.int32, (256, tile), 1)
        cols = None
        for c in range(0, edges, 256):
            ids = spread_ref[c : c + 256, :]
            hot = jnp.concatenate([one_hot(lane + start == ids), one_hot(lane + (start + tile) == ids)], axis=1)
            part = dot(grad_ref[:, c : c + 256], hot)
            cols = part if cols is None else cols + part
        cols = cols[:PART] + cols[PART:]
        for side in range(2):
            part = cols[:, side * tile : (side + 1) * tile]
            out_ref[2 * j + side, :half, :] = part[:half]
            out_ref[2 * j + side, half:, :] = part[HALF : HALF + half]


def scatter_relations(other, place, ids, grads, tiles, width):
    edges = grads.shape[1]
    vmem = pl.BlockSpec(memory_space=pltpu.VMEM)
    return pl.pallas_call(
        functools.partial(scatter_kernel, other),
        out_shape=jax.ShapeDtypeStruct((tiles, width, TILE), jnp.float32),
        in_specs=[pl.BlockSpec(memory_space=pltpu.SMEM), vmem, vmem],
        out_specs=vmem,
        scratch_shapes=[pltpu.VMEM((edges, TILE), jnp.int32)],
        compiler_params=pltpu.CompilerParams(vmem_limit_bytes=VMEM_LIMIT),
        cost_estimate=pl.CostEstimate(
            flops=4 * PART * edges * tiles * TILE, bytes_accessed=tiles * width * TILE * 4, transcendentals=0
        ),
        name="scatter_relations",
    )(place, ids, grads)


def place_kernel(place_ref, *refs):
    chunks, (cols_ref, state_ref, done) = refs[:8], refs[8:]
    width, count = cols_ref.shape
    for core in range(2):
        for chunk in range(4):
            source = chunks[core * 4 + chunk]
            whose = jnp.where(core == 0, place_ref[0], 1 - place_ref[0])

            @pl.loop(0, 8)
            def _(j):
                tile = tile_at(chunk * 8 + j, place_ref, whose)

                @pl.when(tile < count // TILE)
                def _():
                    at = pl.ds(pl.multiple_of(tile * TILE, TILE), TILE)
                    pltpu.make_async_copy(source.at[j, :width, :], cols_ref.at[:, at], done.at[0]).start()
                    pltpu.make_async_copy(source.at[j, width:, :], state_ref.at[:, at], done.at[1]).start()

    pltpu.make_async_copy(cols_ref, cols_ref, done.at[0]).wait()
    pltpu.make_async_copy(state_ref, state_ref, done.at[1]).wait()


def place_columns(place, mine, others, width, count):
    hbm = pl.BlockSpec(memory_space=pl.ANY)
    return pl.pallas_call(
        place_kernel,
        out_shape=(
            jax.ShapeDtypeStruct((width, count), jnp.float32),
            jax.ShapeDtypeStruct((8, count), jnp.float32),
        ),
        in_specs=[pl.BlockSpec(memory_space=pltpu.SMEM)] + [hbm] * 8,
        out_specs=(hbm, hbm),
        scratch_shapes=[pltpu.SemaphoreType.DMA((2,))],
        cost_estimate=pl.CostEstimate(flops=0, bytes_accessed=8 * width * count, transcendentals=0),
        name="place_columns",
    )(place, *mine, *others)


def on_device(
    entities,
    entity_state,
    relations,
    relation_state,
    head_rows,
    relation_ids,
    tail_rows,
    neg_rows,
    edge_counts,
    matching,
):
    me = lax.axis_index("dom")
    core = me & 1
    xor_value = jnp.bitwise_xor(matching[0], me)
    width, count = relations.shape
    edges = head_rows.shape[1]
    mid = edges // 2
    half = -(-count // (64 * TILE)) * 32

    def gather(first):
        ids = relation_ids[:, first : first + mid]
        return lambda live, ids, table: gather_relations(live, ids, table, first), ids

    work, ids = gather(0)
    tail_blk, rels_low = partner_exchange(entities, xor_value, 0, 4, work, edge_counts, ids, relations)
    work, ids = gather(mid)
    tail_blk, rels_high = partner_exchange(tail_blk, xor_value, 4, 4, work, edge_counts, ids, relations)
    rels = jnp.concatenate([rels_low, rels_high], axis=1)
    head_grad, tail_grad, rel_grad = edge_gradients(
        edge_counts, head_rows, tail_rows, neg_rows[0], entities, tail_blk, rels
    )

    column = relation_ids.reshape(edges, 1)
    place = jnp.stack([core, (me >> 6) & 3, (me >> 4) & 3])

    def scatter(place, ids, grads):
        return scatter_relations(True, place, ids, grads, half, width)

    def scatter_and_swap(place, ids, grads, send):
        received = xor_permute(send, 1)
        return scatter_relations(False, place, ids, grads, half, width), received

    tail_grad, send = partner_exchange(tail_grad, xor_value, 0, 4, scatter, place, column, rel_grad)
    tail_grad, (keep, received) = partner_exchange(
        tail_grad, xor_value, 4, 4, scatter_and_swap, place, column, rel_grad, send
    )
    combined = head_grad + tail_grad
    new_entity_state = entity_state + jnp.mean(combined * combined, axis=0)
    new_entities = entities - STEP_RATE * combined / jnp.sqrt(new_entity_state + EPSILON)[None, :]
    new_relations, new_relation_state = update_relations(place, keep, received, relations, relation_state)
    return (new_entities, new_entity_state, new_relations, new_relation_state)


def solution(mesh):
    in_specs = (
        P(None, "dom"),
        P("dom"),
        P(),
        P(),
        P("dom", None),
        P("dom", None),
        P("dom", None),
        P("dom", None, None, None),
        P("dom"),
        P("dom"),
    )
    out_specs = (P(None, "dom"), P("dom"), P(), P())
    return jax.shard_map(
        on_device, mesh=mesh, in_specs=in_specs, out_specs=out_specs, check_vma=False
    )
```

```python
import functools

import jax
import jax.numpy as jnp
from jax import lax
from jax.experimental import pallas as pl
from jax.experimental.pallas import tpu as pltpu
from jax.sharding import PartitionSpec as P

TILE = 128
HALF = 104
PART = 2 * HALF
VMEM_LIMIT = 24 * 2**20
STEP_RATE = 0.3
EPSILON = 1e-08


def pair_permute(value, low_mask, high_mask):
    size = lax.axis_size("dom")
    return lax.ppermute(value, "dom", [(i, i ^ (high_mask if i & 1 else low_mask)) for i in range(size)])


def xor_permute(value, mask):
    return pair_permute(value, mask, mask)


def outer_permute(value, k):
    return pair_permute(value, k << 6, k << 4)


def inner_permute(value, k):
    return pair_permute(value, k << 4, k << 6)


def partner_exchange(value, xor_value, low, width, work, *operands):
    pick = (xor_value >> low) & (2**width - 1)

    def branch(mask, v, *rest):
        moved = xor_permute(v, mask << low) if mask else v
        return moved, work(*rest)

    branches = [functools.partial(branch, mask) for mask in range(2**width)]
    return lax.switch(pick, branches, value, *operands)


def reduce_four(chunks, permute):
    half = chunks[2].shape[0] // 2
    by_one = permute(chunks[2][:half], 1)
    by_three = permute(chunks[2][half:], 3)
    by_one, by_three = lax.optimization_barrier((by_one, by_three))
    for_one = jnp.concatenate([chunks[1][:half], chunks[1][half:] + by_three], axis=0)
    for_three = jnp.concatenate([chunks[3][:half] + by_one, chunks[3][half:]], axis=0)
    return chunks[0] + permute(for_one, 1) + permute(for_three, 3)


def gather_four(own, permute):
    half = own.shape[0] // 2
    one = permute(own, 1)
    three = permute(own, 3)
    one, three = lax.optimization_barrier((one, three))
    low = permute(three[:half], 1)
    high = permute(one[half:], 3)
    return one, (low, high), three


def update_relations(place, keep, received, relations, relation_state):
    half, width, _ = keep.shape
    chunk, owned = half // 4, half // 16
    parts = [keep[k * chunk : (k + 1) * chunk] + received[k * chunk : (k + 1) * chunk] for k in range(4)]
    part = reduce_four(parts, outer_permute)
    part = reduce_four([part[k * owned : (k + 1) * owned] for k in range(4)], inner_permute)
    tile = part[0] + xor_permute(part[1], 2)
    total = tile + xor_permute(tile, 4) + xor_permute(tile, 8) + xor_permute(tile, 12)

    start = tile_at(0, place, place[0]) * TILE
    values = lax.dynamic_slice_in_dim(relations, start, TILE, 1)
    state = lax.dynamic_slice_in_dim(relation_state, start, TILE)
    new_state = state + jnp.mean(total * total, axis=0)
    new_values = values - STEP_RATE * total / jnp.sqrt(new_state + EPSILON)[None, :]
    packed = jnp.concatenate([new_values, jnp.broadcast_to(new_state[None], (8, TILE))], axis=0)
    packed = jnp.stack([packed, xor_permute(packed, 2)])
    one, (low, high), three = gather_four(packed, inner_permute)
    packed = jnp.concatenate([packed, one, low, high, three], axis=0)
    one, (low, high), three = gather_four(packed, outer_permute)
    mine = jnp.concatenate([packed, one, three], axis=0)
    last = jnp.concatenate([low, high], axis=0)
    others = xor_permute(mine, 1)
    others, last = lax.optimization_barrier((others, last))
    other_last = xor_permute(last, 1)
    new_relations, state_row = place_columns(place, mine, last, others, other_last, width, relations.shape[1])
    return new_relations, state_row[0]


def split_parts(x):
    high = x.astype(jnp.bfloat16)
    low = (x - high.astype(jnp.float32)).astype(jnp.bfloat16)
    return high, low


def dot(a, b):
    return jnp.dot(a, b, preferred_element_type=jnp.float32)


def dot_nt(a, b):
    return lax.dot_general(a, b, (((1,), (1,)), ((), ())), preferred_element_type=jnp.float32)


def one_hot(condition):
    return jnp.where(condition, 1.0, 0.0).astype(jnp.bfloat16)


def gather_kernel(first_slot, live_ref, ids_ref, table_ref, out_ref, table, parts, sums, ready):
    width, count = table_ref.shape
    edges = ids_ref.shape[1]
    half = width // 2
    depth = 7
    step = depth * 256
    pieces = count // step

    def piece(i, size=step):
        at = pl.ds(pl.multiple_of(i * step, 256), size)
        return pltpu.make_async_copy(table_ref.at[:, at], table.at[:, at], ready.at[i])

    rest = count - pieces * step
    for i in range(pieces):
        piece(i).start()
    if rest:
        piece(pieces, rest).start()
    sums[...] = jnp.zeros_like(sums)

    def add_tiles(i, tiles):
        @pl.loop(0, tiles)
        def _(k):
            at = pl.ds(pl.multiple_of(i * step + k * 256, 256), 256)
            tile = jnp.concatenate([table[:, at], jnp.zeros((PART - width, 256), jnp.float32)], axis=0)
            there = pl.ds(pl.multiple_of(k * 256, 256), 256)
            high, low = split_parts(tile)
            parts[:PART, there] = high
            parts[PART:, there] = low

        @pl.loop(0, edges // 256)
        def _(c):
            there = pl.ds(pl.multiple_of(c * 256, 256), 256)
            slots = first_slot + c * 256 + lax.broadcasted_iota(jnp.int32, (1, 256), 1)
            ids = jnp.where(slots < live_ref[0], ids_ref[:, there], -1) - i * step
            row = lax.broadcasted_iota(jnp.int32, (256, 256), 0)
            cols = sums[:, there]
            for k in range(tiles):
                cols += dot(parts[:, k * 256 : (k + 1) * 256], one_hot(row + k * 256 == ids))
            sums[:, there] = cols

    @pl.loop(0, pieces)
    def _(i):
        piece(i).wait()
        add_tiles(i, depth)

    if rest:
        piece(pieces, rest).wait()
        add_tiles(pieces, rest // 256)

    @pl.loop(0, edges // 256)
    def _(c):
        there = pl.ds(pl.multiple_of(c * 256, 256), 256)
        cols = sums[:PART, there] + sums[PART:, there]
        out_ref[:HALF, there] = cols[:HALF]
        out_ref[HALF:, there] = cols[half : half + HALF]


def gather_relations(live, ids, relations, first_slot):
    width, count = relations.shape
    edges = ids.shape[1]
    vmem = pl.BlockSpec(memory_space=pltpu.VMEM)
    return pl.pallas_call(
        functools.partial(gather_kernel, first_slot),
        out_shape=jax.ShapeDtypeStruct((PART, edges), jnp.float32),
        in_specs=[pl.BlockSpec(memory_space=pltpu.SMEM), vmem, pl.BlockSpec(memory_space=pl.ANY)],
        out_specs=vmem,
        scratch_shapes=[
            pltpu.VMEM((width, count), jnp.float32),
            pltpu.VMEM((2 * PART, 7 * 256), jnp.bfloat16),
            pltpu.VMEM((2 * PART, edges), jnp.float32),
            pltpu.SemaphoreType.DMA((8,)),
        ],
        compiler_params=pltpu.CompilerParams(vmem_limit_bytes=VMEM_LIMIT),
        cost_estimate=pl.CostEstimate(
            flops=4 * PART * count * edges, bytes_accessed=width * count * 4, transcendentals=0
        ),
        name="gather_relations",
    )(live, ids, relations)


def padded_halves(block):
    half = block.shape[0] // 2
    blank = jnp.zeros((HALF - half, block.shape[1]), block.dtype)
    return jnp.concatenate([block[:half], blank, block[half:], blank], axis=0)


def edge_kernel(
    live_ref, heads_ref, tails_ref, negs_ref, head_ref, tail_ref, rels_ref,
    head_grad_ref, tail_grad_ref, rel_grad_ref,
    cols_ref, flip_ref, wide_ref, query_ref, weight_ref, counts_ref, sums_ref,
):
    width, rows = head_ref.shape
    edges = heads_ref.shape[1]
    chunk = weight_ref.shape[1]
    groups = negs_ref.shape[0]
    half = width // 2

    for side, ref in enumerate((head_ref, tail_ref)):
        block = padded_halves(ref[...])
        high, low = split_parts(block)
        cols_ref[side, :PART, :] = high
        cols_ref[side, PART:, :] = low
        wide_ref[side, :, :rows] = high
        wide_ref[side, :, rows : 2 * rows] = high
        wide_ref[side, :, 2 * rows :] = low
        turned = jnp.concatenate([block, jnp.zeros((256 - PART, rows), jnp.float32)], axis=0).T
        high, low = split_parts(turned)
        flip_ref[side, :, :256] = high
        flip_ref[side, :, 256:512] = high
        flip_ref[side, :, 512:] = low
    for group in range(groups):
        for which in range(2):
            hits = lax.broadcasted_iota(jnp.int32, (rows, negs_ref.shape[-1]), 0) == negs_ref[group, which][None, :]
            count = jnp.sum(jnp.where(hits, 1.0 / negs_ref.shape[-1], 0.0), axis=1, keepdims=True)
            counts_ref[group, which] = jnp.broadcast_to(count, (rows, 128))
    query_ref[...] = jnp.zeros_like(query_ref)
    sums_ref[...] = jnp.zeros_like(sums_ref)

    def put_query(side, query):
        high, low = split_parts(query)
        query_ref[side, :PART, :] = high
        query_ref[side, 256 : 256 + PART, :] = low
        query_ref[side, 512 : 512 + PART, :] = high

    def put_weight(side, weight):
        high, low = split_parts(weight)
        weight_ref[side * 3 * rows : side * 3 * rows + rows, :] = high
        weight_ref[side * 3 * rows + rows : side * 3 * rows + 2 * rows, :] = low
        weight_ref[side * 3 * rows + 2 * rows : side * 3 * rows + 3 * rows, :] = high

    def add_sums(side, left, right, left_again, right_low):
        both = dot_nt(left, right)
        total = both[:PART] + both[256 : 256 + PART]
        if left_again is not None:
            total = total + dot_nt(left_again, right_low)
        sums_ref[side] += total

    @pl.loop(0, edges // chunk)
    def _(c):
        at = pl.ds(pl.multiple_of(c * chunk, chunk), chunk)
        group = c // (edges // groups // chunk)
        slots = c * chunk + lax.broadcasted_iota(jnp.int32, (1, chunk), 1)
        alive = slots < live_ref[0]
        heads = jnp.where(alive, heads_ref[:, at], -1)
        tails = jnp.where(alive, tails_ref[:, at], -1)
        row = lax.broadcasted_iota(jnp.int32, (rows, chunk), 0)
        head_hot = one_hot(row == heads)
        tail_is = row == tails
        tail_hot = one_hot(tail_is)
        h = dot(cols_ref[0], head_hot)
        h = h[:PART] + h[PART:]
        t = dot(cols_ref[1], tail_hot)
        t = t[:PART] + t[PART:]
        r = rels_ref[:, at]
        h_re, h_im, t_re, t_im, r_re, r_im = h[:HALF], h[HALF:], t[:HALF], t[HALF:], r[:HALF], r[HALF:]
        put_query(0, jnp.concatenate([r_re * t_re + r_im * t_im, r_re * t_im - r_im * t_re], axis=0))
        put_query(1, jnp.concatenate([h_re * r_re - h_im * r_im, h_re * r_im + h_im * r_re], axis=0))
        grads = []
        for side in range(2):
            scores = dot(flip_ref[side], query_ref[side])
            chance = 0.5 * jnp.tanh(0.5 * scores) + 0.5
            count = counts_ref[group, 1 - side][:, :1]
            if side == 0:
                weight = chance * count
            else:
                hot = jnp.where(tail_is, 1.0, 0.0)
                weight = chance * (count + hot) - hot
            put_weight(side, weight)
            base = side * 3 * rows
            grads.append(dot(wide_ref[side], weight_ref[base : base + 3 * rows, :]))
            add_sums(
                side, query_ref[side, : 256 + PART, :], weight_ref[base : base + rows, :],
                query_ref[side, :PART, :], weight_ref[base + rows : base + 2 * rows, :],
            )
        qh_re, qh_im, qt_re, qt_im = grads[0][:HALF], grads[0][HALF:], grads[1][:HALF], grads[1][HALF:]
        dh = jnp.concatenate([qt_re * r_re + qt_im * r_im, qt_im * r_re - qt_re * r_im], axis=0)
        dt = jnp.concatenate([qh_re * r_re - qh_im * r_im, qh_re * r_im + qh_im * r_re], axis=0)
        dr = jnp.concatenate(
            [
                qt_re * h_re + qt_im * h_im + qh_re * t_re + qh_im * t_im,
                qt_im * h_re - qt_re * h_im + qh_re * t_im - qh_im * t_re,
            ],
            axis=0,
        )
        high, low = split_parts(dr)
        rel_grad_ref[:PART, at] = high
        rel_grad_ref[PART:, at] = low
        put_query(0, dh)
        add_sums(0, query_ref[0, : 256 + PART, :], head_hot, None, None)
        put_query(1, dt)
        add_sums(1, query_ref[1, : 256 + PART, :], tail_hot, None, None)

    for side, ref in enumerate((head_grad_ref, tail_grad_ref)):
        ref[:half, :] = sums_ref[side, :half, :]
        ref[half:, :] = sums_ref[side, HALF : HALF + half, :]


def edge_gradients(live, heads, tails, negs, head_blk, tail_blk, rels):
    width, rows = head_blk.shape
    edges = heads.shape[1]
    chunk = 512
    vmem = pl.BlockSpec(memory_space=pltpu.VMEM)
    return pl.pallas_call(
        edge_kernel,
        out_shape=(
            jax.ShapeDtypeStruct((width, rows), jnp.float32),
            jax.ShapeDtypeStruct((width, rows), jnp.float32),
            jax.ShapeDtypeStruct((2 * PART, edges), jnp.bfloat16),
        ),
        in_specs=[pl.BlockSpec(memory_space=pltpu.SMEM)] + [vmem] * 6,
        out_specs=(vmem, vmem, vmem),
        scratch_shapes=[
            pltpu.VMEM((2, 2 * PART, rows), jnp.bfloat16),
            pltpu.VMEM((2, rows, 768), jnp.bfloat16),
            pltpu.VMEM((2, PART, 3 * rows), jnp.bfloat16),
            pltpu.VMEM((2, 768, chunk), jnp.bfloat16),
            pltpu.VMEM((6 * rows, chunk), jnp.bfloat16),
            pltpu.VMEM((negs.shape[0], 2, rows, 128), jnp.float32),
            pltpu.VMEM((2, PART, rows), jnp.float32),
        ],
        compiler_params=pltpu.CompilerParams(vmem_limit_bytes=VMEM_LIMIT),
        cost_estimate=pl.CostEstimate(
            flops=40 * PART * rows * edges, bytes_accessed=4 * PART * edges, transcendentals=2 * rows * edges
        ),
        name="edge_gradients",
    )(live, heads, tails, negs, head_blk, tail_blk, rels)


def tile_at(position, place_ref, core):
    outer = (position // 8) ^ place_ref[1 + core]
    inner = (position // 2 % 4) ^ place_ref[2 - core]
    return core * 32 + outer * 8 + inner * 2 + (position % 2 ^ place_ref[3])


def scatter_kernel(other, place_ref, ids_ref, grad_ref, out_ref, spread_ref):
    tiles, width, tile = out_ref.shape
    core = jnp.where(other, 1 - place_ref[0], place_ref[0])
    edges = ids_ref.shape[0]
    half = width // 2
    spread_ref[...] = jnp.broadcast_to(ids_ref[...], spread_ref.shape)

    @pl.loop(0, tiles // 2)
    def _(j):
        first = tile_at(2 * j, place_ref, core) * tile
        second = tile_at(2 * j + 1, place_ref, core) * tile
        lane = lax.broadcasted_iota(jnp.int32, (256, tile), 1)
        cols = None
        for c in range(0, edges, 256):
            ids = spread_ref[c : c + 256, :]
            hot = jnp.concatenate([one_hot(lane + first == ids), one_hot(lane + second == ids)], axis=1)
            part = dot(grad_ref[:, c : c + 256], hot)
            cols = part if cols is None else cols + part
        cols = cols[:PART] + cols[PART:]
        for side in range(2):
            part = cols[:, side * tile : (side + 1) * tile]
            out_ref[2 * j + side, :half, :] = part[:half]
            out_ref[2 * j + side, half:, :] = part[HALF : HALF + half]


def scatter_relations(other, place, ids, grads, tiles, width):
    edges = grads.shape[1]
    vmem = pl.BlockSpec(memory_space=pltpu.VMEM)
    return pl.pallas_call(
        functools.partial(scatter_kernel, other),
        out_shape=jax.ShapeDtypeStruct((tiles, width, TILE), jnp.float32),
        in_specs=[pl.BlockSpec(memory_space=pltpu.SMEM), vmem, vmem],
        out_specs=vmem,
        scratch_shapes=[pltpu.VMEM((edges, TILE), jnp.int32)],
        compiler_params=pltpu.CompilerParams(vmem_limit_bytes=VMEM_LIMIT),
        cost_estimate=pl.CostEstimate(
            flops=4 * PART * edges * tiles * TILE, bytes_accessed=tiles * width * TILE * 4, transcendentals=0
        ),
        name="scatter_relations",
    )(place, ids, grads)


def place_kernel(place_ref, mine_ref, last_ref, others_ref, other_last_ref, cols_ref, state_ref):
    width, count = cols_ref.shape
    sides = ((place_ref[0], mine_ref, last_ref), (1 - place_ref[0], others_ref, other_last_ref))
    for core, most, last in sides:
        for chunk, source, base in ((0, most, 0), (1, most, 8), (3, most, 16), (2, last, 0)):

            @pl.loop(0, 8)
            def _(j):
                tile = tile_at(chunk * 8 + j, place_ref, core)

                @pl.when(tile < count // TILE)
                def _():
                    at = pl.ds(pl.multiple_of(tile * TILE, TILE), TILE)
                    cols_ref[:, at] = source[base + j, :width, :]
                    state_ref[:, at] = source[base + j, width : width + 1, :]


def place_columns(place, mine, last, others, other_last, width, count):
    vmem = pl.BlockSpec(memory_space=pltpu.VMEM)
    return pl.pallas_call(
        place_kernel,
        out_shape=(
            jax.ShapeDtypeStruct((width, count), jnp.float32),
            jax.ShapeDtypeStruct((1, count), jnp.float32),
        ),
        in_specs=[pl.BlockSpec(memory_space=pltpu.SMEM)] + [vmem] * 4,
        out_specs=(vmem, vmem),
        compiler_params=pltpu.CompilerParams(vmem_limit_bytes=VMEM_LIMIT),
        cost_estimate=pl.CostEstimate(flops=0, bytes_accessed=8 * width * count, transcendentals=0),
        name="place_columns",
    )(place, mine, last, others, other_last)


def on_device(
    entities,
    entity_state,
    relations,
    relation_state,
    head_rows,
    relation_ids,
    tail_rows,
    neg_rows,
    edge_counts,
    matching,
):
    me = lax.axis_index("dom")
    core = me & 1
    xor_value = jnp.bitwise_xor(matching[0], me)
    width, count = relations.shape
    edges = head_rows.shape[1]
    mid = edges // 2
    half = -(-count // (64 * TILE)) * 32

    def gather(first):
        ids = relation_ids[:, first : first + mid]
        return lambda live, ids, table: gather_relations(live, ids, table, first), ids

    work, ids = gather(0)
    tail_blk, rels_low = partner_exchange(entities, xor_value, 0, 4, work, edge_counts, ids, relations)
    work, ids = gather(mid)
    tail_blk, rels_high = partner_exchange(tail_blk, xor_value, 4, 4, work, edge_counts, ids, relations)
    rels = jnp.concatenate([rels_low, rels_high], axis=1)
    head_grad, tail_grad, rel_grad = edge_gradients(
        edge_counts, head_rows, tail_rows, neg_rows[0], entities, tail_blk, rels
    )

    column = relation_ids.reshape(edges, 1)
    place = jnp.stack([core, (me >> 6) & 3, (me >> 4) & 3, (me >> 1) & 1])

    def scatter(place, ids, grads):
        return scatter_relations(True, place, ids, grads, half, width)

    def scatter_and_swap(place, ids, grads, send):
        received = xor_permute(send, 1)
        return scatter_relations(False, place, ids, grads, half, width), received

    tail_grad, send = partner_exchange(tail_grad, xor_value, 0, 4, scatter, place, column, rel_grad)
    tail_grad, (keep, received) = partner_exchange(
        tail_grad, xor_value, 4, 4, scatter_and_swap, place, column, rel_grad, send
    )
    combined = head_grad + tail_grad
    new_entity_state = entity_state + jnp.mean(combined * combined, axis=0)
    new_entities = entities - STEP_RATE * combined / jnp.sqrt(new_entity_state + EPSILON)[None, :]
    new_relations, new_relation_state = update_relations(place, keep, received, relations, relation_state)
    return (new_entities, new_entity_state, new_relations, new_relation_state)


def solution(mesh):
    in_specs = (
        P(None, "dom"),
        P("dom"),
        P(),
        P(),
        P("dom", None),
        P("dom", None),
        P("dom", None),
        P("dom", None, None, None),
        P("dom"),
        P("dom"),
    )
    out_specs = (P(None, "dom"), P("dom"), P(), P())
    return jax.shard_map(
        on_device, mesh=mesh, in_specs=in_specs, out_specs=out_specs, check_vma=False
    )
```

```python
import functools

import jax
import jax.numpy as jnp
from jax import lax
from jax.experimental import pallas as pl
from jax.experimental.pallas import tpu as pltpu
from jax.sharding import PartitionSpec as P

TILE = 128
HALF = 104
PART = 2 * HALF
VMEM_LIMIT = 24 * 2**20
STEP_RATE = 0.3
EPSILON = 1e-08


def pair_permute(value, low_mask, high_mask):
    size = lax.axis_size("dom")
    return lax.ppermute(value, "dom", [(i, i ^ (high_mask if i & 1 else low_mask)) for i in range(size)])


def xor_permute(value, mask):
    return pair_permute(value, mask, mask)


def outer_permute(value, k):
    return pair_permute(value, k << 6, k << 4)


def inner_permute(value, k):
    ring, z = k >> 1, k & 1
    return pair_permute(value, ring << 4 | z << 1, ring << 6 | z << 1)


def partner_exchange(value, xor_value):
    for low, width in ((0, 1), (1, 3), (4, 4)):
        pick = (xor_value >> low) & (2**width - 1)
        branches = [lambda v, m=m << low: xor_permute(v, m) if m else v for m in range(2**width)]
        value = lax.switch(pick, branches, value)
    return value


def update_relations(place, keep, received, relations, relation_state, tail_grad, xor_value):
    half, width, _ = keep.shape
    chunk = half // 4
    parts = [keep[k * chunk : (k + 1) * chunk] + received[k * chunk : (k + 1) * chunk] for k in range(4)]
    moved = [outer_permute(parts[k], k) for k in (2, 1, 3)]
    moved, tail_grad = lax.optimization_barrier((moved, partner_exchange(tail_grad, xor_value)))
    part = sum(moved, parts[0])
    moved = [inner_permute(part[k], k) for k in range(1, 8)]
    tile = sum(moved, part[0])
    total = tile + xor_permute(tile, 4) + xor_permute(tile, 8) + xor_permute(tile, 12)

    start = tile_at(0, place, place[0]) * TILE
    values = lax.dynamic_slice_in_dim(relations, start, TILE, 1)
    state = lax.dynamic_slice_in_dim(relation_state, start, TILE)
    new_state = state + jnp.mean(total * total, axis=0)
    new_values = values - STEP_RATE * total / jnp.sqrt(new_state + EPSILON)[None, :]
    packed = jnp.concatenate([new_values, jnp.broadcast_to(new_state[None], (8, TILE))], axis=0)
    packed = jnp.stack([packed] + [inner_permute(packed, k) for k in range(1, 8)])
    moved = {k: outer_permute(packed, k) for k in (2, 1, 3)}
    mine = jnp.concatenate([packed, moved[1], moved[3]], axis=0)
    others = xor_permute(mine, 1)
    others, last = lax.optimization_barrier((others, moved[2]))
    other_last = xor_permute(last, 1)
    new_relations, state_row = place_columns(place, mine, last, others, other_last, width, relations.shape[1])
    return new_relations, state_row[0], tail_grad


def split_parts(x):
    high = x.astype(jnp.bfloat16)
    low = (x - high.astype(jnp.float32)).astype(jnp.bfloat16)
    return high, low


def dot(a, b):
    return jnp.dot(a, b, preferred_element_type=jnp.float32)


def dot_nt(a, b):
    return lax.dot_general(a, b, (((1,), (1,)), ((), ())), preferred_element_type=jnp.float32)


def one_hot(condition):
    return jnp.where(condition, 1.0, 0.0).astype(jnp.bfloat16)


def gather_kernel(shift, first_ref, keys_ref, table_ref, out_ref, parts, sums):
    width, count = table_ref.shape
    block = keys_ref.shape[1]
    edges = keys_ref.size
    half = width // 2
    window = 1024

    @pl.loop(0, count // 256)
    def _(k):
        at = pl.ds(pl.multiple_of(k * 256, 256), 256)
        tile = jnp.concatenate([table_ref[:, at], jnp.zeros((PART - width, 256), jnp.float32)], axis=0)
        high, low = split_parts(tile)
        parts[:PART, at] = high
        parts[PART:, at] = low

    row = lax.broadcasted_iota(jnp.int32, (256, 256), 0)

    @pl.loop(0, edges // 256)
    def _(c):
        there = pl.ds(pl.multiple_of(c * 256, 256), 256)
        group, chunk = c // (block // 256), c % (block // 256)
        ids = keys_ref[pl.ds(group, 1), pl.ds(pl.multiple_of(chunk * 256, 256), 256)] >> shift
        low = first_ref[group, chunk * 256] >> shift
        low = low // 128 * 128
        high = jnp.minimum((first_ref[group, chunk * 256 + 255] >> shift) + 1, count)
        sums[...] = jnp.zeros_like(sums)

        @pl.loop(0, jnp.maximum(high - low + window - 1, 0) // window)
        def _(w):
            wanted = low + w * window
            start = pl.multiple_of(jnp.minimum(wanted, count - window), 128)
            inside = jnp.where(ids < wanted, -1, jnp.where(ids < wanted + window, ids - start, -1))
            cols = None
            for k in range(window // 256):
                part = dot(parts[:, pl.ds(start + k * 256, 256)], one_hot(row + k * 256 == inside))
                cols = part if cols is None else cols + part
            sums[...] += cols

        cols = sums[:PART] + sums[PART:]
        out_ref[:HALF, there] = cols[:HALF]
        out_ref[HALF:, there] = cols[half : half + HALF]


def gather_relations(shift, keys, relations):
    width, count = relations.shape
    edges = keys.size
    vmem = pl.BlockSpec(memory_space=pltpu.VMEM)
    return pl.pallas_call(
        functools.partial(gather_kernel, shift),
        out_shape=jax.ShapeDtypeStruct((PART, edges), jnp.float32),
        in_specs=[pl.BlockSpec(memory_space=pltpu.SMEM), vmem, vmem],
        out_specs=vmem,
        scratch_shapes=[
            pltpu.VMEM((2 * PART, count), jnp.bfloat16),
            pltpu.VMEM((2 * PART, 256), jnp.float32),
        ],
        compiler_params=pltpu.CompilerParams(vmem_limit_bytes=VMEM_LIMIT),
        cost_estimate=pl.CostEstimate(
            flops=PART * count * edges, bytes_accessed=width * count * 4, transcendentals=0
        ),
        name="gather_relations",
    )(keys, keys, relations)


def padded_halves(block):
    half = block.shape[0] // 2
    blank = jnp.zeros((HALF - half, block.shape[1]), block.dtype)
    return jnp.concatenate([block[:half], blank, block[half:], blank], axis=0)


def edge_kernel(
    bits, keys_ref, negs_ref, head_ref, tail_ref, rels_ref,
    head_grad_ref, tail_grad_ref, rel_grad_ref,
    cols_ref, flip_ref, wide_ref, query_ref, weight_ref, counts_ref, sums_ref,
):
    width, rows = head_ref.shape
    edges = keys_ref.size
    chunk = weight_ref.shape[1]
    groups = negs_ref.shape[0]
    half = width // 2

    for side, ref in enumerate((head_ref, tail_ref)):
        block = padded_halves(ref[...])
        high, low = split_parts(block)
        cols_ref[side, :PART, :] = high
        cols_ref[side, PART:, :] = low
        wide_ref[side, :, :rows] = high
        wide_ref[side, :, rows : 2 * rows] = high
        wide_ref[side, :, 2 * rows :] = low
        turned = jnp.concatenate([block, jnp.zeros((256 - PART, rows), jnp.float32)], axis=0).T
        high, low = split_parts(turned)
        flip_ref[side, :, :256] = high
        flip_ref[side, :, 256:512] = high
        flip_ref[side, :, 512:] = low
    for group in range(groups):
        for which in range(2):
            hits = lax.broadcasted_iota(jnp.int32, (rows, negs_ref.shape[-1]), 0) == negs_ref[group, which][None, :]
            count = jnp.sum(jnp.where(hits, 1.0 / negs_ref.shape[-1], 0.0), axis=1, keepdims=True)
            counts_ref[group, which] = jnp.broadcast_to(count, (rows, 128))
    query_ref[...] = jnp.zeros_like(query_ref)
    sums_ref[...] = jnp.zeros_like(sums_ref)

    def put_query(side, query):
        high, low = split_parts(query)
        query_ref[side, :PART, :] = high
        query_ref[side, 256 : 256 + PART, :] = low
        query_ref[side, 512 : 512 + PART, :] = high

    def put_weight(side, weight):
        high, low = split_parts(weight)
        weight_ref[side * 3 * rows : side * 3 * rows + rows, :] = high
        weight_ref[side * 3 * rows + rows : side * 3 * rows + 2 * rows, :] = low
        weight_ref[side * 3 * rows + 2 * rows : side * 3 * rows + 3 * rows, :] = high

    def add_sums(side, left, right, left_again, right_low):
        both = dot_nt(left, right)
        total = both[:PART] + both[256 : 256 + PART]
        if left_again is not None:
            total = total + dot_nt(left_again, right_low)
        sums_ref[side] += total

    @pl.loop(0, edges // chunk)
    def _(c):
        at = pl.ds(pl.multiple_of(c * chunk, chunk), chunk)
        group = c // (edges // groups // chunk)
        inner = edges // groups // chunk
        keys = keys_ref[pl.ds(group, 1), pl.ds(pl.multiple_of(c % inner * chunk, chunk), chunk)]
        heads = keys >> bits & 2**bits - 1
        tails = keys & 2**bits - 1
        row = lax.broadcasted_iota(jnp.int32, (rows, chunk), 0)
        head_hot = one_hot(row == heads)
        tail_is = row == tails
        tail_hot = one_hot(tail_is)
        h = dot(cols_ref[0], head_hot)
        h = h[:PART] + h[PART:]
        t = dot(cols_ref[1], tail_hot)
        t = t[:PART] + t[PART:]
        r = rels_ref[:, at]
        h_re, h_im, t_re, t_im, r_re, r_im = h[:HALF], h[HALF:], t[:HALF], t[HALF:], r[:HALF], r[HALF:]
        put_query(0, jnp.concatenate([r_re * t_re + r_im * t_im, r_re * t_im - r_im * t_re], axis=0))
        put_query(1, jnp.concatenate([h_re * r_re - h_im * r_im, h_re * r_im + h_im * r_re], axis=0))
        grads = []
        for side in range(2):
            scores = dot(flip_ref[side], query_ref[side])
            chance = 0.5 * jnp.tanh(0.5 * scores) + 0.5
            count = counts_ref[group, 1 - side][:, :1]
            if side == 0:
                weight = chance * count
            else:
                hot = jnp.where(tail_is, 1.0, 0.0)
                weight = chance * (count + hot) - hot
            put_weight(side, weight)
            base = side * 3 * rows
            grads.append(dot(wide_ref[side], weight_ref[base : base + 3 * rows, :]))
            add_sums(
                side, query_ref[side, : 256 + PART, :], weight_ref[base : base + rows, :],
                query_ref[side, :PART, :], weight_ref[base + rows : base + 2 * rows, :],
            )
        qh_re, qh_im, qt_re, qt_im = grads[0][:HALF], grads[0][HALF:], grads[1][:HALF], grads[1][HALF:]
        dh = jnp.concatenate([qt_re * r_re + qt_im * r_im, qt_im * r_re - qt_re * r_im], axis=0)
        dt = jnp.concatenate([qh_re * r_re - qh_im * r_im, qh_re * r_im + qh_im * r_re], axis=0)
        dr = jnp.concatenate(
            [
                qt_re * h_re + qt_im * h_im + qh_re * t_re + qh_im * t_im,
                qt_im * h_re - qt_re * h_im + qh_re * t_im - qh_im * t_re,
            ],
            axis=0,
        )
        high, low = split_parts(dr)
        rel_grad_ref[:PART, at] = high
        rel_grad_ref[PART:, at] = low
        put_query(0, dh)
        add_sums(0, query_ref[0, : 256 + PART, :], head_hot, None, None)
        put_query(1, dt)
        add_sums(1, query_ref[1, : 256 + PART, :], tail_hot, None, None)

    for side, ref in enumerate((head_grad_ref, tail_grad_ref)):
        ref[:half, :] = sums_ref[side, :half, :]
        ref[half:, :] = sums_ref[side, HALF : HALF + half, :]


def edge_gradients(bits, keys, negs, head_blk, tail_blk, rels):
    width, rows = head_blk.shape
    edges = keys.size
    chunk = 512
    vmem = pl.BlockSpec(memory_space=pltpu.VMEM)
    return pl.pallas_call(
        functools.partial(edge_kernel, bits),
        out_shape=(
            jax.ShapeDtypeStruct((width, rows), jnp.float32),
            jax.ShapeDtypeStruct((width, rows), jnp.float32),
            jax.ShapeDtypeStruct((2 * PART, edges), jnp.bfloat16),
        ),
        in_specs=[vmem] * 5,
        out_specs=(vmem, vmem, vmem),
        scratch_shapes=[
            pltpu.VMEM((2, 2 * PART, rows), jnp.bfloat16),
            pltpu.VMEM((2, rows, 768), jnp.bfloat16),
            pltpu.VMEM((2, PART, 3 * rows), jnp.bfloat16),
            pltpu.VMEM((2, 768, chunk), jnp.bfloat16),
            pltpu.VMEM((6 * rows, chunk), jnp.bfloat16),
            pltpu.VMEM((negs.shape[0], 2, rows, 128), jnp.float32),
            pltpu.VMEM((2, PART, rows), jnp.float32),
        ],
        compiler_params=pltpu.CompilerParams(vmem_limit_bytes=VMEM_LIMIT),
        cost_estimate=pl.CostEstimate(
            flops=40 * PART * rows * edges, bytes_accessed=4 * PART * edges, transcendentals=2 * rows * edges
        ),
        name="edge_gradients",
    )(keys, negs, head_blk, tail_blk, rels)


def tile_at(position, place_ref, core):
    outer = (position // 8) ^ place_ref[1 + core]
    inner = (position // 2 % 4) ^ place_ref[2 - core]
    return core * 32 + outer * 8 + inner * 2 + (position % 2 ^ place_ref[3])


def scatter_kernel(other, groups, place_ref, starts_ref, ids_ref, grad_ref, out_ref, spread_ref, sums):
    tiles, width, tile = out_ref.shape
    core = jnp.where(other, 1 - place_ref[0], place_ref[0])
    edges = ids_ref.shape[0]
    block = edges // groups
    last = starts_ref.shape[0] // groups - 1
    half = width // 2
    pairs = sums.shape[0]
    spread_ref[...] = jnp.broadcast_to(ids_ref[...], spread_ref.shape)

    @pl.loop(0, tiles // 2 // pairs)
    def _(i):
        lane = lax.broadcasted_iota(jnp.int32, (256, tile), 1)
        row = lax.broadcasted_iota(jnp.int32, (256, tile), 0)
        spans = []
        for u in range(pairs):
            j = i * pairs + u
            first = tile_at(2 * j, place_ref, core)
            base = first // 2 * 2
            total = None
            for group in range(groups):
                low = starts_ref[group * (last + 1) + jnp.minimum(base, last)]
                high = starts_ref[group * (last + 1) + jnp.minimum(base + 2, last)]
                low = low // 128 * 128
                spans.append((u, group, base, low, high))
                at = pl.ds(pl.multiple_of(group * block + jnp.minimum(low, block - 256), 128), 256)
                ids = spread_ref[at, :] - base * tile
                hot = jnp.concatenate([one_hot(lane == ids), one_hot(lane + tile == ids)], axis=1)
                part = dot(grad_ref[:, at], hot)
                total = part if total is None else total + part
            sums[u] = total
        for u, group, base, low, high in spans:

            @pl.loop(1, jnp.maximum(high - low + 255, 256) // 256)
            def _(w):
                wanted = low + w * 256
                start = jnp.minimum(wanted, block - 256)
                at = pl.ds(pl.multiple_of(group * block + start, 128), 256)
                ids = jnp.where(row + start < wanted, -1, spread_ref[at, :] - base * tile)
                hot = jnp.concatenate([one_hot(lane == ids), one_hot(lane + tile == ids)], axis=1)
                sums[u] += dot(grad_ref[:, at], hot)

        for u in range(pairs):
            cols = sums[u, :PART] + sums[u, PART:]
            for side in range(2):
                part = cols[:, side * tile : (side + 1) * tile]
                to = 2 * (i * pairs + u) + (side ^ place_ref[3])
                out_ref[to, :half, :] = part[:half]
                out_ref[to, half:, :] = part[HALF : HALF + half]


def scatter_relations(other, place, starts, ids, grads, tiles, width):
    edges = grads.shape[1]
    vmem = pl.BlockSpec(memory_space=pltpu.VMEM)
    smem = pl.BlockSpec(memory_space=pltpu.SMEM)
    return pl.pallas_call(
        functools.partial(scatter_kernel, other, starts.shape[0]),
        out_shape=jax.ShapeDtypeStruct((tiles, width, TILE), jnp.float32),
        in_specs=[smem, smem, vmem, vmem],
        out_specs=vmem,
        scratch_shapes=[pltpu.VMEM((edges, TILE), jnp.int32), pltpu.VMEM((2, 2 * PART, 2 * TILE), jnp.float32)],
        compiler_params=pltpu.CompilerParams(vmem_limit_bytes=VMEM_LIMIT),
        cost_estimate=pl.CostEstimate(
            flops=PART * edges * tiles * TILE, bytes_accessed=tiles * width * TILE * 4, transcendentals=0
        ),
        name="scatter_relations",
    )(place, starts.reshape(starts.size), ids, grads)


def place_kernel(place_ref, mine_ref, last_ref, others_ref, other_last_ref, cols_ref, state_ref):
    width, count = cols_ref.shape
    sides = ((place_ref[0], mine_ref, last_ref), (1 - place_ref[0], others_ref, other_last_ref))
    for core, most, last in sides:
        for chunk, source, base in ((0, most, 0), (1, most, 8), (3, most, 16), (2, last, 0)):

            @pl.loop(0, 8)
            def _(j):
                tile = tile_at(chunk * 8 + j, place_ref, core)

                @pl.when(tile < count // TILE)
                def _():
                    at = pl.ds(pl.multiple_of(tile * TILE, TILE), TILE)
                    cols_ref[:, at] = source[base + j, :width, :]
                    state_ref[:, at] = source[base + j, width : width + 1, :]


def place_columns(place, mine, last, others, other_last, width, count):
    vmem = pl.BlockSpec(memory_space=pltpu.VMEM)
    return pl.pallas_call(
        place_kernel,
        out_shape=(
            jax.ShapeDtypeStruct((width, count), jnp.float32),
            jax.ShapeDtypeStruct((1, count), jnp.float32),
        ),
        in_specs=[pl.BlockSpec(memory_space=pltpu.SMEM)] + [vmem] * 4,
        out_specs=(vmem, vmem),
        compiler_params=pltpu.CompilerParams(vmem_limit_bytes=VMEM_LIMIT),
        cost_estimate=pl.CostEstimate(flops=0, bytes_accessed=8 * width * count, transcendentals=0),
        name="place_columns",
    )(place, mine, last, others, other_last)


def on_device(
    entities,
    entity_state,
    relations,
    relation_state,
    head_rows,
    relation_ids,
    tail_rows,
    neg_rows,
    edge_counts,
    matching,
):
    me = lax.axis_index("dom")
    core = me & 1
    xor_value = jnp.bitwise_xor(matching[0], me)
    width, count = relations.shape
    edges = head_rows.shape[1]
    half = -(-count // (64 * TILE)) * 32

    groups = neg_rows.shape[1]
    bits = (entities.shape[1] - 1).bit_length()
    shift = 2 * bits
    assert (count - 1).bit_length() + shift <= 31 and count < 2 ** (31 - shift) and entities.shape[1] < 2**bits

    keys = relation_ids << shift | head_rows << bits | tail_rows
    slots = lax.broadcasted_iota(jnp.int32, keys.shape, 1)
    keys = jnp.where(slots < edge_counts[0], keys, 2**31 - 1)
    keys = lax.sort(keys.reshape(groups, edges // groups), dimension=1)
    ids = keys >> shift
    firsts = jnp.arange(count // TILE + 1, dtype=jnp.int32) * TILE
    starts = jnp.sum((ids[:, None, :] < firsts[None, :, None]).astype(jnp.int32), axis=2)

    tail_blk = partner_exchange(entities, xor_value)
    rels = gather_relations(shift, keys, relations)
    head_grad, tail_grad, rel_grad = edge_gradients(
        bits, keys, neg_rows[0], entities, tail_blk, rels
    )

    column = ids.reshape(edges, 1)
    place = jnp.stack([core, (me >> 6) & 3, (me >> 4) & 3, (me >> 1) & 1])
    send = scatter_relations(True, place, starts, column, rel_grad, half, width)
    received = xor_permute(send, 1)
    keep = scatter_relations(False, place, starts, column, rel_grad, half, width)
    new_relations, new_relation_state, tail_grad = update_relations(
        place, keep, received, relations, relation_state, tail_grad, xor_value
    )
    combined = head_grad + tail_grad
    new_entity_state = entity_state + jnp.mean(combined * combined, axis=0)
    new_entities = entities - STEP_RATE * combined / jnp.sqrt(new_entity_state + EPSILON)[None, :]
    return (new_entities, new_entity_state, new_relations, new_relation_state)


def solution(mesh):
    in_specs = (
        P(None, "dom"),
        P("dom"),
        P(),
        P(),
        P("dom", None),
        P("dom", None),
        P("dom", None),
        P("dom", None, None, None),
        P("dom"),
        P("dom"),
    )
    out_specs = (P(None, "dom"), P("dom"), P(), P())
    return jax.shard_map(
        on_device, mesh=mesh, in_specs=in_specs, out_specs=out_specs, check_vma=False
    )
```

```python
import functools

import jax
import jax.numpy as jnp
from jax import lax
from jax.experimental import pallas as pl
from jax.experimental.pallas import tpu as pltpu
from jax.sharding import PartitionSpec as P

TILE = 128
HALF = 104
PART = 2 * HALF
VMEM_LIMIT = 24 * 2**20
STEP_RATE = 0.3
EPSILON = 1e-08


def pair_permute(value, low_mask, high_mask):
    size = lax.axis_size("dom")
    return lax.ppermute(value, "dom", [(i, i ^ (high_mask if i & 1 else low_mask)) for i in range(size)])


def xor_permute(value, mask):
    return pair_permute(value, mask, mask)


def outer_permute(value, k):
    return pair_permute(value, k << 6, k << 4)


def inner_permute(value, k):
    ring, z = k >> 1, k & 1
    return pair_permute(value, ring << 4 | z << 1, ring << 6 | z << 1)


def partner_exchange(value, xor_value, work=None, operands=()):
    extra = None
    for low, width in ((0, 1), (1, 3), (4, 4)):
        pick = (xor_value >> low) & (2**width - 1)
        rest = operands if low == 1 else ()

        def branch(mask, v, *rest):
            moved = xor_permute(v, mask) if mask else v
            return moved, work(*rest) if rest else ()

        branches = [functools.partial(branch, m << low) for m in range(2**width)]
        value, done = lax.switch(pick, branches, value, *rest)
        extra = done if rest else extra
    return value, extra


def gather_four(own, permute):
    half = own.shape[0] // 2
    one, three = lax.optimization_barrier((permute(own, 1), permute(own, 3)))
    return one, three, permute(three[:half], 1), permute(one[half:], 3)


def update_relations(place, keep, received, relations, relation_state, tail_grad, xor_value):
    half, width, _ = keep.shape
    chunk = half // 4
    parts = [keep[k * chunk : (k + 1) * chunk] + received[k * chunk : (k + 1) * chunk] for k in range(4)]
    moved = [outer_permute(parts[k], k) for k in (2, 1, 3)]
    moved, tail_grad = lax.optimization_barrier((moved, partner_exchange(tail_grad, xor_value)[0]))
    part = sum(moved, parts[0])
    moved = [inner_permute(part[k], k) for k in range(1, 8)]
    tile = sum(moved, part[0])
    total = tile + xor_permute(tile, 4) + xor_permute(tile, 8) + xor_permute(tile, 12)

    start = tile_at(0, place, place[0]) * TILE
    values = lax.dynamic_slice_in_dim(relations, start, TILE, 1)
    state = lax.dynamic_slice_in_dim(relation_state, start, TILE)
    new_state = state + jnp.mean(total * total, axis=0)
    new_values = values - STEP_RATE * total / jnp.sqrt(new_state + EPSILON)[None, :]
    packed = jnp.concatenate([new_values, jnp.broadcast_to(new_state[None], (8, TILE))], axis=0)
    packed = jnp.stack([packed, xor_permute(packed, 2)])
    packed = jnp.concatenate([packed] + [inner_permute(packed, k) for k in (2, 4, 6)], axis=0)
    one, three, low, high = gather_four(packed, outer_permute)
    mine = jnp.concatenate([packed, one, three], axis=0)
    others = xor_permute(mine, 1)
    others, low, high = lax.optimization_barrier((others, low, high))
    last = jnp.concatenate([low, high], axis=0)
    other_last = xor_permute(last, 1)
    new_relations, state_row = place_columns(place, mine, last, others, other_last, width, relations.shape[1])
    return new_relations, state_row[0], tail_grad


def split_parts(x):
    high = x.astype(jnp.bfloat16)
    low = (x - high.astype(jnp.float32)).astype(jnp.bfloat16)
    return high, low


def dot(a, b):
    return jnp.dot(a, b, preferred_element_type=jnp.float32)


def dot_nt(a, b):
    return lax.dot_general(a, b, (((1,), (1,)), ((), ())), preferred_element_type=jnp.float32)


def one_hot(condition):
    return jnp.where(condition, 1.0, 0.0).astype(jnp.bfloat16)


def gather_kernel(shift, first_ref, keys_ref, table_ref, out_ref, parts, sums):
    width, count = table_ref.shape
    block = keys_ref.shape[1]
    edges = keys_ref.size
    half = width // 2
    window = 1024

    @pl.loop(0, count // 256)
    def _(k):
        at = pl.ds(pl.multiple_of(k * 256, 256), 256)
        tile = jnp.concatenate([table_ref[:, at], jnp.zeros((PART - width, 256), jnp.float32)], axis=0)
        high, low = split_parts(tile)
        parts[:PART, at] = high
        parts[PART:, at] = low

    row = lax.broadcasted_iota(jnp.int32, (256, 256), 0)

    @pl.loop(0, edges // 256)
    def _(c):
        there = pl.ds(pl.multiple_of(c * 256, 256), 256)
        group, chunk = c // (block // 256), c % (block // 256)
        ids = keys_ref[pl.ds(group, 1), pl.ds(pl.multiple_of(chunk * 256, 256), 256)] >> shift
        low = first_ref[group, chunk * 256] >> shift
        low = low // 128 * 128
        high = jnp.minimum((first_ref[group, chunk * 256 + 255] >> shift) + 1, count)
        sums[...] = jnp.zeros_like(sums)

        @pl.loop(0, jnp.maximum(high - low + window - 1, 0) // window)
        def _(w):
            wanted = low + w * window
            start = pl.multiple_of(jnp.minimum(wanted, count - window), 128)
            inside = jnp.where(ids < wanted, -1, jnp.where(ids < wanted + window, ids - start, -1))
            cols = None
            for k in range(window // 256):
                part = dot(parts[:, pl.ds(start + k * 256, 256)], one_hot(row + k * 256 == inside))
                cols = part if cols is None else cols + part
            sums[...] += cols

        cols = sums[:PART] + sums[PART:]
        out_ref[:HALF, there] = cols[:HALF]
        out_ref[HALF:, there] = cols[half : half + HALF]


def gather_relations(shift, keys, relations):
    width, count = relations.shape
    edges = keys.size
    vmem = pl.BlockSpec(memory_space=pltpu.VMEM)
    return pl.pallas_call(
        functools.partial(gather_kernel, shift),
        out_shape=jax.ShapeDtypeStruct((PART, edges), jnp.float32),
        in_specs=[pl.BlockSpec(memory_space=pltpu.SMEM), vmem, vmem],
        out_specs=vmem,
        scratch_shapes=[
            pltpu.VMEM((2 * PART, count), jnp.bfloat16),
            pltpu.VMEM((2 * PART, 256), jnp.float32),
        ],
        compiler_params=pltpu.CompilerParams(vmem_limit_bytes=VMEM_LIMIT),
        cost_estimate=pl.CostEstimate(
            flops=PART * count * edges, bytes_accessed=width * count * 4, transcendentals=0
        ),
        name="gather_relations",
    )(keys, keys, relations)


def padded_halves(block):
    half = block.shape[0] // 2
    blank = jnp.zeros((HALF - half, block.shape[1]), block.dtype)
    return jnp.concatenate([block[:half], blank, block[half:], blank], axis=0)


def edge_kernel(
    bits, keys_ref, negs_ref, head_ref, tail_ref, rels_ref,
    head_grad_ref, tail_grad_ref, rel_grad_ref,
    cols_ref, flip_ref, wide_ref, query_ref, weight_ref, counts_ref, sums_ref,
):
    width, rows = head_ref.shape
    edges = keys_ref.size
    chunk = weight_ref.shape[1]
    groups = negs_ref.shape[0]
    half = width // 2

    for side, ref in enumerate((head_ref, tail_ref)):
        block = padded_halves(ref[...])
        high, low = split_parts(block)
        cols_ref[side, :PART, :] = high
        cols_ref[side, PART:, :] = low
        wide_ref[side, :, :rows] = high
        wide_ref[side, :, rows : 2 * rows] = high
        wide_ref[side, :, 2 * rows :] = low
        turned = jnp.concatenate([block, jnp.zeros((256 - PART, rows), jnp.float32)], axis=0).T
        high, low = split_parts(turned)
        flip_ref[side, :, :256] = high
        flip_ref[side, :, 256:512] = high
        flip_ref[side, :, 512:] = low
    for group in range(groups):
        for which in range(2):
            hits = lax.broadcasted_iota(jnp.int32, (rows, negs_ref.shape[-1]), 0) == negs_ref[group, which][None, :]
            count = jnp.sum(jnp.where(hits, 1.0 / negs_ref.shape[-1], 0.0), axis=1, keepdims=True)
            counts_ref[group, which] = jnp.broadcast_to(count, (rows, 128))
    query_ref[...] = jnp.zeros_like(query_ref)
    sums_ref[...] = jnp.zeros_like(sums_ref)

    def put_query(side, query):
        high, low = split_parts(query)
        query_ref[side, :PART, :] = high
        query_ref[side, 256 : 256 + PART, :] = low
        query_ref[side, 512 : 512 + PART, :] = high

    def put_weight(side, weight):
        high, low = split_parts(weight)
        weight_ref[side * 3 * rows : side * 3 * rows + rows, :] = high
        weight_ref[side * 3 * rows + rows : side * 3 * rows + 2 * rows, :] = low
        weight_ref[side * 3 * rows + 2 * rows : side * 3 * rows + 3 * rows, :] = high

    def add_sums(side, left, right, left_again, right_low):
        both = dot_nt(left, right)
        total = both[:PART] + both[256 : 256 + PART]
        if left_again is not None:
            total = total + dot_nt(left_again, right_low)
        sums_ref[side] += total

    @pl.loop(0, edges // chunk)
    def _(c):
        at = pl.ds(pl.multiple_of(c * chunk, chunk), chunk)
        group = c // (edges // groups // chunk)
        inner = edges // groups // chunk
        keys = keys_ref[pl.ds(group, 1), pl.ds(pl.multiple_of(c % inner * chunk, chunk), chunk)]
        heads = keys >> bits & 2**bits - 1
        tails = keys & 2**bits - 1
        row = lax.broadcasted_iota(jnp.int32, (rows, chunk), 0)
        head_hot = one_hot(row == heads)
        tail_is = row == tails
        tail_hot = one_hot(tail_is)
        h = dot(cols_ref[0], head_hot)
        h = h[:PART] + h[PART:]
        t = dot(cols_ref[1], tail_hot)
        t = t[:PART] + t[PART:]
        r = rels_ref[:, at]
        h_re, h_im, t_re, t_im, r_re, r_im = h[:HALF], h[HALF:], t[:HALF], t[HALF:], r[:HALF], r[HALF:]
        put_query(0, jnp.concatenate([r_re * t_re + r_im * t_im, r_re * t_im - r_im * t_re], axis=0))
        put_query(1, jnp.concatenate([h_re * r_re - h_im * r_im, h_re * r_im + h_im * r_re], axis=0))
        grads = []
        for side in range(2):
            scores = dot(flip_ref[side], query_ref[side])
            chance = 0.5 * jnp.tanh(0.5 * scores) + 0.5
            count = counts_ref[group, 1 - side][:, :1]
            if side == 0:
                weight = chance * count
            else:
                hot = jnp.where(tail_is, 1.0, 0.0)
                weight = chance * (count + hot) - hot
            put_weight(side, weight)
            base = side * 3 * rows
            grads.append(dot(wide_ref[side], weight_ref[base : base + 3 * rows, :]))
            add_sums(
                side, query_ref[side, : 256 + PART, :], weight_ref[base : base + rows, :],
                query_ref[side, :PART, :], weight_ref[base + rows : base + 2 * rows, :],
            )
        qh_re, qh_im, qt_re, qt_im = grads[0][:HALF], grads[0][HALF:], grads[1][:HALF], grads[1][HALF:]
        dh = jnp.concatenate([qt_re * r_re + qt_im * r_im, qt_im * r_re - qt_re * r_im], axis=0)
        dt = jnp.concatenate([qh_re * r_re - qh_im * r_im, qh_re * r_im + qh_im * r_re], axis=0)
        dr = jnp.concatenate(
            [
                qt_re * h_re + qt_im * h_im + qh_re * t_re + qh_im * t_im,
                qt_im * h_re - qt_re * h_im + qh_re * t_im - qh_im * t_re,
            ],
            axis=0,
        )
        high, low = split_parts(dr)
        rel_grad_ref[:PART, at] = high
        rel_grad_ref[PART:, at] = low
        put_query(0, dh)
        add_sums(0, query_ref[0, : 256 + PART, :], head_hot, None, None)
        put_query(1, dt)
        add_sums(1, query_ref[1, : 256 + PART, :], tail_hot, None, None)

    for side, ref in enumerate((head_grad_ref, tail_grad_ref)):
        ref[:half, :] = sums_ref[side, :half, :]
        ref[half:, :] = sums_ref[side, HALF : HALF + half, :]


def edge_gradients(bits, keys, negs, head_blk, tail_blk, rels):
    width, rows = head_blk.shape
    edges = keys.size
    chunk = 512
    vmem = pl.BlockSpec(memory_space=pltpu.VMEM)
    return pl.pallas_call(
        functools.partial(edge_kernel, bits),
        out_shape=(
            jax.ShapeDtypeStruct((width, rows), jnp.float32),
            jax.ShapeDtypeStruct((width, rows), jnp.float32),
            jax.ShapeDtypeStruct((2 * PART, edges), jnp.bfloat16),
        ),
        in_specs=[vmem] * 5,
        out_specs=(vmem, vmem, vmem),
        scratch_shapes=[
            pltpu.VMEM((2, 2 * PART, rows), jnp.bfloat16),
            pltpu.VMEM((2, rows, 768), jnp.bfloat16),
            pltpu.VMEM((2, PART, 3 * rows), jnp.bfloat16),
            pltpu.VMEM((2, 768, chunk), jnp.bfloat16),
            pltpu.VMEM((6 * rows, chunk), jnp.bfloat16),
            pltpu.VMEM((negs.shape[0], 2, rows, 128), jnp.float32),
            pltpu.VMEM((2, PART, rows), jnp.float32),
        ],
        compiler_params=pltpu.CompilerParams(vmem_limit_bytes=VMEM_LIMIT),
        cost_estimate=pl.CostEstimate(
            flops=40 * PART * rows * edges, bytes_accessed=4 * PART * edges, transcendentals=2 * rows * edges
        ),
        name="edge_gradients",
    )(keys, negs, head_blk, tail_blk, rels)


def tile_at(position, place_ref, core):
    outer = (position // 8) ^ place_ref[1 + core]
    inner = (position // 2 % 4) ^ place_ref[2 - core]
    return core * 32 + outer * 8 + inner * 2 + (position % 2 ^ place_ref[3])


def scatter_kernel(other, groups, place_ref, starts_ref, ids_ref, grad_ref, out_ref, spread_ref, sums):
    tiles, width, tile = out_ref.shape
    core = jnp.where(other, 1 - place_ref[0], place_ref[0])
    edges = ids_ref.shape[0]
    block = edges // groups
    last = starts_ref.shape[0] // groups - 1
    half = width // 2
    pairs = sums.shape[0]
    spread_ref[...] = jnp.broadcast_to(ids_ref[...], spread_ref.shape)

    @pl.loop(0, tiles // 2 // pairs)
    def _(i):
        lane = lax.broadcasted_iota(jnp.int32, (256, tile), 1)
        row = lax.broadcasted_iota(jnp.int32, (256, tile), 0)
        spans = []
        for u in range(pairs):
            j = i * pairs + u
            first = tile_at(2 * j, place_ref, core)
            base = first // 2 * 2
            total = None
            for group in range(groups):
                low = starts_ref[group * (last + 1) + jnp.minimum(base, last)]
                high = starts_ref[group * (last + 1) + jnp.minimum(base + 2, last)]
                low = low // 128 * 128
                spans.append((u, group, base, low, high))
                at = pl.ds(pl.multiple_of(group * block + jnp.minimum(low, block - 256), 128), 256)
                ids = spread_ref[at, :] - base * tile
                hot = jnp.concatenate([one_hot(lane == ids), one_hot(lane + tile == ids)], axis=1)
                part = dot(grad_ref[:, at], hot)
                total = part if total is None else total + part
            sums[u] = total
        for u, group, base, low, high in spans:

            @pl.loop(1, jnp.maximum(high - low + 255, 256) // 256)
            def _(w):
                wanted = low + w * 256
                start = jnp.minimum(wanted, block - 256)
                at = pl.ds(pl.multiple_of(group * block + start, 128), 256)
                ids = jnp.where(row + start < wanted, -1, spread_ref[at, :] - base * tile)
                hot = jnp.concatenate([one_hot(lane == ids), one_hot(lane + tile == ids)], axis=1)
                sums[u] += dot(grad_ref[:, at], hot)

        for u in range(pairs):
            cols = sums[u, :PART] + sums[u, PART:]
            for side in range(2):
                part = cols[:, side * tile : (side + 1) * tile]
                to = 2 * (i * pairs + u) + (side ^ place_ref[3])
                out_ref[to, :half, :] = part[:half]
                out_ref[to, half:, :] = part[HALF : HALF + half]


def scatter_relations(other, place, starts, ids, grads, tiles, width):
    edges = grads.shape[1]
    vmem = pl.BlockSpec(memory_space=pltpu.VMEM)
    smem = pl.BlockSpec(memory_space=pltpu.SMEM)
    return pl.pallas_call(
        functools.partial(scatter_kernel, other, starts.shape[0]),
        out_shape=jax.ShapeDtypeStruct((tiles, width, TILE), jnp.float32),
        in_specs=[smem, smem, vmem, vmem],
        out_specs=vmem,
        scratch_shapes=[pltpu.VMEM((edges, TILE), jnp.int32), pltpu.VMEM((2, 2 * PART, 2 * TILE), jnp.float32)],
        compiler_params=pltpu.CompilerParams(vmem_limit_bytes=VMEM_LIMIT),
        cost_estimate=pl.CostEstimate(
            flops=PART * edges * tiles * TILE, bytes_accessed=tiles * width * TILE * 4, transcendentals=0
        ),
        name="scatter_relations",
    )(place, starts.reshape(starts.size), ids, grads)


def place_kernel(place_ref, mine_ref, last_ref, others_ref, other_last_ref, out_ref, state_ref, low_ref, high_ref, sent):
    width, count = out_ref.shape
    sources = ((mine_ref, last_ref), (others_ref, other_last_ref))
    copies = []
    for half, cols_ref in enumerate((low_ref, high_ref)):
        first = half * 32 * TILE
        for own in range(2):
            most, last = sources[(own + half) % 2]

            @pl.when(place_ref[0] == own)
            def _():
                for chunk, source, base in ((0, most, 0), (1, most, 8), (3, most, 16), (2, last, 0)):

                    @pl.loop(0, 8)
                    def _(j):
                        tile = tile_at(chunk * 8 + j, place_ref, half)

                        @pl.when(tile < count // TILE)
                        def _():
                            at = pl.multiple_of(tile * TILE, TILE)
                            here = pl.multiple_of(at - first, TILE)
                            cols_ref[:, pl.ds(here, TILE)] = source[base + j, :width, :]
                            state_ref[:, pl.ds(at, TILE)] = source[base + j, width : width + 1, :]

        there = out_ref.at[:, pl.ds(first, cols_ref.shape[1])]
        copies.append(pltpu.make_async_copy(cols_ref, there, sent.at[half]))
        copies[-1].start()
    for copy in copies:
        copy.wait()


def place_columns(place, mine, last, others, other_last, width, count):
    vmem = pl.BlockSpec(memory_space=pltpu.VMEM)
    return pl.pallas_call(
        place_kernel,
        out_shape=(
            jax.ShapeDtypeStruct((width, count), jnp.float32),
            jax.ShapeDtypeStruct((1, count), jnp.float32),
        ),
        in_specs=[pl.BlockSpec(memory_space=pltpu.SMEM)] + [vmem] * 4,
        out_specs=(pl.BlockSpec(memory_space=pl.ANY), vmem),
        scratch_shapes=[
            pltpu.VMEM((width, 32 * TILE), jnp.float32),
            pltpu.VMEM((width, count - 32 * TILE), jnp.float32),
            pltpu.SemaphoreType.DMA((2,)),
        ],
        compiler_params=pltpu.CompilerParams(vmem_limit_bytes=VMEM_LIMIT),
        cost_estimate=pl.CostEstimate(flops=0, bytes_accessed=8 * width * count, transcendentals=0),
        name="place_columns",
    )(place, mine, last, others, other_last)


def on_device(
    entities,
    entity_state,
    relations,
    relation_state,
    head_rows,
    relation_ids,
    tail_rows,
    neg_rows,
    edge_counts,
    matching,
):
    me = lax.axis_index("dom")
    core = me & 1
    xor_value = jnp.bitwise_xor(matching[0], me)
    width, count = relations.shape
    edges = head_rows.shape[1]
    half = -(-count // (64 * TILE)) * 32

    groups = neg_rows.shape[1]
    bits = (entities.shape[1] - 1).bit_length()
    shift = 2 * bits
    assert groups <= 2 and (count - 1).bit_length() + shift <= 31 and count < 2 ** (31 - shift) and entities.shape[1] < 2**bits

    keys = (relation_ids << shift | head_rows << bits | tail_rows)[0]
    slots = lax.broadcasted_iota(jnp.int32, keys.shape, 0)
    keys = jnp.where(slots < edge_counts[0], keys, 2**31 - 1).astype(jnp.uint32)
    keys = lax.sort(keys | (slots // (edges // groups)).astype(jnp.uint32) << 31)
    keys = (keys & jnp.uint32(2**31 - 1)).astype(jnp.int32).reshape(groups, edges // groups)
    ids = keys >> shift
    firsts = jnp.arange(count // TILE + 1, dtype=jnp.int32) * TILE
    starts = jnp.sum((ids[:, None, :] < firsts[None, :, None]).astype(jnp.int32), axis=2)

    tail_blk, rels = partner_exchange(
        entities, xor_value, functools.partial(gather_relations, shift), (keys, relations)
    )
    head_grad, tail_grad, rel_grad = edge_gradients(
        bits, keys, neg_rows[0], entities, tail_blk, rels
    )

    column = ids.reshape(edges, 1)
    place = jnp.stack([core, (me >> 6) & 3, (me >> 4) & 3, (me >> 1) & 1])
    send = scatter_relations(True, place, starts, column, rel_grad, half, width)
    received = xor_permute(send, 1)
    keep = scatter_relations(False, place, starts, column, rel_grad, half, width)
    new_relations, new_relation_state, tail_grad = update_relations(
        place, keep, received, relations, relation_state, tail_grad, xor_value
    )
    combined = head_grad + tail_grad
    new_entity_state = entity_state + jnp.mean(combined * combined, axis=0)
    new_entities = entities - STEP_RATE * combined / jnp.sqrt(new_entity_state + EPSILON)[None, :]
    return (new_entities, new_entity_state, new_relations, new_relation_state)


def solution(mesh):
    in_specs = (
        P(None, "dom"),
        P("dom"),
        P(),
        P(),
        P("dom", None),
        P("dom", None),
        P("dom", None),
        P("dom", None, None, None),
        P("dom"),
        P("dom"),
    )
    out_specs = (P(None, "dom"), P("dom"), P(), P())
    return jax.shard_map(
        on_device, mesh=mesh, in_specs=in_specs, out_specs=out_specs, check_vma=False
    )
```

```python
import functools

import jax
import jax.numpy as jnp
from jax import lax
from jax.experimental import pallas as pl
from jax.experimental.pallas import tpu as pltpu
from jax.sharding import PartitionSpec as P

TILE = 128
HALF = 104
PART = 2 * HALF
VMEM_LIMIT = 24 * 2**20
STEP_RATE = 0.3
EPSILON = 1e-08


def pair_permute(value, low_mask, high_mask):
    size = lax.axis_size("dom")
    return lax.ppermute(value, "dom", [(i, i ^ (high_mask if i & 1 else low_mask)) for i in range(size)])


def xor_permute(value, mask):
    return pair_permute(value, mask, mask)


def outer_permute(value, k):
    return pair_permute(value, k << 6, k << 4)


def inner_permute(value, k):
    ring, z = k >> 1, k & 1
    return pair_permute(value, ring << 4 | z << 1, ring << 6 | z << 1)


def partner_hop(value, xor_value, low, width, work=None, *operands):
    pick = (xor_value >> low) & (2**width - 1)

    def branch(mask, v, *rest):
        moved = xor_permute(v, mask) if mask else v
        return (moved, work(*rest)) if work else moved

    return lax.switch(pick, [functools.partial(branch, m << low) for m in range(2**width)], value, *operands)


def gather_four(own, permute):
    half = own.shape[0] // 2
    one, three = lax.optimization_barrier((permute(own, 1), permute(own, 3)))
    return one, three, permute(three[:half], 1), permute(one[half:], 3)


def update_relations(place, keep, received, relations, relation_state, tail_grad, xor_value):
    half, width, _ = keep.shape
    chunk = half // 4
    parts = [keep[k * chunk : (k + 1) * chunk] + received[k * chunk : (k + 1) * chunk] for k in range(4)]
    moved = [outer_permute(parts[k], k) for k in (2, 1, 3)]
    tail_grad = partner_hop(partner_hop(tail_grad, xor_value, 0, 1), xor_value, 1, 3)
    moved, tail_grad = lax.optimization_barrier((moved, tail_grad))
    part = sum(moved, parts[0])
    moved = [inner_permute(part[k], k) for k in range(1, 8)]
    tile = sum(moved, part[0])
    moved = [xor_permute(tile, mask) for mask in (4, 8, 12)]
    moved, tail_grad = lax.optimization_barrier((moved, partner_hop(tail_grad, xor_value, 4, 4)))
    total = sum(moved, tile)

    start = tile_at(0, place, place[0]) * TILE
    values = lax.dynamic_slice_in_dim(relations, start, TILE, 1)
    state = lax.dynamic_slice_in_dim(relation_state, start, TILE)
    new_state = state + jnp.mean(total * total, axis=0)
    new_values = values - STEP_RATE * total / jnp.sqrt(new_state + EPSILON)[None, :]
    packed = jnp.concatenate([new_values, jnp.broadcast_to(new_state[None], (8, TILE))], axis=0)
    packed = jnp.stack([packed, xor_permute(packed, 2)])
    packed = jnp.concatenate([packed] + [inner_permute(packed, k) for k in (2, 4, 6)], axis=0)
    one, three, low, high = gather_four(packed, outer_permute)
    mine = jnp.concatenate([packed, one, three], axis=0)
    others = xor_permute(mine, 1)
    others, low, high = lax.optimization_barrier((others, low, high))
    last = jnp.concatenate([low, high], axis=0)
    other_last = xor_permute(last, 1)
    new_relations, state_row = place_columns(place, mine, last, others, other_last, width, relations.shape[1])
    return new_relations, state_row[0], tail_grad


def split_parts(x):
    high = x.astype(jnp.bfloat16)
    low = (x - high.astype(jnp.float32)).astype(jnp.bfloat16)
    return high, low


def dot(a, b):
    return jnp.dot(a, b, preferred_element_type=jnp.float32)


def dot_nt(a, b):
    return lax.dot_general(a, b, (((1,), (1,)), ((), ())), preferred_element_type=jnp.float32)


def one_hot(condition):
    return jnp.where(condition, 1.0, 0.0).astype(jnp.bfloat16)


def gather_kernel(shift, first_ref, keys_ref, table_ref, out_ref, parts, sums):
    width, count = table_ref.shape
    block = keys_ref.shape[1]
    edges = keys_ref.size
    half = width // 2
    window = 1024

    @pl.loop(0, count // 256)
    def _(k):
        at = pl.ds(pl.multiple_of(k * 256, 256), 256)
        tile = jnp.concatenate([table_ref[:, at], jnp.zeros((PART - width, 256), jnp.float32)], axis=0)
        high, low = split_parts(tile)
        parts[:PART, at] = high
        parts[PART:, at] = low

    row = lax.broadcasted_iota(jnp.int32, (256, 256), 0)

    @pl.loop(0, edges // 256)
    def _(c):
        there = pl.ds(pl.multiple_of(c * 256, 256), 256)
        group, chunk = c // (block // 256), c % (block // 256)
        ids = keys_ref[pl.ds(group, 1), pl.ds(pl.multiple_of(chunk * 256, 256), 256)] >> shift
        low = first_ref[group, chunk * 256] >> shift
        low = low // 128 * 128
        high = jnp.minimum((first_ref[group, chunk * 256 + 255] >> shift) + 1, count)
        sums[...] = jnp.zeros_like(sums)

        @pl.loop(0, jnp.maximum(high - low + window - 1, 0) // window)
        def _(w):
            wanted = low + w * window
            start = pl.multiple_of(jnp.minimum(wanted, count - window), 128)
            inside = jnp.where(ids < wanted, -1, jnp.where(ids < wanted + window, ids - start, -1))
            cols = None
            for k in range(window // 256):
                part = dot(parts[:, pl.ds(start + k * 256, 256)], one_hot(row + k * 256 == inside))
                cols = part if cols is None else cols + part
            sums[...] += cols

        cols = sums[:PART] + sums[PART:]
        out_ref[:HALF, there] = cols[:HALF]
        out_ref[HALF:, there] = cols[half : half + HALF]


def gather_relations(shift, keys, relations):
    width, count = relations.shape
    edges = keys.size
    vmem = pl.BlockSpec(memory_space=pltpu.VMEM)
    return pl.pallas_call(
        functools.partial(gather_kernel, shift),
        out_shape=jax.ShapeDtypeStruct((PART, edges), jnp.float32),
        in_specs=[pl.BlockSpec(memory_space=pltpu.SMEM), vmem, vmem],
        out_specs=vmem,
        scratch_shapes=[
            pltpu.VMEM((2 * PART, count), jnp.bfloat16),
            pltpu.VMEM((2 * PART, 256), jnp.float32),
        ],
        compiler_params=pltpu.CompilerParams(vmem_limit_bytes=VMEM_LIMIT),
        cost_estimate=pl.CostEstimate(
            flops=PART * count * edges, bytes_accessed=width * count * 4, transcendentals=0
        ),
        name="gather_relations",
    )(keys, keys, relations)


def padded_halves(block):
    half = block.shape[0] // 2
    blank = jnp.zeros((HALF - half, block.shape[1]), block.dtype)
    return jnp.concatenate([block[:half], blank, block[half:], blank], axis=0)


def edge_kernel(
    bits, keys_ref, negs_ref, head_ref, tail_ref, rels_ref,
    head_grad_ref, tail_grad_ref, rel_grad_ref,
    cols_ref, flip_ref, wide_ref, query_ref, weight_ref, counts_ref, sums_ref,
):
    width, rows = head_ref.shape
    edges = keys_ref.size
    chunk = weight_ref.shape[1]
    groups = negs_ref.shape[0]
    half = width // 2

    for side, ref in enumerate((head_ref, tail_ref)):
        block = padded_halves(ref[...])
        high, low = split_parts(block)
        cols_ref[side, :PART, :] = high
        cols_ref[side, PART:, :] = low
        wide_ref[side, :, :rows] = high
        wide_ref[side, :, rows : 2 * rows] = high
        wide_ref[side, :, 2 * rows :] = low
        turned = jnp.concatenate([block, jnp.zeros((256 - PART, rows), jnp.float32)], axis=0).T
        high, low = split_parts(turned)
        flip_ref[side, :, :256] = high
        flip_ref[side, :, 256:512] = high
        flip_ref[side, :, 512:] = low
    for group in range(groups):
        for which in range(2):
            hits = lax.broadcasted_iota(jnp.int32, (rows, negs_ref.shape[-1]), 0) == negs_ref[group, which][None, :]
            count = jnp.sum(jnp.where(hits, 1.0 / negs_ref.shape[-1], 0.0), axis=1, keepdims=True)
            counts_ref[group, which] = jnp.broadcast_to(count, (rows, 128))
    query_ref[...] = jnp.zeros_like(query_ref)
    sums_ref[...] = jnp.zeros_like(sums_ref)

    def put_query(side, query):
        high, low = split_parts(query)
        query_ref[side, :PART, :] = high
        query_ref[side, 256 : 256 + PART, :] = low
        query_ref[side, 512 : 512 + PART, :] = high

    def put_weight(side, weight):
        high, low = split_parts(weight)
        weight_ref[side * 3 * rows : side * 3 * rows + rows, :] = high
        weight_ref[side * 3 * rows + rows : side * 3 * rows + 2 * rows, :] = low
        weight_ref[side * 3 * rows + 2 * rows : side * 3 * rows + 3 * rows, :] = high

    def add_sums(side, left, right, left_again, right_low):
        both = dot_nt(left, right)
        total = both[:PART] + both[256 : 256 + PART]
        if left_again is not None:
            total = total + dot_nt(left_again, right_low)
        sums_ref[side] += total

    @pl.loop(0, edges // chunk)
    def _(c):
        at = pl.ds(pl.multiple_of(c * chunk, chunk), chunk)
        group = c // (edges // groups // chunk)
        inner = edges // groups // chunk
        keys = keys_ref[pl.ds(group, 1), pl.ds(pl.multiple_of(c % inner * chunk, chunk), chunk)]
        heads = keys >> bits & 2**bits - 1
        tails = keys & 2**bits - 1
        row = lax.broadcasted_iota(jnp.int32, (rows, chunk), 0)
        head_hot = one_hot(row == heads)
        tail_is = row == tails
        tail_hot = one_hot(tail_is)
        h = dot(cols_ref[0], head_hot)
        h = h[:PART] + h[PART:]
        t = dot(cols_ref[1], tail_hot)
        t = t[:PART] + t[PART:]
        r = rels_ref[:, at]
        h_re, h_im, t_re, t_im, r_re, r_im = h[:HALF], h[HALF:], t[:HALF], t[HALF:], r[:HALF], r[HALF:]
        put_query(0, jnp.concatenate([r_re * t_re + r_im * t_im, r_re * t_im - r_im * t_re], axis=0))
        put_query(1, jnp.concatenate([h_re * r_re - h_im * r_im, h_re * r_im + h_im * r_re], axis=0))
        grads = []
        for side in range(2):
            scores = dot(flip_ref[side], query_ref[side])
            chance = 0.5 * jnp.tanh(0.5 * scores) + 0.5
            count = counts_ref[group, 1 - side][:, :1]
            if side == 0:
                weight = chance * count
            else:
                hot = jnp.where(tail_is, 1.0, 0.0)
                weight = chance * (count + hot) - hot
            put_weight(side, weight)
            base = side * 3 * rows
            grads.append(dot(wide_ref[side], weight_ref[base : base + 3 * rows, :]))
            add_sums(
                side, query_ref[side, : 256 + PART, :], weight_ref[base : base + rows, :],
                query_ref[side, :PART, :], weight_ref[base + rows : base + 2 * rows, :],
            )
        qh_re, qh_im, qt_re, qt_im = grads[0][:HALF], grads[0][HALF:], grads[1][:HALF], grads[1][HALF:]
        dh = jnp.concatenate([qt_re * r_re + qt_im * r_im, qt_im * r_re - qt_re * r_im], axis=0)
        dt = jnp.concatenate([qh_re * r_re - qh_im * r_im, qh_re * r_im + qh_im * r_re], axis=0)
        dr = jnp.concatenate(
            [
                qt_re * h_re + qt_im * h_im + qh_re * t_re + qh_im * t_im,
                qt_im * h_re - qt_re * h_im + qh_re * t_im - qh_im * t_re,
            ],
            axis=0,
        )
        high, low = split_parts(dr)
        rel_grad_ref[:PART, at] = high
        rel_grad_ref[PART:, at] = low
        put_query(0, dh)
        add_sums(0, query_ref[0, : 256 + PART, :], head_hot, None, None)
        put_query(1, dt)
        add_sums(1, query_ref[1, : 256 + PART, :], tail_hot, None, None)

    for side, ref in enumerate((head_grad_ref, tail_grad_ref)):
        ref[:half, :] = sums_ref[side, :half, :]
        ref[half:, :] = sums_ref[side, HALF : HALF + half, :]


def edge_gradients(bits, keys, negs, head_blk, tail_blk, rels):
    width, rows = head_blk.shape
    edges = keys.size
    chunk = edges // negs.shape[0]
    vmem = pl.BlockSpec(memory_space=pltpu.VMEM)
    return pl.pallas_call(
        functools.partial(edge_kernel, bits),
        out_shape=(
            jax.ShapeDtypeStruct((width, rows), jnp.float32),
            jax.ShapeDtypeStruct((width, rows), jnp.float32),
            jax.ShapeDtypeStruct((2 * PART, edges), jnp.bfloat16),
        ),
        in_specs=[vmem] * 5,
        out_specs=(vmem, vmem, vmem),
        scratch_shapes=[
            pltpu.VMEM((2, 2 * PART, rows), jnp.bfloat16),
            pltpu.VMEM((2, rows, 768), jnp.bfloat16),
            pltpu.VMEM((2, PART, 3 * rows), jnp.bfloat16),
            pltpu.VMEM((2, 768, chunk), jnp.bfloat16),
            pltpu.VMEM((6 * rows, chunk), jnp.bfloat16),
            pltpu.VMEM((negs.shape[0], 2, rows, 128), jnp.float32),
            pltpu.VMEM((2, PART, rows), jnp.float32),
        ],
        compiler_params=pltpu.CompilerParams(vmem_limit_bytes=VMEM_LIMIT),
        cost_estimate=pl.CostEstimate(
            flops=40 * PART * rows * edges, bytes_accessed=4 * PART * edges, transcendentals=2 * rows * edges
        ),
        name="edge_gradients",
    )(keys, negs, head_blk, tail_blk, rels)


def tile_at(position, place_ref, core):
    outer = (position // 8) ^ place_ref[1 + core]
    inner = (position // 2 % 4) ^ place_ref[2 - core]
    return core * 32 + outer * 8 + inner * 2 + (position % 2 ^ place_ref[3])


def scatter_kernel(other, groups, place_ref, starts_ref, ids_ref, grad_ref, out_ref, spread_ref, sums):
    tiles, width, tile = out_ref.shape
    core = jnp.where(other, 1 - place_ref[0], place_ref[0])
    edges = ids_ref.shape[0]
    block = edges // groups
    last = starts_ref.shape[0] // groups - 1
    half = width // 2
    pairs = sums.shape[0]
    spread_ref[...] = jnp.broadcast_to(ids_ref[...], spread_ref.shape)

    @pl.loop(0, tiles // 2 // pairs)
    def _(i):
        lane = lax.broadcasted_iota(jnp.int32, (256, tile), 1)
        row = lax.broadcasted_iota(jnp.int32, (256, tile), 0)
        spans = []
        for u in range(pairs):
            j = i * pairs + u
            first = tile_at(2 * j, place_ref, core)
            base = first // 2 * 2
            total = None
            for group in range(groups):
                low = starts_ref[group * (last + 1) + jnp.minimum(base, last)]
                high = starts_ref[group * (last + 1) + jnp.minimum(base + 2, last)]
                low = low // 128 * 128
                spans.append((u, group, base, low, high))
                at = pl.ds(pl.multiple_of(group * block + jnp.minimum(low, block - 256), 128), 256)
                ids = spread_ref[at, :] - base * tile
                hot = jnp.concatenate([one_hot(lane == ids), one_hot(lane + tile == ids)], axis=1)
                part = dot(grad_ref[:, at], hot)
                total = part if total is None else total + part
            sums[u] = total
        for u, group, base, low, high in spans:

            @pl.loop(1, jnp.maximum(high - low + 255, 256) // 256)
            def _(w):
                wanted = low + w * 256
                start = jnp.minimum(wanted, block - 256)
                at = pl.ds(pl.multiple_of(group * block + start, 128), 256)
                ids = jnp.where(row + start < wanted, -1, spread_ref[at, :] - base * tile)
                hot = jnp.concatenate([one_hot(lane == ids), one_hot(lane + tile == ids)], axis=1)
                sums[u] += dot(grad_ref[:, at], hot)

        for u in range(pairs):
            cols = sums[u, :PART] + sums[u, PART:]
            for side in range(2):
                part = cols[:, side * tile : (side + 1) * tile]
                to = 2 * (i * pairs + u) + (side ^ place_ref[3])
                out_ref[to, :half, :] = part[:half]
                out_ref[to, half:, :] = part[HALF : HALF + half]


def scatter_relations(other, place, starts, ids, grads, tiles, width):
    edges = grads.shape[1]
    vmem = pl.BlockSpec(memory_space=pltpu.VMEM)
    smem = pl.BlockSpec(memory_space=pltpu.SMEM)
    return pl.pallas_call(
        functools.partial(scatter_kernel, other, starts.shape[0]),
        out_shape=jax.ShapeDtypeStruct((tiles, width, TILE), jnp.float32),
        in_specs=[smem, smem, vmem, vmem],
        out_specs=vmem,
        scratch_shapes=[pltpu.VMEM((edges, TILE), jnp.int32), pltpu.VMEM((2, 2 * PART, 2 * TILE), jnp.float32)],
        compiler_params=pltpu.CompilerParams(vmem_limit_bytes=VMEM_LIMIT),
        cost_estimate=pl.CostEstimate(
            flops=PART * edges * tiles * TILE, bytes_accessed=tiles * width * TILE * 4, transcendentals=0
        ),
        name="scatter_relations",
    )(place, starts.reshape(starts.size), ids, grads)


def place_kernel(place_ref, mine_ref, last_ref, others_ref, other_last_ref, out_ref, state_ref, low_ref, high_ref, sent):
    width, count = out_ref.shape
    sources = ((mine_ref, last_ref), (others_ref, other_last_ref))
    copies = []
    for half, cols_ref in enumerate((low_ref, high_ref)):
        first = half * 32 * TILE
        for own in range(2):
            most, last = sources[(own + half) % 2]

            @pl.when(place_ref[0] == own)
            def _():
                for chunk, source, base in ((0, most, 0), (1, most, 8), (3, most, 16), (2, last, 0)):

                    @pl.loop(0, 8)
                    def _(j):
                        tile = tile_at(chunk * 8 + j, place_ref, half)

                        @pl.when(tile < count // TILE)
                        def _():
                            at = pl.multiple_of(tile * TILE, TILE)
                            here = pl.multiple_of(at - first, TILE)
                            cols_ref[:, pl.ds(here, TILE)] = source[base + j, :width, :]
                            state_ref[:, pl.ds(at, TILE)] = source[base + j, width : width + 1, :]

        there = out_ref.at[:, pl.ds(first, cols_ref.shape[1])]
        copies.append(pltpu.make_async_copy(cols_ref, there, sent.at[half]))
        copies[-1].start()
    for copy in copies:
        copy.wait()


def place_columns(place, mine, last, others, other_last, width, count):
    vmem = pl.BlockSpec(memory_space=pltpu.VMEM)
    return pl.pallas_call(
        place_kernel,
        out_shape=(
            jax.ShapeDtypeStruct((width, count), jnp.float32),
            jax.ShapeDtypeStruct((1, count), jnp.float32),
        ),
        in_specs=[pl.BlockSpec(memory_space=pltpu.SMEM)] + [vmem] * 4,
        out_specs=(pl.BlockSpec(memory_space=pl.ANY), vmem),
        scratch_shapes=[
            pltpu.VMEM((width, 32 * TILE), jnp.float32),
            pltpu.VMEM((width, count - 32 * TILE), jnp.float32),
            pltpu.SemaphoreType.DMA((2,)),
        ],
        compiler_params=pltpu.CompilerParams(vmem_limit_bytes=VMEM_LIMIT),
        cost_estimate=pl.CostEstimate(flops=0, bytes_accessed=8 * width * count, transcendentals=0),
        name="place_columns",
    )(place, mine, last, others, other_last)


def on_device(
    entities,
    entity_state,
    relations,
    relation_state,
    head_rows,
    relation_ids,
    tail_rows,
    neg_rows,
    edge_counts,
    matching,
):
    me = lax.axis_index("dom")
    core = me & 1
    xor_value = jnp.bitwise_xor(matching[0], me)
    width, count = relations.shape
    edges = head_rows.shape[1]
    half = -(-count // (64 * TILE)) * 32

    groups = neg_rows.shape[1]
    bits = (entities.shape[1] - 1).bit_length()
    shift = 2 * bits
    assert groups <= 2 and (count - 1).bit_length() + shift <= 31 and count < 2 ** (31 - shift) and entities.shape[1] < 2**bits

    keys = (relation_ids << shift | head_rows << bits | tail_rows)[0]
    slots = lax.broadcasted_iota(jnp.int32, keys.shape, 0)
    keys = jnp.where(slots < edge_counts[0], keys, 2**31 - 1).astype(jnp.uint32)
    keys = keys | (slots // (edges // groups)).astype(jnp.uint32) << 31

    def sort_keys(keys):
        keys = lax.sort(keys)
        keys = (keys & jnp.uint32(2**31 - 1)).astype(jnp.int32).reshape(groups, edges // groups)
        firsts = jnp.arange(count // TILE + 1, dtype=jnp.int32) * TILE
        before = (keys >> shift)[:, None, :] < firsts[None, :, None]
        return keys, jnp.sum(before.astype(jnp.int32), axis=2)

    tail_blk, (keys, starts) = partner_hop(entities, xor_value, 0, 1, sort_keys, keys)
    tail_blk = partner_hop(tail_blk, xor_value, 4, 4)
    gather = functools.partial(gather_relations, shift)
    tail_blk, rels = partner_hop(tail_blk, xor_value, 1, 3, gather, keys, relations)
    head_grad, tail_grad, rel_grad = edge_gradients(
        bits, keys, neg_rows[0], entities, tail_blk, rels
    )

    column = (keys >> shift).reshape(edges, 1)
    place = jnp.stack([core, (me >> 6) & 3, (me >> 4) & 3, (me >> 1) & 1])
    send = scatter_relations(True, place, starts, column, rel_grad, half, width)
    received = xor_permute(send, 1)
    keep = scatter_relations(False, place, starts, column, rel_grad, half, width)
    new_relations, new_relation_state, tail_grad = update_relations(
        place, keep, received, relations, relation_state, tail_grad, xor_value
    )
    combined = head_grad + tail_grad
    new_entity_state = entity_state + jnp.mean(combined * combined, axis=0)
    new_entities = entities - STEP_RATE * combined / jnp.sqrt(new_entity_state + EPSILON)[None, :]
    return (new_entities, new_entity_state, new_relations, new_relation_state)


def solution(mesh):
    in_specs = (
        P(None, "dom"),
        P("dom"),
        P(),
        P(),
        P("dom", None),
        P("dom", None),
        P("dom", None),
        P("dom", None, None, None),
        P("dom"),
        P("dom"),
    )
    out_specs = (P(None, "dom"), P("dom"), P(), P())
    return jax.shard_map(
        on_device, mesh=mesh, in_specs=in_specs, out_specs=out_specs, check_vma=False
    )
```

```python
import functools

import jax
import jax.numpy as jnp
from jax import lax
from jax.experimental import pallas as pl
from jax.experimental.pallas import tpu as pltpu
from jax.sharding import PartitionSpec as P

TILE = 128
HALF = 104
PART = 2 * HALF
VMEM_LIMIT = 24 * 2**20
STEP_RATE = 0.3
EPSILON = 1e-08


def pair_permute(value, low_mask, high_mask):
    size = lax.axis_size("dom")
    return lax.ppermute(value, "dom", [(i, i ^ (high_mask if i & 1 else low_mask)) for i in range(size)])


def xor_permute(value, mask):
    return pair_permute(value, mask, mask)


def outer_permute(value, k):
    return pair_permute(value, k << 6, k << 4)


def inner_permute(value, k):
    ring, z = k >> 1, k & 1
    return pair_permute(value, ring << 4 | z << 1, ring << 6 | z << 1)


def partner_hop(value, xor_value, low, width, work=None, *operands):
    pick = (xor_value >> low) & (2**width - 1)

    def branch(mask, v, *rest):
        moved = xor_permute(v, mask) if mask else v
        return (moved, work(*rest)) if work else moved

    return lax.switch(pick, [functools.partial(branch, m << low) for m in range(2**width)], value, *operands)


def update_relations(place, keep, received, relations, relation_state, tail_grad, xor_value):
    half, width, _ = keep.shape
    chunk = half // 4
    parts = [keep[k * chunk : (k + 1) * chunk] + received[k * chunk : (k + 1) * chunk] for k in range(4)]
    moved = [outer_permute(parts[k], k) for k in (2, 1, 3)]
    tail_grad = partner_hop(partner_hop(tail_grad, xor_value, 0, 1), xor_value, 4, 4)
    moved, tail_grad = lax.optimization_barrier((moved, tail_grad))
    part = sum(moved, parts[0])
    moved = [inner_permute(part[k], k) for k in range(1, 8)]
    tile = sum(moved, part[0])
    moved = [xor_permute(tile, mask) for mask in (4, 8, 12)]
    total = sum(moved, tile)

    start = tile_at(0, place, place[0]) * TILE
    values = lax.dynamic_slice_in_dim(relations, start, TILE, 1)
    state = lax.dynamic_slice_in_dim(relation_state, start, TILE)
    new_state = state + jnp.mean(total * total, axis=0)
    new_values = values - STEP_RATE * total / jnp.sqrt(new_state + EPSILON)[None, :]
    packed = jnp.concatenate([new_values, jnp.broadcast_to(new_state[None], (8, TILE))], axis=0)
    packed = jnp.stack([packed, xor_permute(packed, 2)])
    packed = jnp.concatenate([packed] + [inner_permute(packed, k) for k in (2, 4, 6)], axis=0)
    one, three = outer_permute(packed, 1), outer_permute(packed, 3)
    one, three, tail_grad = lax.optimization_barrier((one, three, partner_hop(tail_grad, xor_value, 1, 3)))
    half = packed.shape[0] // 2
    low, high = outer_permute(three[:half], 1), outer_permute(one[half:], 3)
    mine = jnp.concatenate([packed, one, three], axis=0)
    others = xor_permute(mine, 1)
    others, low, high = lax.optimization_barrier((others, low, high))
    last = jnp.concatenate([low, high], axis=0)
    other_last = xor_permute(last, 1)
    new_relations, state_row = place_columns(place, mine, last, others, other_last, width, relations.shape[1])
    return new_relations, state_row[0], tail_grad


def split_parts(x):
    high = x.astype(jnp.bfloat16)
    low = (x - high.astype(jnp.float32)).astype(jnp.bfloat16)
    return high, low


def dot(a, b):
    return jnp.dot(a, b, preferred_element_type=jnp.float32)


def dot_nt(a, b):
    return lax.dot_general(a, b, (((1,), (1,)), ((), ())), preferred_element_type=jnp.float32)


def one_hot(condition):
    return jnp.where(condition, 1.0, 0.0).astype(jnp.bfloat16)


def gather_kernel(shift, first_ref, keys_ref, table_ref, out_ref, parts, sums):
    width, count = table_ref.shape
    block = keys_ref.shape[1]
    edges = keys_ref.size
    half = width // 2
    window = 1024

    @pl.loop(0, count // 256)
    def _(k):
        at = pl.ds(pl.multiple_of(k * 256, 256), 256)
        tile = jnp.concatenate([table_ref[:, at], jnp.zeros((PART - width, 256), jnp.float32)], axis=0)
        high, low = split_parts(tile)
        parts[:PART, at] = high
        parts[PART:, at] = low

    row = lax.broadcasted_iota(jnp.int32, (256, 256), 0)

    @pl.loop(0, edges // 256)
    def _(c):
        there = pl.ds(pl.multiple_of(c * 256, 256), 256)
        group, chunk = c // (block // 256), c % (block // 256)
        ids = keys_ref[pl.ds(group, 1), pl.ds(pl.multiple_of(chunk * 256, 256), 256)] >> shift
        low = first_ref[group, chunk * 256] >> shift
        low = low // 128 * 128
        high = jnp.minimum((first_ref[group, chunk * 256 + 255] >> shift) + 1, count)
        sums[...] = jnp.zeros_like(sums)

        @pl.loop(0, jnp.maximum(high - low + window - 1, 0) // window)
        def _(w):
            wanted = low + w * window
            start = pl.multiple_of(jnp.minimum(wanted, count - window), 128)
            inside = jnp.where(ids < wanted, -1, jnp.where(ids < wanted + window, ids - start, -1))
            cols = None
            for k in range(window // 256):
                part = dot(parts[:, pl.ds(start + k * 256, 256)], one_hot(row + k * 256 == inside))
                cols = part if cols is None else cols + part
            sums[...] += cols

        cols = sums[:PART] + sums[PART:]
        out_ref[:HALF, there] = cols[:HALF]
        out_ref[HALF:, there] = cols[half : half + HALF]


def gather_relations(shift, keys, relations):
    width, count = relations.shape
    edges = keys.size
    vmem = pl.BlockSpec(memory_space=pltpu.VMEM)
    return pl.pallas_call(
        functools.partial(gather_kernel, shift),
        out_shape=jax.ShapeDtypeStruct((PART, edges), jnp.float32),
        in_specs=[pl.BlockSpec(memory_space=pltpu.SMEM), vmem, vmem],
        out_specs=vmem,
        scratch_shapes=[
            pltpu.VMEM((2 * PART, count), jnp.bfloat16),
            pltpu.VMEM((2 * PART, 256), jnp.float32),
        ],
        compiler_params=pltpu.CompilerParams(vmem_limit_bytes=VMEM_LIMIT),
        cost_estimate=pl.CostEstimate(
            flops=PART * count * edges, bytes_accessed=width * count * 4, transcendentals=0
        ),
        name="gather_relations",
    )(keys, keys, relations)


def padded_halves(block):
    half = block.shape[0] // 2
    blank = jnp.zeros((HALF - half, block.shape[1]), block.dtype)
    return jnp.concatenate([block[:half], blank, block[half:], blank], axis=0)


def edge_kernel(
    bits, keys_ref, negs_ref, head_ref, tail_ref, rels_ref,
    head_grad_ref, tail_grad_ref, rel_grad_ref,
    cols_ref, flip_ref, wide_ref, query_ref, weight_ref, counts_ref, sums_ref,
):
    width, rows = head_ref.shape
    edges = keys_ref.size
    chunk = weight_ref.shape[1]
    groups = negs_ref.shape[0]
    half = width // 2

    for side, ref in enumerate((head_ref, tail_ref)):
        block = padded_halves(ref[...])
        high, low = split_parts(block)
        cols_ref[side, :PART, :] = high
        cols_ref[side, PART:, :] = low
        wide_ref[side, :, :rows] = high
        wide_ref[side, :, rows : 2 * rows] = high
        wide_ref[side, :, 2 * rows :] = low
        turned = jnp.concatenate([block, jnp.zeros((256 - PART, rows), jnp.float32)], axis=0).T
        high, low = split_parts(turned)
        flip_ref[side, :, :256] = high
        flip_ref[side, :, 256:512] = high
        flip_ref[side, :, 512:] = low
    for group in range(groups):
        for which in range(2):
            hits = lax.broadcasted_iota(jnp.int32, (rows, negs_ref.shape[-1]), 0) == negs_ref[group, which][None, :]
            count = jnp.sum(jnp.where(hits, 1.0 / negs_ref.shape[-1], 0.0), axis=1, keepdims=True)
            counts_ref[group, which] = jnp.broadcast_to(count, (rows, 128))
    query_ref[...] = jnp.zeros_like(query_ref)
    sums_ref[...] = jnp.zeros_like(sums_ref)

    def put_query(side, query):
        high, low = split_parts(query)
        query_ref[side, :PART, :] = high
        query_ref[side, 256 : 256 + PART, :] = low
        query_ref[side, 512 : 512 + PART, :] = high

    def put_weight(side, weight):
        high, low = split_parts(weight)
        weight_ref[side * 3 * rows : side * 3 * rows + rows, :] = high
        weight_ref[side * 3 * rows + rows : side * 3 * rows + 2 * rows, :] = low
        weight_ref[side * 3 * rows + 2 * rows : side * 3 * rows + 3 * rows, :] = high

    def add_sums(side, left, right, left_again, right_low):
        both = dot_nt(left, right)
        total = both[:PART] + both[256 : 256 + PART]
        if left_again is not None:
            total = total + dot_nt(left_again, right_low)
        sums_ref[side] += total

    @pl.loop(0, edges // chunk)
    def _(c):
        at = pl.ds(pl.multiple_of(c * chunk, chunk), chunk)
        group = c // (edges // groups // chunk)
        inner = edges // groups // chunk
        keys = keys_ref[pl.ds(group, 1), pl.ds(pl.multiple_of(c % inner * chunk, chunk), chunk)]
        heads = keys >> bits & 2**bits - 1
        tails = keys & 2**bits - 1
        row = lax.broadcasted_iota(jnp.int32, (rows, chunk), 0)
        head_hot = one_hot(row == heads)
        tail_is = row == tails
        tail_hot = one_hot(tail_is)
        h = dot(cols_ref[0], head_hot)
        h = h[:PART] + h[PART:]
        t = dot(cols_ref[1], tail_hot)
        t = t[:PART] + t[PART:]
        r = rels_ref[:, at]
        h_re, h_im, t_re, t_im, r_re, r_im = h[:HALF], h[HALF:], t[:HALF], t[HALF:], r[:HALF], r[HALF:]
        put_query(0, jnp.concatenate([r_re * t_re + r_im * t_im, r_re * t_im - r_im * t_re], axis=0))
        put_query(1, jnp.concatenate([h_re * r_re - h_im * r_im, h_re * r_im + h_im * r_re], axis=0))
        grads = []
        for side in range(2):
            scores = dot(flip_ref[side], query_ref[side])
            chance = 0.5 * jnp.tanh(0.5 * scores) + 0.5
            count = counts_ref[group, 1 - side][:, :1]
            if side == 0:
                weight = chance * count
            else:
                hot = jnp.where(tail_is, 1.0, 0.0)
                weight = chance * (count + hot) - hot
            put_weight(side, weight)
            base = side * 3 * rows
            grads.append(dot(wide_ref[side], weight_ref[base : base + 3 * rows, :]))
            add_sums(
                side, query_ref[side, : 256 + PART, :], weight_ref[base : base + rows, :],
                query_ref[side, :PART, :], weight_ref[base + rows : base + 2 * rows, :],
            )
        qh_re, qh_im, qt_re, qt_im = grads[0][:HALF], grads[0][HALF:], grads[1][:HALF], grads[1][HALF:]
        dh = jnp.concatenate([qt_re * r_re + qt_im * r_im, qt_im * r_re - qt_re * r_im], axis=0)
        dt = jnp.concatenate([qh_re * r_re - qh_im * r_im, qh_re * r_im + qh_im * r_re], axis=0)
        dr = jnp.concatenate(
            [
                qt_re * h_re + qt_im * h_im + qh_re * t_re + qh_im * t_im,
                qt_im * h_re - qt_re * h_im + qh_re * t_im - qh_im * t_re,
            ],
            axis=0,
        )
        high, low = split_parts(dr)
        rel_grad_ref[:PART, at] = high
        rel_grad_ref[PART:, at] = low
        put_query(0, dh)
        add_sums(0, query_ref[0, : 256 + PART, :], head_hot, None, None)
        put_query(1, dt)
        add_sums(1, query_ref[1, : 256 + PART, :], tail_hot, None, None)

    for side, ref in enumerate((head_grad_ref, tail_grad_ref)):
        ref[:half, :] = sums_ref[side, :half, :]
        ref[half:, :] = sums_ref[side, HALF : HALF + half, :]


def edge_gradients(bits, keys, negs, head_blk, tail_blk, rels):
    width, rows = head_blk.shape
    edges = keys.size
    chunk = edges // negs.shape[0]
    vmem = pl.BlockSpec(memory_space=pltpu.VMEM)
    return pl.pallas_call(
        functools.partial(edge_kernel, bits),
        out_shape=(
            jax.ShapeDtypeStruct((width, rows), jnp.float32),
            jax.ShapeDtypeStruct((width, rows), jnp.float32),
            jax.ShapeDtypeStruct((2 * PART, edges), jnp.bfloat16),
        ),
        in_specs=[vmem] * 5,
        out_specs=(vmem, vmem, vmem),
        scratch_shapes=[
            pltpu.VMEM((2, 2 * PART, rows), jnp.bfloat16),
            pltpu.VMEM((2, rows, 768), jnp.bfloat16),
            pltpu.VMEM((2, PART, 3 * rows), jnp.bfloat16),
            pltpu.VMEM((2, 768, chunk), jnp.bfloat16),
            pltpu.VMEM((6 * rows, chunk), jnp.bfloat16),
            pltpu.VMEM((negs.shape[0], 2, rows, 128), jnp.float32),
            pltpu.VMEM((2, PART, rows), jnp.float32),
        ],
        compiler_params=pltpu.CompilerParams(vmem_limit_bytes=VMEM_LIMIT),
        cost_estimate=pl.CostEstimate(
            flops=40 * PART * rows * edges, bytes_accessed=4 * PART * edges, transcendentals=2 * rows * edges
        ),
        name="edge_gradients",
    )(keys, negs, head_blk, tail_blk, rels)


def tile_at(position, place_ref, core):
    outer = (position // 8) ^ place_ref[1 + core]
    inner = (position // 2 % 4) ^ place_ref[2 - core]
    return core * 32 + outer * 8 + inner * 2 + (position % 2 ^ place_ref[3])


def scatter_kernel(other, groups, place_ref, starts_ref, ids_ref, grad_ref, out_ref, spread_ref, sums):
    tiles, width, tile = out_ref.shape
    core = jnp.where(other, 1 - place_ref[0], place_ref[0])
    edges = ids_ref.shape[0]
    block = edges // groups
    last = starts_ref.shape[0] // groups - 1
    half = width // 2
    pairs = sums.shape[0]
    spread_ref[...] = jnp.broadcast_to(ids_ref[...], spread_ref.shape)

    @pl.loop(0, tiles // 2 // pairs)
    def _(i):
        lane = lax.broadcasted_iota(jnp.int32, (256, tile), 1)
        row = lax.broadcasted_iota(jnp.int32, (256, tile), 0)
        spans = []
        for u in range(pairs):
            j = i * pairs + u
            first = tile_at(2 * j, place_ref, core)
            base = first // 2 * 2
            total = None
            for group in range(groups):
                low = starts_ref[group * (last + 1) + jnp.minimum(base, last)]
                high = starts_ref[group * (last + 1) + jnp.minimum(base + 2, last)]
                low = low // 128 * 128
                spans.append((u, group, base, low, high))
                at = pl.ds(pl.multiple_of(group * block + jnp.minimum(low, block - 256), 128), 256)
                ids = spread_ref[at, :] - base * tile
                hot = jnp.concatenate([one_hot(lane == ids), one_hot(lane + tile == ids)], axis=1)
                part = dot(grad_ref[:, at], hot)
                total = part if total is None else total + part
            sums[u] = total
        for u, group, base, low, high in spans:

            @pl.loop(1, jnp.maximum(high - low + 255, 256) // 256)
            def _(w):
                wanted = low + w * 256
                start = jnp.minimum(wanted, block - 256)
                at = pl.ds(pl.multiple_of(group * block + start, 128), 256)
                ids = jnp.where(row + start < wanted, -1, spread_ref[at, :] - base * tile)
                hot = jnp.concatenate([one_hot(lane == ids), one_hot(lane + tile == ids)], axis=1)
                sums[u] += dot(grad_ref[:, at], hot)

        for u in range(pairs):
            cols = sums[u, :PART] + sums[u, PART:]
            for side in range(2):
                part = cols[:, side * tile : (side + 1) * tile]
                to = 2 * (i * pairs + u) + (side ^ place_ref[3])
                out_ref[to, :half, :] = part[:half]
                out_ref[to, half:, :] = part[HALF : HALF + half]


def scatter_relations(other, place, starts, ids, grads, tiles, width):
    edges = grads.shape[1]
    vmem = pl.BlockSpec(memory_space=pltpu.VMEM)
    smem = pl.BlockSpec(memory_space=pltpu.SMEM)
    return pl.pallas_call(
        functools.partial(scatter_kernel, other, starts.shape[0]),
        out_shape=jax.ShapeDtypeStruct((tiles, width, TILE), jnp.float32),
        in_specs=[smem, smem, vmem, vmem],
        out_specs=vmem,
        scratch_shapes=[pltpu.VMEM((edges, TILE), jnp.int32), pltpu.VMEM((2, 2 * PART, 2 * TILE), jnp.float32)],
        compiler_params=pltpu.CompilerParams(vmem_limit_bytes=VMEM_LIMIT),
        cost_estimate=pl.CostEstimate(
            flops=PART * edges * tiles * TILE, bytes_accessed=tiles * width * TILE * 4, transcendentals=0
        ),
        name="scatter_relations",
    )(place, starts.reshape(starts.size), ids, grads)


def place_kernel(place_ref, mine_ref, last_ref, others_ref, other_last_ref, out_ref, state_ref, low_ref, high_ref, sent):
    width, count = out_ref.shape
    sources = ((mine_ref, last_ref), (others_ref, other_last_ref))
    copies = []
    for half, cols_ref in enumerate((low_ref, high_ref)):
        first = half * 32 * TILE
        for own in range(2):
            most, last = sources[(own + half) % 2]

            @pl.when(place_ref[0] == own)
            def _():
                for chunk, source, base in ((0, most, 0), (1, most, 8), (3, most, 16), (2, last, 0)):

                    @pl.loop(0, 8)
                    def _(j):
                        tile = tile_at(chunk * 8 + j, place_ref, half)

                        @pl.when(tile < count // TILE)
                        def _():
                            at = pl.multiple_of(tile * TILE, TILE)
                            here = pl.multiple_of(at - first, TILE)
                            cols_ref[:, pl.ds(here, TILE)] = source[base + j, :width, :]
                            state_ref[:, pl.ds(at, TILE)] = source[base + j, width : width + 1, :]

        there = out_ref.at[:, pl.ds(first, cols_ref.shape[1])]
        copies.append(pltpu.make_async_copy(cols_ref, there, sent.at[half]))
        copies[-1].start()
    for copy in copies:
        copy.wait()


def place_columns(place, mine, last, others, other_last, width, count):
    vmem = pl.BlockSpec(memory_space=pltpu.VMEM)
    return pl.pallas_call(
        place_kernel,
        out_shape=(
            jax.ShapeDtypeStruct((width, count), jnp.float32),
            jax.ShapeDtypeStruct((1, count), jnp.float32),
        ),
        in_specs=[pl.BlockSpec(memory_space=pltpu.SMEM)] + [vmem] * 4,
        out_specs=(pl.BlockSpec(memory_space=pl.ANY), vmem),
        scratch_shapes=[
            pltpu.VMEM((width, 32 * TILE), jnp.float32),
            pltpu.VMEM((width, count - 32 * TILE), jnp.float32),
            pltpu.SemaphoreType.DMA((2,)),
        ],
        compiler_params=pltpu.CompilerParams(vmem_limit_bytes=VMEM_LIMIT),
        cost_estimate=pl.CostEstimate(flops=0, bytes_accessed=8 * width * count, transcendentals=0),
        name="place_columns",
    )(place, mine, last, others, other_last)


def on_device(
    entities,
    entity_state,
    relations,
    relation_state,
    head_rows,
    relation_ids,
    tail_rows,
    neg_rows,
    edge_counts,
    matching,
):
    me = lax.axis_index("dom")
    core = me & 1
    xor_value = jnp.bitwise_xor(matching[0], me)
    width, count = relations.shape
    edges = head_rows.shape[1]
    half = -(-count // (64 * TILE)) * 32

    groups = neg_rows.shape[1]
    bits = (entities.shape[1] - 1).bit_length()
    shift = 2 * bits
    assert groups <= 2 and (count - 1).bit_length() + shift <= 31 and count < 2 ** (31 - shift) and entities.shape[1] < 2**bits

    keys = (relation_ids << shift | head_rows << bits | tail_rows)[0]
    slots = lax.broadcasted_iota(jnp.int32, keys.shape, 0)
    keys = jnp.where(slots < edge_counts[0], keys, 2**31 - 1).astype(jnp.uint32)
    keys = keys | (slots // (edges // groups)).astype(jnp.uint32) << 31

    def sort_keys(keys):
        keys = lax.sort(keys)
        keys = (keys & jnp.uint32(2**31 - 1)).astype(jnp.int32).reshape(groups, edges // groups)
        firsts = jnp.arange(count // TILE + 1, dtype=jnp.int32) * TILE
        before = (keys >> shift)[:, None, :] < firsts[None, :, None]
        return keys, jnp.sum(before.astype(jnp.int32), axis=2)

    tail_blk, (keys, starts) = partner_hop(entities, xor_value, 0, 1, sort_keys, keys)
    tail_blk = partner_hop(tail_blk, xor_value, 4, 4)
    gather = functools.partial(gather_relations, shift)
    tail_blk, rels = partner_hop(tail_blk, xor_value, 1, 3, gather, keys, relations)
    head_grad, tail_grad, rel_grad = edge_gradients(
        bits, keys, neg_rows[0], entities, tail_blk, rels
    )

    column = (keys >> shift).reshape(edges, 1)
    place = jnp.stack([core, (me >> 6) & 3, (me >> 4) & 3, (me >> 1) & 1])
    send = scatter_relations(True, place, starts, column, rel_grad, half, width)
    received = xor_permute(send, 1)
    keep = scatter_relations(False, place, starts, column, rel_grad, half, width)
    new_relations, new_relation_state, tail_grad = update_relations(
        place, keep, received, relations, relation_state, tail_grad, xor_value
    )
    combined = head_grad + tail_grad
    new_entity_state = entity_state + jnp.mean(combined * combined, axis=0)
    new_entities = entities - STEP_RATE * combined / jnp.sqrt(new_entity_state + EPSILON)[None, :]
    return (new_entities, new_entity_state, new_relations, new_relation_state)


def solution(mesh):
    in_specs = (
        P(None, "dom"),
        P("dom"),
        P(),
        P(),
        P("dom", None),
        P("dom", None),
        P("dom", None),
        P("dom", None, None, None),
        P("dom"),
        P("dom"),
    )
    out_specs = (P(None, "dom"), P("dom"), P(), P())
    return jax.shard_map(
        on_device, mesh=mesh, in_specs=in_specs, out_specs=out_specs, check_vma=False
    )
```

```python
import functools

import jax
import jax.numpy as jnp
from jax import lax
from jax.experimental import pallas as pl
from jax.experimental.pallas import tpu as pltpu
from jax.sharding import PartitionSpec as P

TILE = 128
HALF = 104
PART = 2 * HALF
VMEM_LIMIT = 24 * 2**20
STEP_RATE = 0.3
EPSILON = 1e-08


def pair_permute(value, low_mask, high_mask):
    size = lax.axis_size("dom")
    return lax.ppermute(value, "dom", [(i, i ^ (high_mask if i & 1 else low_mask)) for i in range(size)])


def xor_permute(value, mask):
    return pair_permute(value, mask, mask)


def outer_permute(value, k):
    return pair_permute(value, k << 6, k << 4)


def inner_permute(value, k):
    ring, z = k >> 1, k & 1
    return pair_permute(value, ring << 4 | z << 1, ring << 6 | z << 1)


def partner_hop(value, xor_value, low, width, work=None, *operands):
    pick = (xor_value >> low) & (2**width - 1)

    def branch(mask, v, *rest):
        moved = xor_permute(v, mask) if mask else v
        return (moved, work(*rest)) if work else moved

    return lax.switch(pick, [functools.partial(branch, m << low) for m in range(2**width)], value, *operands)


def update_relations(place, keep, received, relations, relation_state, tail_grad, xor_value):
    half, width, _ = keep.shape
    chunk = half // 4
    parts = [keep[k * chunk : (k + 1) * chunk] + received[k * chunk : (k + 1) * chunk] for k in range(4)]
    moved = [outer_permute(parts[k], k) for k in (2, 1, 3)]
    tail_grad = partner_hop(partner_hop(tail_grad, xor_value, 0, 1), xor_value, 1, 3)
    moved, tail_grad = lax.optimization_barrier((moved, tail_grad))
    part = sum(moved, parts[0])
    moved = [inner_permute(part[k], k) for k in range(1, 8)]
    tile = sum(moved, part[0])
    moved = [xor_permute(tile, mask) for mask in (4, 8, 12)]
    moved, tail_grad = lax.optimization_barrier((moved, partner_hop(tail_grad, xor_value, 6, 2)))
    total = sum(moved, tile)

    start = tile_at(0, place, place[0]) * TILE
    values = lax.dynamic_slice_in_dim(relations, start, TILE, 1)
    state = lax.dynamic_slice_in_dim(relation_state, start, TILE)
    new_state = state + jnp.mean(total * total, axis=0)
    new_values = values - STEP_RATE * total / jnp.sqrt(new_state + EPSILON)[None, :]
    packed = jnp.concatenate([new_values, jnp.broadcast_to(new_state[None], (8, TILE))], axis=0)
    packed = jnp.stack([packed, xor_permute(packed, 2)])
    packed = jnp.concatenate([packed] + [inner_permute(packed, k) for k in (2, 4, 6)], axis=0)
    one, three = outer_permute(packed, 1), outer_permute(packed, 3)
    one, three, tail_grad = lax.optimization_barrier((one, three, partner_hop(tail_grad, xor_value, 4, 2)))
    half = packed.shape[0] // 2
    low, high = outer_permute(three[:half], 1), outer_permute(one[half:], 3)
    mine = jnp.concatenate([packed, one, three], axis=0)
    others = xor_permute(mine, 1)
    others, low, high = lax.optimization_barrier((others, low, high))
    last = jnp.concatenate([low, high], axis=0)
    other_last = xor_permute(last, 1)
    new_relations, state_row = place_columns(place, mine, last, others, other_last, width, relations.shape[1])
    return new_relations, state_row[0], tail_grad


def split_parts(x):
    high = x.astype(jnp.bfloat16)
    low = (x - high.astype(jnp.float32)).astype(jnp.bfloat16)
    return high, low


def dot(a, b):
    return jnp.dot(a, b, preferred_element_type=jnp.float32)


def dot_nt(a, b):
    return lax.dot_general(a, b, (((1,), (1,)), ((), ())), preferred_element_type=jnp.float32)


def one_hot(condition):
    return jnp.where(condition, 1.0, 0.0).astype(jnp.bfloat16)


def gather_kernel(shift, first_ref, keys_ref, table_ref, out_ref, parts, sums):
    width, count = table_ref.shape
    block = keys_ref.shape[1]
    edges = keys_ref.size
    half = width // 2
    window = 1024

    @pl.loop(0, count // 256)
    def _(k):
        at = pl.ds(pl.multiple_of(k * 256, 256), 256)
        tile = jnp.concatenate([table_ref[:, at], jnp.zeros((PART - width, 256), jnp.float32)], axis=0)
        high, low = split_parts(tile)
        parts[:PART, at] = high
        parts[PART:, at] = low

    row = lax.broadcasted_iota(jnp.int32, (256, 256), 0)

    @pl.loop(0, edges // 256)
    def _(c):
        there = pl.ds(pl.multiple_of(c * 256, 256), 256)
        group, chunk = c // (block // 256), c % (block // 256)
        ids = keys_ref[pl.ds(group, 1), pl.ds(pl.multiple_of(chunk * 256, 256), 256)] >> shift
        low = first_ref[group, chunk * 256] >> shift
        low = low // 128 * 128
        high = jnp.minimum((first_ref[group, chunk * 256 + 255] >> shift) + 1, count)
        sums[...] = jnp.zeros_like(sums)

        @pl.loop(0, jnp.maximum(high - low + window - 1, 0) // window)
        def _(w):
            wanted = low + w * window
            start = pl.multiple_of(jnp.minimum(wanted, count - window), 128)
            inside = jnp.where(ids < wanted, -1, jnp.where(ids < wanted + window, ids - start, -1))
            cols = None
            for k in range(window // 256):
                part = dot(parts[:, pl.ds(start + k * 256, 256)], one_hot(row + k * 256 == inside))
                cols = part if cols is None else cols + part
            sums[...] += cols

        cols = sums[:PART] + sums[PART:]
        out_ref[:HALF, there] = cols[:HALF]
        out_ref[HALF:, there] = cols[half : half + HALF]


def gather_relations(shift, keys, relations):
    width, count = relations.shape
    edges = keys.size
    vmem = pl.BlockSpec(memory_space=pltpu.VMEM)
    return pl.pallas_call(
        functools.partial(gather_kernel, shift),
        out_shape=jax.ShapeDtypeStruct((PART, edges), jnp.float32),
        in_specs=[pl.BlockSpec(memory_space=pltpu.SMEM), vmem, vmem],
        out_specs=vmem,
        scratch_shapes=[
            pltpu.VMEM((2 * PART, count), jnp.bfloat16),
            pltpu.VMEM((2 * PART, 256), jnp.float32),
        ],
        compiler_params=pltpu.CompilerParams(vmem_limit_bytes=VMEM_LIMIT),
        cost_estimate=pl.CostEstimate(
            flops=PART * count * edges, bytes_accessed=width * count * 4, transcendentals=0
        ),
        name="gather_relations",
    )(keys, keys, relations)


def padded_halves(block):
    half = block.shape[0] // 2
    blank = jnp.zeros((HALF - half, block.shape[1]), block.dtype)
    return jnp.concatenate([block[:half], blank, block[half:], blank], axis=0)


def edge_kernel(
    bits, keys_ref, negs_ref, head_ref, tail_ref, rels_ref,
    head_grad_ref, tail_grad_ref, rel_grad_ref,
    cols_ref, flip_ref, wide_ref, query_ref, weight_ref, counts_ref, sums_ref,
):
    width, rows = head_ref.shape
    edges = keys_ref.size
    chunk = weight_ref.shape[1]
    groups = negs_ref.shape[0]
    half = width // 2

    for side, ref in enumerate((head_ref, tail_ref)):
        block = padded_halves(ref[...])
        high, low = split_parts(block)
        cols_ref[side, :PART, :] = high
        cols_ref[side, PART:, :] = low
        wide_ref[side, :, :rows] = high
        wide_ref[side, :, rows : 2 * rows] = high
        wide_ref[side, :, 2 * rows :] = low
        turned = jnp.concatenate([block, jnp.zeros((256 - PART, rows), jnp.float32)], axis=0).T
        high, low = split_parts(turned)
        flip_ref[side, :, :256] = high
        flip_ref[side, :, 256:512] = high
        flip_ref[side, :, 512:] = low
    for group in range(groups):
        for which in range(2):
            hits = lax.broadcasted_iota(jnp.int32, (rows, negs_ref.shape[-1]), 0) == negs_ref[group, which][None, :]
            count = jnp.sum(jnp.where(hits, 1.0 / negs_ref.shape[-1], 0.0), axis=1, keepdims=True)
            counts_ref[group, which] = jnp.broadcast_to(count, (rows, 128))
    query_ref[...] = jnp.zeros_like(query_ref)
    sums_ref[...] = jnp.zeros_like(sums_ref)

    def put_query(side, query):
        high, low = split_parts(query)
        query_ref[side, :PART, :] = high
        query_ref[side, 256 : 256 + PART, :] = low
        query_ref[side, 512 : 512 + PART, :] = high

    def put_weight(side, weight):
        high, low = split_parts(weight)
        weight_ref[side * 3 * rows : side * 3 * rows + rows, :] = high
        weight_ref[side * 3 * rows + rows : side * 3 * rows + 2 * rows, :] = low
        weight_ref[side * 3 * rows + 2 * rows : side * 3 * rows + 3 * rows, :] = high

    def add_sums(side, left, right, left_again, right_low):
        both = dot_nt(left, right)
        total = both[:PART] + both[256 : 256 + PART]
        if left_again is not None:
            total = total + dot_nt(left_again, right_low)
        sums_ref[side] += total

    @pl.loop(0, edges // chunk)
    def _(c):
        at = pl.ds(pl.multiple_of(c * chunk, chunk), chunk)
        group = c // (edges // groups // chunk)
        inner = edges // groups // chunk
        keys = keys_ref[pl.ds(group, 1), pl.ds(pl.multiple_of(c % inner * chunk, chunk), chunk)]
        heads = keys >> bits & 2**bits - 1
        tails = keys & 2**bits - 1
        row = lax.broadcasted_iota(jnp.int32, (rows, chunk), 0)
        head_hot = one_hot(row == heads)
        tail_is = row == tails
        tail_hot = one_hot(tail_is)
        h = dot(cols_ref[0], head_hot)
        h = h[:PART] + h[PART:]
        t = dot(cols_ref[1], tail_hot)
        t = t[:PART] + t[PART:]
        r = rels_ref[:, at]
        h_re, h_im, t_re, t_im, r_re, r_im = h[:HALF], h[HALF:], t[:HALF], t[HALF:], r[:HALF], r[HALF:]
        put_query(0, jnp.concatenate([r_re * t_re + r_im * t_im, r_re * t_im - r_im * t_re], axis=0))
        put_query(1, jnp.concatenate([h_re * r_re - h_im * r_im, h_re * r_im + h_im * r_re], axis=0))
        grads = []
        for side in range(2):
            scores = dot(flip_ref[side], query_ref[side])
            chance = 0.5 * jnp.tanh(0.5 * scores) + 0.5
            count = counts_ref[group, 1 - side][:, :1]
            if side == 0:
                weight = chance * count
            else:
                hot = jnp.where(tail_is, 1.0, 0.0)
                weight = chance * (count + hot) - hot
            put_weight(side, weight)
            base = side * 3 * rows
            grads.append(dot(wide_ref[side], weight_ref[base : base + 3 * rows, :]))
            add_sums(
                side, query_ref[side, : 256 + PART, :], weight_ref[base : base + rows, :],
                query_ref[side, :PART, :], weight_ref[base + rows : base + 2 * rows, :],
            )
        qh_re, qh_im, qt_re, qt_im = grads[0][:HALF], grads[0][HALF:], grads[1][:HALF], grads[1][HALF:]
        dh = jnp.concatenate([qt_re * r_re + qt_im * r_im, qt_im * r_re - qt_re * r_im], axis=0)
        dt = jnp.concatenate([qh_re * r_re - qh_im * r_im, qh_re * r_im + qh_im * r_re], axis=0)
        dr = jnp.concatenate(
            [
                qt_re * h_re + qt_im * h_im + qh_re * t_re + qh_im * t_im,
                qt_im * h_re - qt_re * h_im + qh_re * t_im - qh_im * t_re,
            ],
            axis=0,
        )
        high, low = split_parts(dr)
        rel_grad_ref[:PART, at] = high
        rel_grad_ref[PART:, at] = low
        put_query(0, dh)
        add_sums(0, query_ref[0, : 256 + PART, :], head_hot, None, None)
        put_query(1, dt)
        add_sums(1, query_ref[1, : 256 + PART, :], tail_hot, None, None)

    for side, ref in enumerate((head_grad_ref, tail_grad_ref)):
        ref[:half, :] = sums_ref[side, :half, :]
        ref[half:, :] = sums_ref[side, HALF : HALF + half, :]


def edge_gradients(bits, keys, negs, head_blk, tail_blk, rels):
    width, rows = head_blk.shape
    edges = keys.size
    chunk = edges // negs.shape[0]
    vmem = pl.BlockSpec(memory_space=pltpu.VMEM)
    return pl.pallas_call(
        functools.partial(edge_kernel, bits),
        out_shape=(
            jax.ShapeDtypeStruct((width, rows), jnp.float32),
            jax.ShapeDtypeStruct((width, rows), jnp.float32),
            jax.ShapeDtypeStruct((2 * PART, edges), jnp.bfloat16),
        ),
        in_specs=[vmem] * 5,
        out_specs=(vmem, vmem, vmem),
        scratch_shapes=[
            pltpu.VMEM((2, 2 * PART, rows), jnp.bfloat16),
            pltpu.VMEM((2, rows, 768), jnp.bfloat16),
            pltpu.VMEM((2, PART, 3 * rows), jnp.bfloat16),
            pltpu.VMEM((2, 768, chunk), jnp.bfloat16),
            pltpu.VMEM((6 * rows, chunk), jnp.bfloat16),
            pltpu.VMEM((negs.shape[0], 2, rows, 128), jnp.float32),
            pltpu.VMEM((2, PART, rows), jnp.float32),
        ],
        compiler_params=pltpu.CompilerParams(vmem_limit_bytes=VMEM_LIMIT),
        cost_estimate=pl.CostEstimate(
            flops=40 * PART * rows * edges, bytes_accessed=4 * PART * edges, transcendentals=2 * rows * edges
        ),
        name="edge_gradients",
    )(keys, negs, head_blk, tail_blk, rels)


def tile_at(position, place_ref, core):
    outer = (position // 8) ^ place_ref[1 + core]
    inner = (position // 2 % 4) ^ place_ref[2 - core]
    return core * 32 + outer * 8 + inner * 2 + (position % 2 ^ place_ref[3])


def scatter_kernel(other, groups, place_ref, starts_ref, ids_ref, grad_ref, out_ref, spread_ref, sums):
    tiles, width, tile = out_ref.shape
    core = jnp.where(other, 1 - place_ref[0], place_ref[0])
    edges = ids_ref.shape[0]
    block = edges // groups
    last = starts_ref.shape[0] // groups - 1
    half = width // 2
    pairs = sums.shape[0]
    spread_ref[...] = jnp.broadcast_to(ids_ref[...], spread_ref.shape)

    @pl.loop(0, tiles // 2 // pairs)
    def _(i):
        lane = lax.broadcasted_iota(jnp.int32, (256, tile), 1)
        row = lax.broadcasted_iota(jnp.int32, (256, tile), 0)
        spans = []
        for u in range(pairs):
            j = i * pairs + u
            first = tile_at(2 * j, place_ref, core)
            base = first // 2 * 2
            total = None
            for group in range(groups):
                low = starts_ref[group * (last + 1) + jnp.minimum(base, last)]
                high = starts_ref[group * (last + 1) + jnp.minimum(base + 2, last)]
                low = low // 128 * 128
                spans.append((u, group, base, low, high))
                at = pl.ds(pl.multiple_of(group * block + jnp.minimum(low, block - 256), 128), 256)
                ids = spread_ref[at, :] - base * tile
                hot = jnp.concatenate([one_hot(lane == ids), one_hot(lane + tile == ids)], axis=1)
                part = dot(grad_ref[:, at], hot)
                total = part if total is None else total + part
            sums[u] = total
        for u, group, base, low, high in spans:

            @pl.loop(1, jnp.maximum(high - low + 255, 256) // 256)
            def _(w):
                wanted = low + w * 256
                start = jnp.minimum(wanted, block - 256)
                at = pl.ds(pl.multiple_of(group * block + start, 128), 256)
                ids = jnp.where(row + start < wanted, -1, spread_ref[at, :] - base * tile)
                hot = jnp.concatenate([one_hot(lane == ids), one_hot(lane + tile == ids)], axis=1)
                sums[u] += dot(grad_ref[:, at], hot)

        for u in range(pairs):
            cols = sums[u, :PART] + sums[u, PART:]
            for side in range(2):
                part = cols[:, side * tile : (side + 1) * tile]
                to = 2 * (i * pairs + u) + (side ^ place_ref[3])
                out_ref[to, :half, :] = part[:half]
                out_ref[to, half:, :] = part[HALF : HALF + half]


def scatter_relations(other, place, starts, ids, grads, tiles, width):
    edges = grads.shape[1]
    vmem = pl.BlockSpec(memory_space=pltpu.VMEM)
    smem = pl.BlockSpec(memory_space=pltpu.SMEM)
    return pl.pallas_call(
        functools.partial(scatter_kernel, other, starts.shape[0]),
        out_shape=jax.ShapeDtypeStruct((tiles, width, TILE), jnp.float32),
        in_specs=[smem, smem, vmem, vmem],
        out_specs=vmem,
        scratch_shapes=[pltpu.VMEM((edges, TILE), jnp.int32), pltpu.VMEM((2, 2 * PART, 2 * TILE), jnp.float32)],
        compiler_params=pltpu.CompilerParams(vmem_limit_bytes=VMEM_LIMIT),
        cost_estimate=pl.CostEstimate(
            flops=PART * edges * tiles * TILE, bytes_accessed=tiles * width * TILE * 4, transcendentals=0
        ),
        name="scatter_relations",
    )(place, starts.reshape(starts.size), ids, grads)


def place_kernel(place_ref, mine_ref, last_ref, others_ref, other_last_ref, out_ref, state_ref, low_ref, high_ref, sent):
    width, count = out_ref.shape
    sources = ((mine_ref, last_ref), (others_ref, other_last_ref))
    copies = []
    for half, cols_ref in enumerate((low_ref, high_ref)):
        first = half * 32 * TILE
        for own in range(2):
            most, last = sources[(own + half) % 2]

            @pl.when(place_ref[0] == own)
            def _():
                for chunk, source, base in ((0, most, 0), (1, most, 8), (3, most, 16), (2, last, 0)):

                    @pl.loop(0, 8)
                    def _(j):
                        tile = tile_at(chunk * 8 + j, place_ref, half)

                        @pl.when(tile < count // TILE)
                        def _():
                            at = pl.multiple_of(tile * TILE, TILE)
                            here = pl.multiple_of(at - first, TILE)
                            cols_ref[:, pl.ds(here, TILE)] = source[base + j, :width, :]
                            state_ref[:, pl.ds(at, TILE)] = source[base + j, width : width + 1, :]

        there = out_ref.at[:, pl.ds(first, cols_ref.shape[1])]
        copies.append(pltpu.make_async_copy(cols_ref, there, sent.at[half]))
        copies[-1].start()
    for copy in copies:
        copy.wait()


def place_columns(place, mine, last, others, other_last, width, count):
    vmem = pl.BlockSpec(memory_space=pltpu.VMEM)
    return pl.pallas_call(
        place_kernel,
        out_shape=(
            jax.ShapeDtypeStruct((width, count), jnp.float32),
            jax.ShapeDtypeStruct((1, count), jnp.float32),
        ),
        in_specs=[pl.BlockSpec(memory_space=pltpu.SMEM)] + [vmem] * 4,
        out_specs=(pl.BlockSpec(memory_space=pl.ANY), vmem),
        scratch_shapes=[
            pltpu.VMEM((width, 32 * TILE), jnp.float32),
            pltpu.VMEM((width, count - 32 * TILE), jnp.float32),
            pltpu.SemaphoreType.DMA((2,)),
        ],
        compiler_params=pltpu.CompilerParams(vmem_limit_bytes=VMEM_LIMIT),
        cost_estimate=pl.CostEstimate(flops=0, bytes_accessed=8 * width * count, transcendentals=0),
        name="place_columns",
    )(place, mine, last, others, other_last)


def on_device(
    entities,
    entity_state,
    relations,
    relation_state,
    head_rows,
    relation_ids,
    tail_rows,
    neg_rows,
    edge_counts,
    matching,
):
    me = lax.axis_index("dom")
    core = me & 1
    xor_value = jnp.bitwise_xor(matching[0], me)
    width, count = relations.shape
    edges = head_rows.shape[1]
    half = -(-count // (64 * TILE)) * 32

    groups = neg_rows.shape[1]
    bits = (entities.shape[1] - 1).bit_length()
    shift = 2 * bits
    assert groups <= 2 and (count - 1).bit_length() + shift <= 31 and count < 2 ** (31 - shift) and entities.shape[1] < 2**bits

    keys = (relation_ids << shift | head_rows << bits | tail_rows)[0]
    slots = lax.broadcasted_iota(jnp.int32, keys.shape, 0)
    keys = jnp.where(slots < edge_counts[0], keys, 2**31 - 1).astype(jnp.uint32)
    keys = keys | (slots // (edges // groups)).astype(jnp.uint32) << 31

    def sort_keys(keys):
        keys = lax.sort(keys)
        keys = (keys & jnp.uint32(2**31 - 1)).astype(jnp.int32).reshape(groups, edges // groups)
        firsts = jnp.arange(count // TILE + 1, dtype=jnp.int32) * TILE
        before = (keys >> shift)[:, None, :] < firsts[None, :, None]
        return keys, jnp.sum(before.astype(jnp.int32), axis=2)

    tail_blk, (keys, starts) = partner_hop(entities, xor_value, 0, 1, sort_keys, keys)
    tail_blk = partner_hop(partner_hop(tail_blk, xor_value, 4, 2), xor_value, 6, 2)
    gather = functools.partial(gather_relations, shift)
    tail_blk, rels = partner_hop(tail_blk, xor_value, 1, 3, gather, keys, relations)
    head_grad, tail_grad, rel_grad = edge_gradients(
        bits, keys, neg_rows[0], entities, tail_blk, rels
    )

    column = (keys >> shift).reshape(edges, 1)
    place = jnp.stack([core, (me >> 6) & 3, (me >> 4) & 3, (me >> 1) & 1])
    send = scatter_relations(True, place, starts, column, rel_grad, half, width)
    received = xor_permute(send, 1)
    keep = scatter_relations(False, place, starts, column, rel_grad, half, width)
    new_relations, new_relation_state, tail_grad = update_relations(
        place, keep, received, relations, relation_state, tail_grad, xor_value
    )
    combined = head_grad + tail_grad
    new_entity_state = entity_state + jnp.mean(combined * combined, axis=0)
    new_entities = entities - STEP_RATE * combined / jnp.sqrt(new_entity_state + EPSILON)[None, :]
    return (new_entities, new_entity_state, new_relations, new_relation_state)


def solution(mesh):
    in_specs = (
        P(None, "dom"),
        P("dom"),
        P(),
        P(),
        P("dom", None),
        P("dom", None),
        P("dom", None),
        P("dom", None, None, None),
        P("dom"),
        P("dom"),
    )
    out_specs = (P(None, "dom"), P("dom"), P(), P())
    return jax.shard_map(
        on_device, mesh=mesh, in_specs=in_specs, out_specs=out_specs, check_vma=False
    )
```

```python
import functools

import jax
import jax.numpy as jnp
from jax import lax
from jax.experimental import pallas as pl
from jax.experimental.pallas import tpu as pltpu
from jax.sharding import PartitionSpec as P

TILE = 128
HALF = 104
PART = 2 * HALF
VMEM_LIMIT = 24 * 2**20
STEP_RATE = 0.3
EPSILON = 1e-08


def pair_permute(value, low_mask, high_mask):
    size = lax.axis_size("dom")
    return lax.ppermute(value, "dom", [(i, i ^ (high_mask if i & 1 else low_mask)) for i in range(size)])


def xor_permute(value, mask):
    return pair_permute(value, mask, mask)


def outer_permute(value, k):
    return pair_permute(value, k << 6, k << 4)


def inner_permute(value, k):
    ring, z = k >> 1, k & 1
    return pair_permute(value, ring << 4 | z << 1, ring << 6 | z << 1)


def partner_hop(value, xor_value, low, width, work=None, *operands):
    pick = (xor_value >> low) & (2**width - 1)

    def branch(mask, v, *rest):
        moved = xor_permute(v, mask) if mask else v
        return (moved, work(*rest)) if work else moved

    return lax.switch(pick, [functools.partial(branch, m << low) for m in range(2**width)], value, *operands)


def update_relations(place, keep, received, relations, relation_state, tail_grad, xor_value):
    half, width, _ = keep.shape
    chunk = half // 4
    parts = [keep[k * chunk : (k + 1) * chunk] + received[k * chunk : (k + 1) * chunk] for k in range(4)]
    moved = [outer_permute(parts[k], k) for k in (2, 1, 3)]
    tail_grad = partner_hop(partner_hop(tail_grad, xor_value, 0, 1), xor_value, 1, 3)
    moved, tail_grad = lax.optimization_barrier((moved, tail_grad))
    part = sum(moved, parts[0])
    moved = [inner_permute(part[k], k) for k in range(1, 8)]
    tile = sum(moved, part[0])
    moved = [xor_permute(tile, mask) for mask in (4, 8, 12)]
    total = sum(moved, tile)

    start = tile_at(0, place, place[0]) * TILE
    values = lax.dynamic_slice_in_dim(relations, start, TILE, 1)
    state = lax.dynamic_slice_in_dim(relation_state, start, TILE)
    new_state = state + jnp.mean(total * total, axis=0)
    new_values = values - STEP_RATE * total / jnp.sqrt(new_state + EPSILON)[None, :]
    packed = jnp.concatenate([new_values, jnp.broadcast_to(new_state[None], (8, TILE))], axis=0)
    packed = jnp.stack([packed, xor_permute(packed, 2)])
    moved = lax.optimization_barrier([inner_permute(packed, k) for k in (2, 4, 6)])
    packed = jnp.concatenate([packed] + moved, axis=0)
    one, three = outer_permute(packed, 1), outer_permute(packed, 3)
    one, three, tail_grad = lax.optimization_barrier((one, three, partner_hop(tail_grad, xor_value, 4, 2)))
    half = packed.shape[0] // 2
    low, high = outer_permute(three[:half], 1), outer_permute(one[half:], 3)
    mine = jnp.concatenate([packed, one, three], axis=0)
    others = xor_permute(mine, 1)
    tail_grad = partner_hop(tail_grad, xor_value, 6, 2)
    others, low, high, tail_grad = lax.optimization_barrier((others, low, high, tail_grad))
    last = jnp.concatenate([low, high], axis=0)
    other_last = xor_permute(last, 1)
    new_relations, state_row = place_columns(place, mine, last, others, other_last, width, relations.shape[1])
    return new_relations, state_row[0], tail_grad


def split_parts(x):
    high = x.astype(jnp.bfloat16)
    low = (x - high.astype(jnp.float32)).astype(jnp.bfloat16)
    return high, low


def dot(a, b):
    return jnp.dot(a, b, preferred_element_type=jnp.float32)


def dot_nt(a, b):
    return lax.dot_general(a, b, (((1,), (1,)), ((), ())), preferred_element_type=jnp.float32)


def one_hot(condition):
    return jnp.where(condition, 1.0, 0.0).astype(jnp.bfloat16)


def gather_kernel(shift, first_ref, keys_ref, table_ref, out_ref, parts, sums):
    width, count = table_ref.shape
    block = keys_ref.shape[1]
    edges = keys_ref.size
    half = width // 2
    window = 1024

    @pl.loop(0, count // 256)
    def _(k):
        at = pl.ds(pl.multiple_of(k * 256, 256), 256)
        tile = jnp.concatenate([table_ref[:, at], jnp.zeros((PART - width, 256), jnp.float32)], axis=0)
        high, low = split_parts(tile)
        parts[:PART, at] = high
        parts[PART:, at] = low

    row = lax.broadcasted_iota(jnp.int32, (256, 256), 0)

    @pl.loop(0, edges // 256)
    def _(c):
        there = pl.ds(pl.multiple_of(c * 256, 256), 256)
        group, chunk = c // (block // 256), c % (block // 256)
        ids = keys_ref[pl.ds(group, 1), pl.ds(pl.multiple_of(chunk * 256, 256), 256)] >> shift
        low = first_ref[group, chunk * 256] >> shift
        low = low // 128 * 128
        high = jnp.minimum((first_ref[group, chunk * 256 + 255] >> shift) + 1, count)
        sums[...] = jnp.zeros_like(sums)

        @pl.loop(0, jnp.maximum(high - low + window - 1, 0) // window)
        def _(w):
            wanted = low + w * window
            start = pl.multiple_of(jnp.minimum(wanted, count - window), 128)
            inside = jnp.where(ids < wanted, -1, jnp.where(ids < wanted + window, ids - start, -1))
            cols = None
            for k in range(window // 256):
                part = dot(parts[:, pl.ds(start + k * 256, 256)], one_hot(row + k * 256 == inside))
                cols = part if cols is None else cols + part
            sums[...] += cols

        cols = sums[:PART] + sums[PART:]
        out_ref[:HALF, there] = cols[:HALF]
        out_ref[HALF:, there] = cols[half : half + HALF]


def gather_relations(shift, keys, relations):
    width, count = relations.shape
    edges = keys.size
    vmem = pl.BlockSpec(memory_space=pltpu.VMEM)
    return pl.pallas_call(
        functools.partial(gather_kernel, shift),
        out_shape=jax.ShapeDtypeStruct((PART, edges), jnp.float32),
        in_specs=[pl.BlockSpec(memory_space=pltpu.SMEM), vmem, vmem],
        out_specs=vmem,
        scratch_shapes=[
            pltpu.VMEM((2 * PART, count), jnp.bfloat16),
            pltpu.VMEM((2 * PART, 256), jnp.float32),
        ],
        compiler_params=pltpu.CompilerParams(vmem_limit_bytes=VMEM_LIMIT),
        cost_estimate=pl.CostEstimate(
            flops=PART * count * edges, bytes_accessed=width * count * 4, transcendentals=0
        ),
        name="gather_relations",
    )(keys, keys, relations)


def padded_halves(block):
    half = block.shape[0] // 2
    blank = jnp.zeros((HALF - half, block.shape[1]), block.dtype)
    return jnp.concatenate([block[:half], blank, block[half:], blank], axis=0)


def edge_kernel(
    bits, keys_ref, negs_ref, head_ref, tail_ref, rels_ref,
    head_grad_ref, tail_grad_ref, rel_grad_ref,
    cols_ref, flip_ref, wide_ref, query_ref, weight_ref, counts_ref, sums_ref,
):
    width, rows = head_ref.shape
    edges = keys_ref.size
    chunk = weight_ref.shape[1]
    groups = negs_ref.shape[0]
    half = width // 2

    for side, ref in enumerate((head_ref, tail_ref)):
        block = padded_halves(ref[...])
        high, low = split_parts(block)
        cols_ref[side, :PART, :] = high
        cols_ref[side, PART:, :] = low
        wide_ref[side, :, :rows] = high
        wide_ref[side, :, rows : 2 * rows] = high
        wide_ref[side, :, 2 * rows :] = low
        turned = jnp.concatenate([block, jnp.zeros((256 - PART, rows), jnp.float32)], axis=0).T
        high, low = split_parts(turned)
        flip_ref[side, :, :256] = high
        flip_ref[side, :, 256:512] = high
        flip_ref[side, :, 512:] = low
    for group in range(groups):
        for which in range(2):
            hits = lax.broadcasted_iota(jnp.int32, (rows, negs_ref.shape[-1]), 0) == negs_ref[group, which][None, :]
            count = jnp.sum(jnp.where(hits, 1.0 / negs_ref.shape[-1], 0.0), axis=1, keepdims=True)
            counts_ref[group, which] = jnp.broadcast_to(count, (rows, 128))
    query_ref[...] = jnp.zeros_like(query_ref)
    sums_ref[...] = jnp.zeros_like(sums_ref)

    def put_query(side, query):
        high, low = split_parts(query)
        query_ref[side, :PART, :] = high
        query_ref[side, 256 : 256 + PART, :] = low
        query_ref[side, 512 : 512 + PART, :] = high

    def put_weight(side, weight):
        high, low = split_parts(weight)
        weight_ref[side * 3 * rows : side * 3 * rows + rows, :] = high
        weight_ref[side * 3 * rows + rows : side * 3 * rows + 2 * rows, :] = low
        weight_ref[side * 3 * rows + 2 * rows : side * 3 * rows + 3 * rows, :] = high

    def add_sums(side, left, right, left_again, right_low):
        both = dot_nt(left, right)
        total = both[:PART] + both[256 : 256 + PART]
        if left_again is not None:
            total = total + dot_nt(left_again, right_low)
        sums_ref[side] += total

    @pl.loop(0, edges // chunk)
    def _(c):
        at = pl.ds(pl.multiple_of(c * chunk, chunk), chunk)
        group = c // (edges // groups // chunk)
        inner = edges // groups // chunk
        keys = keys_ref[pl.ds(group, 1), pl.ds(pl.multiple_of(c % inner * chunk, chunk), chunk)]
        heads = keys >> bits & 2**bits - 1
        tails = keys & 2**bits - 1
        row = lax.broadcasted_iota(jnp.int32, (rows, chunk), 0)
        head_hot = one_hot(row == heads)
        tail_is = row == tails
        tail_hot = one_hot(tail_is)
        h = dot(cols_ref[0], head_hot)
        h = h[:PART] + h[PART:]
        t = dot(cols_ref[1], tail_hot)
        t = t[:PART] + t[PART:]
        r = rels_ref[:, at]
        h_re, h_im, t_re, t_im, r_re, r_im = h[:HALF], h[HALF:], t[:HALF], t[HALF:], r[:HALF], r[HALF:]
        put_query(0, jnp.concatenate([r_re * t_re + r_im * t_im, r_re * t_im - r_im * t_re], axis=0))
        put_query(1, jnp.concatenate([h_re * r_re - h_im * r_im, h_re * r_im + h_im * r_re], axis=0))
        grads = []
        for side in range(2):
            scores = dot(flip_ref[side], query_ref[side])
            chance = 0.5 * jnp.tanh(0.5 * scores) + 0.5
            count = counts_ref[group, 1 - side][:, :1]
            if side == 0:
                weight = chance * count
            else:
                hot = jnp.where(tail_is, 1.0, 0.0)
                weight = chance * (count + hot) - hot
            put_weight(side, weight)
            base = side * 3 * rows
            grads.append(dot(wide_ref[side], weight_ref[base : base + 3 * rows, :]))
            add_sums(
                side, query_ref[side, : 256 + PART, :], weight_ref[base : base + rows, :],
                query_ref[side, :PART, :], weight_ref[base + rows : base + 2 * rows, :],
            )
        qh_re, qh_im, qt_re, qt_im = grads[0][:HALF], grads[0][HALF:], grads[1][:HALF], grads[1][HALF:]
        dh = jnp.concatenate([qt_re * r_re + qt_im * r_im, qt_im * r_re - qt_re * r_im], axis=0)
        dt = jnp.concatenate([qh_re * r_re - qh_im * r_im, qh_re * r_im + qh_im * r_re], axis=0)
        dr = jnp.concatenate(
            [
                qt_re * h_re + qt_im * h_im + qh_re * t_re + qh_im * t_im,
                qt_im * h_re - qt_re * h_im + qh_re * t_im - qh_im * t_re,
            ],
            axis=0,
        )
        high, low = split_parts(dr)
        rel_grad_ref[:PART, at] = high
        rel_grad_ref[PART:, at] = low
        put_query(0, dh)
        add_sums(0, query_ref[0, : 256 + PART, :], head_hot, None, None)
        put_query(1, dt)
        add_sums(1, query_ref[1, : 256 + PART, :], tail_hot, None, None)

    for side, ref in enumerate((head_grad_ref, tail_grad_ref)):
        ref[:half, :] = sums_ref[side, :half, :]
        ref[half:, :] = sums_ref[side, HALF : HALF + half, :]


def edge_gradients(bits, keys, negs, head_blk, tail_blk, rels):
    width, rows = head_blk.shape
    edges = keys.size
    chunk = edges // negs.shape[0]
    vmem = pl.BlockSpec(memory_space=pltpu.VMEM)
    return pl.pallas_call(
        functools.partial(edge_kernel, bits),
        out_shape=(
            jax.ShapeDtypeStruct((width, rows), jnp.float32),
            jax.ShapeDtypeStruct((width, rows), jnp.float32),
            jax.ShapeDtypeStruct((2 * PART, edges), jnp.bfloat16),
        ),
        in_specs=[vmem] * 5,
        out_specs=(vmem, vmem, vmem),
        scratch_shapes=[
            pltpu.VMEM((2, 2 * PART, rows), jnp.bfloat16),
            pltpu.VMEM((2, rows, 768), jnp.bfloat16),
            pltpu.VMEM((2, PART, 3 * rows), jnp.bfloat16),
            pltpu.VMEM((2, 768, chunk), jnp.bfloat16),
            pltpu.VMEM((6 * rows, chunk), jnp.bfloat16),
            pltpu.VMEM((negs.shape[0], 2, rows, 128), jnp.float32),
            pltpu.VMEM((2, PART, rows), jnp.float32),
        ],
        compiler_params=pltpu.CompilerParams(vmem_limit_bytes=VMEM_LIMIT),
        cost_estimate=pl.CostEstimate(
            flops=40 * PART * rows * edges, bytes_accessed=4 * PART * edges, transcendentals=2 * rows * edges
        ),
        name="edge_gradients",
    )(keys, negs, head_blk, tail_blk, rels)


def tile_at(position, place_ref, core):
    outer = (position // 8) ^ place_ref[1 + core]
    inner = (position // 2 % 4) ^ place_ref[2 - core]
    return core * 32 + outer * 8 + inner * 2 + (position % 2 ^ place_ref[3])


def scatter_kernel(other, groups, place_ref, starts_ref, ids_ref, grad_ref, out_ref, spread_ref, sums):
    tiles, width, tile = out_ref.shape
    core = jnp.where(other, 1 - place_ref[0], place_ref[0])
    edges = ids_ref.shape[0]
    block = edges // groups
    last = starts_ref.shape[0] // groups - 1
    half = width // 2
    pairs = sums.shape[0]
    spread_ref[...] = jnp.broadcast_to(ids_ref[...], spread_ref.shape)

    @pl.loop(0, tiles // 2 // pairs)
    def _(i):
        lane = lax.broadcasted_iota(jnp.int32, (256, tile), 1)
        row = lax.broadcasted_iota(jnp.int32, (256, tile), 0)
        spans = []
        for u in range(pairs):
            j = i * pairs + u
            first = tile_at(2 * j, place_ref, core)
            base = first // 2 * 2
            total = None
            for group in range(groups):
                low = starts_ref[group * (last + 1) + jnp.minimum(base, last)]
                high = starts_ref[group * (last + 1) + jnp.minimum(base + 2, last)]
                low = low // 128 * 128
                spans.append((u, group, base, low, high))
                at = pl.ds(pl.multiple_of(group * block + jnp.minimum(low, block - 256), 128), 256)
                ids = spread_ref[at, :] - base * tile
                hot = jnp.concatenate([one_hot(lane == ids), one_hot(lane + tile == ids)], axis=1)
                part = dot(grad_ref[:, at], hot)
                total = part if total is None else total + part
            sums[u] = total
        for u, group, base, low, high in spans:

            @pl.loop(1, jnp.maximum(high - low + 255, 256) // 256)
            def _(w):
                wanted = low + w * 256
                start = jnp.minimum(wanted, block - 256)
                at = pl.ds(pl.multiple_of(group * block + start, 128), 256)
                ids = jnp.where(row + start < wanted, -1, spread_ref[at, :] - base * tile)
                hot = jnp.concatenate([one_hot(lane == ids), one_hot(lane + tile == ids)], axis=1)
                sums[u] += dot(grad_ref[:, at], hot)

        for u in range(pairs):
            cols = sums[u, :PART] + sums[u, PART:]
            for side in range(2):
                part = cols[:, side * tile : (side + 1) * tile]
                to = 2 * (i * pairs + u) + (side ^ place_ref[3])
                out_ref[to, :half, :] = part[:half]
                out_ref[to, half:, :] = part[HALF : HALF + half]


def scatter_relations(other, place, starts, ids, grads, tiles, width):
    edges = grads.shape[1]
    vmem = pl.BlockSpec(memory_space=pltpu.VMEM)
    smem = pl.BlockSpec(memory_space=pltpu.SMEM)
    return pl.pallas_call(
        functools.partial(scatter_kernel, other, starts.shape[0]),
        out_shape=jax.ShapeDtypeStruct((tiles, width, TILE), jnp.float32),
        in_specs=[smem, smem, vmem, vmem],
        out_specs=vmem,
        scratch_shapes=[pltpu.VMEM((edges, TILE), jnp.int32), pltpu.VMEM((2, 2 * PART, 2 * TILE), jnp.float32)],
        compiler_params=pltpu.CompilerParams(vmem_limit_bytes=VMEM_LIMIT),
        cost_estimate=pl.CostEstimate(
            flops=PART * edges * tiles * TILE, bytes_accessed=tiles * width * TILE * 4, transcendentals=0
        ),
        name="scatter_relations",
    )(place, starts.reshape(starts.size), ids, grads)


def place_kernel(place_ref, mine_ref, last_ref, others_ref, other_last_ref, out_ref, state_ref, low_ref, high_ref, sent):
    width, count = out_ref.shape
    sources = ((mine_ref, last_ref), (others_ref, other_last_ref))
    copies = []
    for half, cols_ref in enumerate((low_ref, high_ref)):
        first = half * 32 * TILE
        for own in range(2):
            most, last = sources[(own + half) % 2]

            @pl.when(place_ref[0] == own)
            def _():
                for chunk, source, base in ((0, most, 0), (1, most, 8), (3, most, 16), (2, last, 0)):

                    @pl.loop(0, 8)
                    def _(j):
                        tile = tile_at(chunk * 8 + j, place_ref, half)

                        @pl.when(tile < count // TILE)
                        def _():
                            at = pl.multiple_of(tile * TILE, TILE)
                            here = pl.multiple_of(at - first, TILE)
                            cols_ref[:, pl.ds(here, TILE)] = source[base + j, :width, :]
                            state_ref[:, pl.ds(at, TILE)] = source[base + j, width : width + 1, :]

        there = out_ref.at[:, pl.ds(first, cols_ref.shape[1])]
        copies.append(pltpu.make_async_copy(cols_ref, there, sent.at[half]))
        copies[-1].start()
    for copy in copies:
        copy.wait()


def place_columns(place, mine, last, others, other_last, width, count):
    vmem = pl.BlockSpec(memory_space=pltpu.VMEM)
    return pl.pallas_call(
        place_kernel,
        out_shape=(
            jax.ShapeDtypeStruct((width, count), jnp.float32),
            jax.ShapeDtypeStruct((1, count), jnp.float32),
        ),
        in_specs=[pl.BlockSpec(memory_space=pltpu.SMEM)] + [vmem] * 4,
        out_specs=(pl.BlockSpec(memory_space=pl.ANY), vmem),
        scratch_shapes=[
            pltpu.VMEM((width, 32 * TILE), jnp.float32),
            pltpu.VMEM((width, count - 32 * TILE), jnp.float32),
            pltpu.SemaphoreType.DMA((2,)),
        ],
        compiler_params=pltpu.CompilerParams(vmem_limit_bytes=VMEM_LIMIT),
        cost_estimate=pl.CostEstimate(flops=0, bytes_accessed=8 * width * count, transcendentals=0),
        name="place_columns",
    )(place, mine, last, others, other_last)


def on_device(
    entities,
    entity_state,
    relations,
    relation_state,
    head_rows,
    relation_ids,
    tail_rows,
    neg_rows,
    edge_counts,
    matching,
):
    me = lax.axis_index("dom")
    core = me & 1
    xor_value = jnp.bitwise_xor(matching[0], me)
    width, count = relations.shape
    edges = head_rows.shape[1]
    half = -(-count // (64 * TILE)) * 32

    groups = neg_rows.shape[1]
    bits = (entities.shape[1] - 1).bit_length()
    shift = 2 * bits
    assert groups <= 2 and (count - 1).bit_length() + shift <= 31 and count < 2 ** (31 - shift) and entities.shape[1] < 2**bits

    keys = (relation_ids << shift | head_rows << bits | tail_rows)[0]
    slots = lax.broadcasted_iota(jnp.int32, keys.shape, 0)
    keys = jnp.where(slots < edge_counts[0], keys, 2**31 - 1).astype(jnp.uint32)
    keys = keys | (slots // (edges // groups)).astype(jnp.uint32) << 31

    def sort_keys(keys):
        keys = lax.sort(keys)
        keys = (keys & jnp.uint32(2**31 - 1)).astype(jnp.int32).reshape(groups, edges // groups)
        firsts = jnp.arange(count // TILE + 1, dtype=jnp.int32) * TILE
        before = (keys >> shift)[:, None, :] < firsts[None, :, None]
        return keys, jnp.sum(before.astype(jnp.int32), axis=2)

    tail_blk, (keys, starts) = partner_hop(entities, xor_value, 0, 1, sort_keys, keys)
    tail_blk = partner_hop(partner_hop(tail_blk, xor_value, 4, 2), xor_value, 6, 2)
    gather = functools.partial(gather_relations, shift)
    tail_blk, rels = partner_hop(tail_blk, xor_value, 1, 3, gather, keys, relations)
    head_grad, tail_grad, rel_grad = edge_gradients(
        bits, keys, neg_rows[0], entities, tail_blk, rels
    )

    column = (keys >> shift).reshape(edges, 1)
    place = jnp.stack([core, (me >> 6) & 3, (me >> 4) & 3, (me >> 1) & 1])
    send = scatter_relations(True, place, starts, column, rel_grad, half, width)
    received = xor_permute(send, 1)
    keep = scatter_relations(False, place, starts, column, rel_grad, half, width)
    new_relations, new_relation_state, tail_grad = update_relations(
        place, keep, received, relations, relation_state, tail_grad, xor_value
    )
    combined = head_grad + tail_grad
    new_entity_state = entity_state + jnp.mean(combined * combined, axis=0)
    new_entities = entities - STEP_RATE * combined / jnp.sqrt(new_entity_state + EPSILON)[None, :]
    return (new_entities, new_entity_state, new_relations, new_relation_state)


def solution(mesh):
    in_specs = (
        P(None, "dom"),
        P("dom"),
        P(),
        P(),
        P("dom", None),
        P("dom", None),
        P("dom", None),
        P("dom", None, None, None),
        P("dom"),
        P("dom"),
    )
    out_specs = (P(None, "dom"), P("dom"), P(), P())
    return jax.shard_map(
        on_device, mesh=mesh, in_specs=in_specs, out_specs=out_specs, check_vma=False
    )
```

```python
import functools

import jax
import jax.numpy as jnp
from jax import lax
from jax.experimental import pallas as pl
from jax.experimental.pallas import tpu as pltpu
from jax.sharding import PartitionSpec as P

TILE = 128
HALF = 104
PART = 2 * HALF
VMEM_LIMIT = 24 * 2**20
STEP_RATE = 0.3
EPSILON = 1e-08


def pair_permute(value, low_mask, high_mask):
    size = lax.axis_size("dom")
    return lax.ppermute(value, "dom", [(i, i ^ (high_mask if i & 1 else low_mask)) for i in range(size)])


def xor_permute(value, mask):
    return pair_permute(value, mask, mask)


def outer_permute(value, k):
    return pair_permute(value, k << 6, k << 4)


def inner_permute(value, k):
    ring, z = k >> 1, k & 1
    return pair_permute(value, ring << 4 | z << 1, ring << 6 | z << 1)


def partner_hop(value, xor_value, low, width, work=None, *operands):
    pick = (xor_value >> low) & (2**width - 1)

    def branch(mask, v, *rest):
        moved = xor_permute(v, mask) if mask else v
        return (moved, work(*rest)) if work else moved

    return lax.switch(pick, [functools.partial(branch, m << low) for m in range(2**width)], value, *operands)


def update_relations(place, keep, received, relations, relation_state, tail_grad, xor_value):
    half, width, _ = keep.shape
    chunk = half // 4
    parts = [keep[k * chunk : (k + 1) * chunk] + received[k * chunk : (k + 1) * chunk] for k in range(4)]
    moved = [outer_permute(parts[k], k) for k in (2, 1, 3)]
    tail_grad = partner_hop(partner_hop(tail_grad, xor_value, 0, 1), xor_value, 1, 3)
    moved, tail_grad = lax.optimization_barrier((moved, tail_grad))
    part = sum(moved, parts[0])
    moved = [inner_permute(part[k], k) for k in range(1, 8)]
    tile = sum(moved, part[0])
    moved = [xor_permute(tile, mask) for mask in (4, 8, 12)]
    moved, tail_grad = lax.optimization_barrier((moved, partner_hop(tail_grad, xor_value, 6, 2)))
    total = sum(moved, tile)

    start = tile_at(0, place, place[0]) * TILE
    values = lax.dynamic_slice_in_dim(relations, start, TILE, 1)
    state = lax.dynamic_slice_in_dim(relation_state, start, TILE)
    new_state = state + jnp.mean(total * total, axis=0)
    new_values = values - STEP_RATE * total / jnp.sqrt(new_state + EPSILON)[None, :]
    packed = jnp.concatenate([new_values, jnp.broadcast_to(new_state[None], (8, TILE))], axis=0)
    packed = jnp.stack([packed, xor_permute(packed, 2)])
    packed = jnp.concatenate([packed] + [inner_permute(packed, k) for k in (2, 4, 6)], axis=0)
    one, three = outer_permute(packed, 1), outer_permute(packed, 3)
    one, three, tail_grad = lax.optimization_barrier((one, three, partner_hop(tail_grad, xor_value, 4, 2)))
    half = packed.shape[0] // 2
    low, high = outer_permute(three[:half], 1), outer_permute(one[half:], 3)
    mine = jnp.concatenate([packed, one, three], axis=0)
    others = xor_permute(mine, 1)
    others, low, high = lax.optimization_barrier((others, low, high))
    last = jnp.concatenate([low, high], axis=0)
    other_last = xor_permute(last, 1)
    new_relations, state_row = place_columns(place, mine, last, others, other_last, width, relations.shape[1])
    return new_relations, state_row[0], tail_grad


def split_parts(x):
    high = x.astype(jnp.bfloat16)
    low = (x - high.astype(jnp.float32)).astype(jnp.bfloat16)
    return high, low


def dot(a, b):
    return jnp.dot(a, b, preferred_element_type=jnp.float32)


def dot_nt(a, b):
    return lax.dot_general(a, b, (((1,), (1,)), ((), ())), preferred_element_type=jnp.float32)


def one_hot(condition):
    return jnp.where(condition, 1.0, 0.0).astype(jnp.bfloat16)


def gather_kernel(shift, first_ref, keys_ref, table_ref, out_ref, parts, sums):
    width, count = table_ref.shape
    block = keys_ref.shape[1]
    edges = keys_ref.size
    half = width // 2
    window = 1024

    @pl.loop(0, count // 256)
    def _(k):
        at = pl.ds(pl.multiple_of(k * 256, 256), 256)
        tile = jnp.concatenate([table_ref[:, at], jnp.zeros((PART - width, 256), jnp.float32)], axis=0)
        high, low = split_parts(tile)
        parts[:PART, at] = high
        parts[PART:, at] = low

    row = lax.broadcasted_iota(jnp.int32, (256, 256), 0)

    @pl.loop(0, edges // 256)
    def _(c):
        there = pl.ds(pl.multiple_of(c * 256, 256), 256)
        group, chunk = c // (block // 256), c % (block // 256)
        ids = keys_ref[pl.ds(group, 1), pl.ds(pl.multiple_of(chunk * 256, 256), 256)] >> shift
        low = first_ref[group, chunk * 256] >> shift
        low = low // 128 * 128
        high = jnp.minimum((first_ref[group, chunk * 256 + 255] >> shift) + 1, count)
        sums[...] = jnp.zeros_like(sums)

        @pl.loop(0, jnp.maximum(high - low + window - 1, 0) // window)
        def _(w):
            wanted = low + w * window
            start = pl.multiple_of(jnp.minimum(wanted, count - window), 128)
            inside = jnp.where(ids < wanted, -1, jnp.where(ids < wanted + window, ids - start, -1))
            cols = None
            for k in range(window // 256):
                part = dot(parts[:, pl.ds(start + k * 256, 256)], one_hot(row + k * 256 == inside))
                cols = part if cols is None else cols + part
            sums[...] += cols

        cols = sums[:PART] + sums[PART:]
        out_ref[:HALF, there] = cols[:HALF]
        out_ref[HALF:, there] = cols[half : half + HALF]


def gather_relations(shift, keys, relations):
    width, count = relations.shape
    edges = keys.size
    vmem = pl.BlockSpec(memory_space=pltpu.VMEM)
    return pl.pallas_call(
        functools.partial(gather_kernel, shift),
        out_shape=jax.ShapeDtypeStruct((PART, edges), jnp.float32),
        in_specs=[pl.BlockSpec(memory_space=pltpu.SMEM), vmem, vmem],
        out_specs=vmem,
        scratch_shapes=[
            pltpu.VMEM((2 * PART, count), jnp.bfloat16),
            pltpu.VMEM((2 * PART, 256), jnp.float32),
        ],
        compiler_params=pltpu.CompilerParams(vmem_limit_bytes=VMEM_LIMIT),
        cost_estimate=pl.CostEstimate(
            flops=PART * count * edges, bytes_accessed=width * count * 4, transcendentals=0
        ),
        name="gather_relations",
    )(keys, keys, relations)


def padded_halves(block):
    half = block.shape[0] // 2
    blank = jnp.zeros((HALF - half, block.shape[1]), block.dtype)
    return jnp.concatenate([block[:half], blank, block[half:], blank], axis=0)


def edge_kernel(
    bits, keys_ref, negs_ref, head_ref, tail_ref, rels_ref,
    head_grad_ref, tail_grad_ref, rel_grad_ref,
    cols_ref, flip_ref, wide_ref, query_ref, weight_ref, counts_ref, sums_ref,
):
    width, rows = head_ref.shape
    edges = keys_ref.size
    chunk = weight_ref.shape[1]
    groups = negs_ref.shape[0]
    half = width // 2

    for side, ref in enumerate((head_ref, tail_ref)):
        block = padded_halves(ref[...])
        high, low = split_parts(block)
        cols_ref[side, :PART, :] = high
        cols_ref[side, PART:, :] = low
        wide_ref[side, :, :rows] = high
        wide_ref[side, :, rows : 2 * rows] = high
        wide_ref[side, :, 2 * rows :] = low
        turned = jnp.concatenate([block, jnp.zeros((256 - PART, rows), jnp.float32)], axis=0).T
        high, low = split_parts(turned)
        flip_ref[side, :, :256] = high
        flip_ref[side, :, 256:512] = high
        flip_ref[side, :, 512:] = low
    for group in range(groups):
        for which in range(2):
            hits = lax.broadcasted_iota(jnp.int32, (rows, negs_ref.shape[-1]), 0) == negs_ref[group, which][None, :]
            count = jnp.sum(jnp.where(hits, 1.0 / negs_ref.shape[-1], 0.0), axis=1, keepdims=True)
            counts_ref[group, which] = jnp.broadcast_to(count, (rows, 128))
    query_ref[...] = jnp.zeros_like(query_ref)
    sums_ref[...] = jnp.zeros_like(sums_ref)

    def put_query(side, query):
        high, low = split_parts(query)
        query_ref[side, :PART, :] = high
        query_ref[side, 256 : 256 + PART, :] = low
        query_ref[side, 512 : 512 + PART, :] = high

    def put_weight(side, weight):
        high, low = split_parts(weight)
        weight_ref[side * 3 * rows : side * 3 * rows + rows, :] = high
        weight_ref[side * 3 * rows + rows : side * 3 * rows + 2 * rows, :] = low
        weight_ref[side * 3 * rows + 2 * rows : side * 3 * rows + 3 * rows, :] = high

    def add_sums(side, left, right, left_again, right_low):
        both = dot_nt(left, right)
        total = both[:PART] + both[256 : 256 + PART]
        if left_again is not None:
            total = total + dot_nt(left_again, right_low)
        sums_ref[side] += total

    @pl.loop(0, edges // chunk)
    def _(c):
        at = pl.ds(pl.multiple_of(c * chunk, chunk), chunk)
        group = c // (edges // groups // chunk)
        inner = edges // groups // chunk
        keys = keys_ref[pl.ds(group, 1), pl.ds(pl.multiple_of(c % inner * chunk, chunk), chunk)]
        heads = keys >> bits & 2**bits - 1
        tails = keys & 2**bits - 1
        row = lax.broadcasted_iota(jnp.int32, (rows, chunk), 0)
        head_hot = one_hot(row == heads)
        tail_is = row == tails
        tail_hot = one_hot(tail_is)
        h = dot(cols_ref[0], head_hot)
        h = h[:PART] + h[PART:]
        t = dot(cols_ref[1], tail_hot)
        t = t[:PART] + t[PART:]
        r = rels_ref[:, at]
        h_re, h_im, t_re, t_im, r_re, r_im = h[:HALF], h[HALF:], t[:HALF], t[HALF:], r[:HALF], r[HALF:]
        put_query(0, jnp.concatenate([r_re * t_re + r_im * t_im, r_re * t_im - r_im * t_re], axis=0))
        put_query(1, jnp.concatenate([h_re * r_re - h_im * r_im, h_re * r_im + h_im * r_re], axis=0))
        grads = []
        for side in range(2):
            scores = dot(flip_ref[side], query_ref[side])
            chance = 0.5 * jnp.tanh(0.5 * scores) + 0.5
            count = counts_ref[group, 1 - side][:, :1]
            if side == 0:
                weight = chance * count
            else:
                hot = jnp.where(tail_is, 1.0, 0.0)
                weight = chance * (count + hot) - hot
            put_weight(side, weight)
            base = side * 3 * rows
            grads.append(dot(wide_ref[side], weight_ref[base : base + 3 * rows, :]))
            add_sums(
                side, query_ref[side, : 256 + PART, :], weight_ref[base : base + rows, :],
                query_ref[side, :PART, :], weight_ref[base + rows : base + 2 * rows, :],
            )
        qh_re, qh_im, qt_re, qt_im = grads[0][:HALF], grads[0][HALF:], grads[1][:HALF], grads[1][HALF:]
        dh = jnp.concatenate([qt_re * r_re + qt_im * r_im, qt_im * r_re - qt_re * r_im], axis=0)
        dt = jnp.concatenate([qh_re * r_re - qh_im * r_im, qh_re * r_im + qh_im * r_re], axis=0)
        dr = jnp.concatenate(
            [
                qt_re * h_re + qt_im * h_im + qh_re * t_re + qh_im * t_im,
                qt_im * h_re - qt_re * h_im + qh_re * t_im - qh_im * t_re,
            ],
            axis=0,
        )
        high, low = split_parts(dr)
        rel_grad_ref[:PART, at] = high
        rel_grad_ref[PART:, at] = low
        put_query(0, dh)
        add_sums(0, query_ref[0, : 256 + PART, :], head_hot, None, None)
        put_query(1, dt)
        add_sums(1, query_ref[1, : 256 + PART, :], tail_hot, None, None)

    for side, ref in enumerate((head_grad_ref, tail_grad_ref)):
        ref[:half, :] = sums_ref[side, :half, :]
        ref[half:, :] = sums_ref[side, HALF : HALF + half, :]


def edge_gradients(bits, keys, negs, head_blk, tail_blk, rels):
    width, rows = head_blk.shape
    edges = keys.size
    chunk = edges // negs.shape[0]
    vmem = pl.BlockSpec(memory_space=pltpu.VMEM)
    return pl.pallas_call(
        functools.partial(edge_kernel, bits),
        out_shape=(
            jax.ShapeDtypeStruct((width, rows), jnp.float32),
            jax.ShapeDtypeStruct((width, rows), jnp.float32),
            jax.ShapeDtypeStruct((2 * PART, edges), jnp.bfloat16),
        ),
        in_specs=[vmem] * 5,
        out_specs=(vmem, vmem, vmem),
        scratch_shapes=[
            pltpu.VMEM((2, 2 * PART, rows), jnp.bfloat16),
            pltpu.VMEM((2, rows, 768), jnp.bfloat16),
            pltpu.VMEM((2, PART, 3 * rows), jnp.bfloat16),
            pltpu.VMEM((2, 768, chunk), jnp.bfloat16),
            pltpu.VMEM((6 * rows, chunk), jnp.bfloat16),
            pltpu.VMEM((negs.shape[0], 2, rows, 128), jnp.float32),
            pltpu.VMEM((2, PART, rows), jnp.float32),
        ],
        compiler_params=pltpu.CompilerParams(vmem_limit_bytes=VMEM_LIMIT),
        cost_estimate=pl.CostEstimate(
            flops=40 * PART * rows * edges, bytes_accessed=4 * PART * edges, transcendentals=2 * rows * edges
        ),
        name="edge_gradients",
    )(keys, negs, head_blk, tail_blk, rels)


def tile_at(position, place_ref, core):
    outer = (position // 8) ^ place_ref[1 + core]
    inner = (position // 2 % 4) ^ place_ref[2 - core]
    return core * 32 + outer * 8 + inner * 2 + (position % 2 ^ place_ref[3])


def scatter_kernel(other, groups, place_ref, starts_ref, ids_ref, grad_ref, out_ref, spread_ref, sums):
    tiles, width, tile = out_ref.shape
    core = jnp.where(other, 1 - place_ref[0], place_ref[0])
    edges = ids_ref.shape[0]
    block = edges // groups
    last = starts_ref.shape[0] // groups - 1
    half = width // 2
    pairs = sums.shape[0]
    spread_ref[...] = jnp.broadcast_to(ids_ref[...], spread_ref.shape)

    @pl.loop(0, tiles // 2 // pairs)
    def _(i):
        lane = lax.broadcasted_iota(jnp.int32, (256, tile), 1)
        row = lax.broadcasted_iota(jnp.int32, (256, tile), 0)
        spans = []
        for u in range(pairs):
            j = i * pairs + u
            first = tile_at(2 * j, place_ref, core)
            base = first // 2 * 2
            total = None
            for group in range(groups):
                low = starts_ref[group * (last + 1) + jnp.minimum(base, last)]
                high = starts_ref[group * (last + 1) + jnp.minimum(base + 2, last)]
                low = low // 128 * 128
                spans.append((u, group, base, low, high))
                at = pl.ds(pl.multiple_of(group * block + jnp.minimum(low, block - 256), 128), 256)
                ids = spread_ref[at, :] - base * tile
                hot = jnp.concatenate([one_hot(lane == ids), one_hot(lane + tile == ids)], axis=1)
                part = dot(grad_ref[:, at], hot)
                total = part if total is None else total + part
            sums[u] = total
        for u, group, base, low, high in spans:

            @pl.loop(1, jnp.maximum(high - low + 255, 256) // 256)
            def _(w):
                wanted = low + w * 256
                start = jnp.minimum(wanted, block - 256)
                at = pl.ds(pl.multiple_of(group * block + start, 128), 256)
                ids = jnp.where(row + start < wanted, -1, spread_ref[at, :] - base * tile)
                hot = jnp.concatenate([one_hot(lane == ids), one_hot(lane + tile == ids)], axis=1)
                sums[u] += dot(grad_ref[:, at], hot)

        for u in range(pairs):
            cols = sums[u, :PART] + sums[u, PART:]
            for side in range(2):
                part = cols[:, side * tile : (side + 1) * tile]
                to = 2 * (i * pairs + u) + (side ^ place_ref[3])
                out_ref[to, :half, :] = part[:half]
                out_ref[to, half:, :] = part[HALF : HALF + half]


def scatter_relations(other, place, starts, ids, grads, tiles, width):
    edges = grads.shape[1]
    vmem = pl.BlockSpec(memory_space=pltpu.VMEM)
    smem = pl.BlockSpec(memory_space=pltpu.SMEM)
    return pl.pallas_call(
        functools.partial(scatter_kernel, other, starts.shape[0]),
        out_shape=jax.ShapeDtypeStruct((tiles, width, TILE), jnp.float32),
        in_specs=[smem, smem, vmem, vmem],
        out_specs=vmem,
        scratch_shapes=[pltpu.VMEM((edges, TILE), jnp.int32), pltpu.VMEM((2, 2 * PART, 2 * TILE), jnp.float32)],
        compiler_params=pltpu.CompilerParams(vmem_limit_bytes=VMEM_LIMIT),
        cost_estimate=pl.CostEstimate(
            flops=PART * edges * tiles * TILE, bytes_accessed=tiles * width * TILE * 4, transcendentals=0
        ),
        name="scatter_relations",
    )(place, starts.reshape(starts.size), ids, grads)


def place_kernel(place_ref, mine_ref, last_ref, others_ref, other_last_ref, out_ref, state_ref, low_ref, high_ref, sent):
    width, count = out_ref.shape
    sources = ((mine_ref, last_ref), (others_ref, other_last_ref))
    copies = []
    for half, cols_ref in enumerate((low_ref, high_ref)):
        first = half * 32 * TILE
        for own in range(2):
            most, last = sources[(own + half) % 2]

            @pl.when(place_ref[0] == own)
            def _():
                for chunk, source, base in ((0, most, 0), (1, most, 8), (3, most, 16), (2, last, 0)):

                    @pl.loop(0, 8)
                    def _(j):
                        tile = tile_at(chunk * 8 + j, place_ref, half)

                        @pl.when(tile < count // TILE)
                        def _():
                            at = pl.multiple_of(tile * TILE, TILE)
                            here = pl.multiple_of(at - first, TILE)
                            cols_ref[:, pl.ds(here, TILE)] = source[base + j, :width, :]
                            state_ref[:, pl.ds(at, TILE)] = source[base + j, width : width + 1, :]

        there = out_ref.at[:, pl.ds(first, cols_ref.shape[1])]
        copies.append(pltpu.make_async_copy(cols_ref, there, sent.at[half]))
        copies[-1].start()
    for copy in copies:
        copy.wait()


def place_columns(place, mine, last, others, other_last, width, count):
    vmem = pl.BlockSpec(memory_space=pltpu.VMEM)
    return pl.pallas_call(
        place_kernel,
        out_shape=(
            jax.ShapeDtypeStruct((width, count), jnp.float32),
            jax.ShapeDtypeStruct((1, count), jnp.float32),
        ),
        in_specs=[pl.BlockSpec(memory_space=pltpu.SMEM)] + [vmem] * 4,
        out_specs=(pl.BlockSpec(memory_space=pl.ANY), vmem),
        scratch_shapes=[
            pltpu.VMEM((width, 32 * TILE), jnp.float32),
            pltpu.VMEM((width, count - 32 * TILE), jnp.float32),
            pltpu.SemaphoreType.DMA((2,)),
        ],
        compiler_params=pltpu.CompilerParams(vmem_limit_bytes=VMEM_LIMIT),
        cost_estimate=pl.CostEstimate(flops=0, bytes_accessed=8 * width * count, transcendentals=0),
        name="place_columns",
    )(place, mine, last, others, other_last)


def on_device(
    entities,
    entity_state,
    relations,
    relation_state,
    head_rows,
    relation_ids,
    tail_rows,
    neg_rows,
    edge_counts,
    matching,
):
    me = lax.axis_index("dom")
    core = me & 1
    xor_value = jnp.bitwise_xor(matching[0], me)
    width, count = relations.shape
    edges = head_rows.shape[1]
    half = -(-count // (64 * TILE)) * 32

    groups = neg_rows.shape[1]
    bits = (entities.shape[1] - 1).bit_length()
    shift = 2 * bits
    assert groups <= 2 and (count - 1).bit_length() + shift <= 31 and count < 2 ** (31 - shift) and entities.shape[1] < 2**bits

    keys = (relation_ids << shift | head_rows << bits | tail_rows)[0]
    slots = lax.broadcasted_iota(jnp.int32, keys.shape, 0)
    keys = jnp.where(slots < edge_counts[0], keys, 2**31 - 1).astype(jnp.uint32)
    keys = keys | (slots // (edges // groups)).astype(jnp.uint32) << 31

    def sort_keys(keys):
        keys = lax.sort(keys)
        keys = (keys & jnp.uint32(2**31 - 1)).astype(jnp.int32).reshape(groups, edges // groups)
        firsts = jnp.arange(count // TILE + 1, dtype=jnp.int32) * TILE
        before = (keys >> shift)[:, None, :] < firsts[None, :, None]
        return keys, jnp.sum(before.astype(jnp.int32), axis=2)

    tail_blk, (keys, starts) = partner_hop(entities, xor_value, 0, 1, sort_keys, keys)
    tail_blk = partner_hop(tail_blk, xor_value, 4, 4)
    gather = functools.partial(gather_relations, shift)
    tail_blk, rels = partner_hop(tail_blk, xor_value, 1, 3, gather, keys, relations)
    head_grad, tail_grad, rel_grad = edge_gradients(
        bits, keys, neg_rows[0], entities, tail_blk, rels
    )

    column = (keys >> shift).reshape(edges, 1)
    place = jnp.stack([core, (me >> 6) & 3, (me >> 4) & 3, (me >> 1) & 1])
    send = scatter_relations(True, place, starts, column, rel_grad, half, width)
    received = xor_permute(send, 1)
    keep = scatter_relations(False, place, starts, column, rel_grad, half, width)
    new_relations, new_relation_state, tail_grad = update_relations(
        place, keep, received, relations, relation_state, tail_grad, xor_value
    )
    combined = head_grad + tail_grad
    new_entity_state = entity_state + jnp.mean(combined * combined, axis=0)
    new_entities = entities - STEP_RATE * combined / jnp.sqrt(new_entity_state + EPSILON)[None, :]
    return (new_entities, new_entity_state, new_relations, new_relation_state)


def solution(mesh):
    in_specs = (
        P(None, "dom"),
        P("dom"),
        P(),
        P(),
        P("dom", None),
        P("dom", None),
        P("dom", None),
        P("dom", None, None, None),
        P("dom"),
        P("dom"),
    )
    out_specs = (P(None, "dom"), P("dom"), P(), P())
    return jax.shard_map(
        on_device, mesh=mesh, in_specs=in_specs, out_specs=out_specs, check_vma=False
    )
```
